128 devices in a mesh: cells: 128 (over x, y, z, core).
Axes of the slice: x: 4, y: 4, z: 4, core: 2. Of those that a mesh axis runs over, the one named last changes fastest.
Arguments:
- position: float32 [3, 2097152], P(None, 'cells'), may hold values from -1 to 1
- velocity: float32 [3, 2097152], P(None, 'cells'), may hold values from -6 to 6
- particle_mass: float32 [2097152], P('cells'), may hold values from 0.5 to 2
- entropy: float32 [2097152], P('cells'), may hold values from 0.5 to 2
- density_old: float32 [2097152], P('cells'), may hold values from 0.25 to 2
- active: int32 [2097152], P('cells'), may hold values 0 or 1
- neighbours: int32 [8192, 6], P('cells'), may hold values from 0 to 8191, as said below
- destination: int32 [2097152], P('cells'), may hold values from 0 to 127, as said below
- recv_slot: int32 [2097152], P('cells'), may hold values from 0 to 24575, as said below
Outputs:
- moved_state: float32 [9, 3145728], P(None, 'cells')
The draws below stay inside these ranges and needn't reach their ends.
Inputs may be any that keep to these rules, and one draw needn't show every extreme that they name: `neighbours`: row c begins with c itself; its other entries are distinct cells (c + o) mod 8192 with 0 < |o| <= 4; every even cell lists c + 4 and every odd cell c - 4. `destination`: A particle of device d goes to (d + o) mod 128 with |o| <= 4; some device sends exactly 1024 particles to another one, and none sends more. `recv_slot`: A particle that stays keeps its own row among its device's first 16384; one arriving from offset o (numbered g = 0 to 7 for o = -4 .. -1, 1 .. 4) takes a row 16384 + g * 1024 + r with r < 1024; no two particles of one destination share a row.
All inputs are finite; a program needn't handle non-finite values. No bound on the sum of `active` on one device may be relied on, other than what follows from the above.
Results may differ from the reference program's by a relative error of at most 0.00002.
Values sent between devices are 32-bit elements; how exact they have to be, the bound alone decides.
No kernel may reach another device: no remote copies, remote signals or barrier semaphores. Data moves between devices by JAX's collectives and lax.ppermute only.
A program may use at most 64 MiB of HBM per device.

```python
import math
import jax
import jax.numpy as jnp
from jax import lax

CELL_PARTICLES = 256
NEIGHBOUR_CELLS = 6
HALO = 4
REACH = 4
PART_DEV = 16384
MOST = 1024
CELLS = 8192
PARTS_SIZE = 2097152
RECV_DEV = 24576
N_CELLS = 128


def migration_plan(key):
    dev_count = PARTS_SIZE // PART_DEV
    groups = 2 * REACH
    key_count, key_full, key_order = jax.random.split(key, 3)
    counts = jax.random.randint(key_count, (dev_count, groups), MOST // 3, MOST // 2 + 1)
    full_group = jax.random.randint(key_full, (dev_count,), 0, groups)
    counts = jnp.where(jnp.arange(groups)[None, :] == full_group[:, None], MOST, counts)
    shuffled = jax.vmap(lambda subkey: jax.random.permutation(subkey, PART_DEV))(jax.random.split(key_order, dev_count))
    group_ends = jnp.cumsum(counts, axis=1)
    group_starts = group_ends - counts
    placed = jnp.arange(PART_DEV)[None, :]
    group_of = jnp.sum((placed[:, :, None] >= group_ends[:, None, :]).astype(jnp.int32), axis=2)
    moving = group_of < groups
    group_safe = jnp.minimum(group_of, groups - 1)
    rank_in = placed - jnp.take_along_axis(group_starts, group_safe, axis=1)
    candidates = jnp.concatenate([jnp.arange(-REACH, 0), jnp.arange(1, REACH + 1)])
    home_dev = jnp.arange(dev_count)[:, None]
    dest_sorted = jnp.where(moving, (home_dev + candidates[group_safe]) % dev_count, home_dev)
    slot_sorted = jnp.where(moving, PART_DEV + group_safe * MOST + rank_in, shuffled)
    inverse = jnp.argsort(shuffled, axis=1)
    dest_of = jnp.take_along_axis(dest_sorted, inverse, axis=1).reshape(-1)
    slot_of = jnp.take_along_axis(slot_sorted, inverse, axis=1).reshape(-1)
    return (dest_of.astype(jnp.int32), slot_of.astype(jnp.int32))


def draw_destination(key, part):
    return migration_plan(key)[0]


def draw_recv_slot(key, part):
    return migration_plan(key)[1]


def draw_neighbours(key, part):
    key = jax.random.fold_in(key, 7)
    candidates = jnp.concatenate([jnp.arange(-HALO, 0), jnp.arange(1, HALO + 1)])
    ranks = jax.vmap(lambda subkey: jax.random.permutation(subkey, 2 * HALO))(jax.random.split(key, CELLS))
    cell_index_list = jnp.arange(CELLS)
    forced = jnp.where(cell_index_list % 2 == 0, 2 * HALO - 1, 0)
    ranks = jnp.where(jnp.arange(2 * HALO)[None, :] == forced[:, None], -1, ranks)
    picked = jnp.argsort(ranks, axis=1)[:, :NEIGHBOUR_CELLS - 1]
    others = (cell_index_list[:, None] + candidates[picked]) % CELLS
    return jnp.concatenate([cell_index_list[:, None], others], axis=1).astype(jnp.int32)


def set_ends(array, rng, smallest, top_value):
    spot = [jax.random.randint(jax.random.fold_in(rng, axis), (), 0, length) for axis, length in enumerate(array.shape)]
    main_axis = array.shape.index(max(array.shape))
    next_to = spot[:main_axis] + [(spot[main_axis] + 1) % array.shape[main_axis]] + spot[main_axis + 1:]
    return array.at[tuple(spot)].set(smallest).at[tuple(next_to)].set(top_value)


def block_scale(own_key, shape, pieces, low, largest):
    def one(dim, blocks):
        draws = jax.random.uniform(jax.random.fold_in(jax.random.fold_in(own_key, 6), dim), (blocks,), jnp.float32, low / len(pieces), largest / len(pieces))
        return jnp.repeat(jnp.exp(draws), shape[dim] // blocks).reshape((-1,) + (1,) * (len(shape) - dim - 1))

    factor_of = one(*pieces[0])
    for cut in pieces[1:]:
        factor_of = factor_of * one(*cut)
    return factor_of


def centred(own_key, dims, deviation, most, cuts=(), kind=jnp.bfloat16):
    values = jax.random.normal(own_key, dims, jnp.float32) * deviation
    if len(cuts) > 0:
        values = block_scale(own_key, dims, cuts, -0.22, 0.18) * values
    return jnp.clip(values, min=-most, max=most).astype(kind)


def setup_inputs(seed: int = 0) -> dict:
    key_of = jax.random.split(jax.random.key(seed), 10)
    return {
        "position": jnp.clip(jax.random.uniform(key_of[0], (3, PARTS_SIZE), jnp.float32, -1.0, 1.0) * block_scale(key_of[0], (3, PARTS_SIZE), ((1, 128),), -0.4, 0.0), -1.0, 1.0),
        "velocity": centred(key_of[1], (3, PARTS_SIZE), 1.0, 6.0, ((1, 128),), jnp.float32),
        "particle_mass": jnp.clip(jnp.exp(math.log(2.0) - 1.3862944 * jax.random.uniform(key_of[2], (PARTS_SIZE,), jnp.float32) ** block_scale(key_of[2], (PARTS_SIZE,), ((0, 128),), -0.2, 0.2)), 0.5, 2.0),
        "entropy": jnp.clip(jnp.exp(math.log(2.0) - 1.3862944 * jax.random.uniform(key_of[3], (PARTS_SIZE,), jnp.float32) ** block_scale(key_of[3], (PARTS_SIZE,), ((0, 128),), -0.2, 0.2)), 0.5, 2.0),
        "density_old": jnp.clip(jnp.exp(math.log(2.0) - 2.0794415 * jax.random.uniform(key_of[4], (PARTS_SIZE,), jnp.float32) ** block_scale(key_of[4], (PARTS_SIZE,), ((0, 128),), -0.2, 0.2)), 0.25, 2.0),
        "active": set_ends((jax.random.randint(key_of[5], (PARTS_SIZE,), 0, 32) < 1).astype(jnp.int32), jax.random.fold_in(key_of[5], 1), 0, 1),
        "neighbours": draw_neighbours(jax.random.fold_in(key_of[9], 71), 0),
        "destination": draw_destination(jax.random.fold_in(key_of[9], 71), 0),
        "recv_slot": draw_recv_slot(jax.random.fold_in(key_of[9], 71), 0),
    }


cell_block = 8
time_step = 0.25
gamma_rate = 5.0 / 3.0


def squared_distance(target_particles, source_particles):
    separation = target_particles[0][:, None, :, None] - source_particles[0][:, :, None, :]
    squared = separation * separation
    for component in (1, 2):
        separation = target_particles[component][:, None, :, None] - source_particles[component][:, :, None, :]
        squared = squared + separation * separation
    return squared


def summed_density(target_particles, source_particles, kernel_scale):
    kernel_baseline = jnp.maximum(1.0 - 0.25 * squared_distance(target_particles, source_particles), 0.0)
    kernel_weight = kernel_scale * kernel_baseline * kernel_baseline * kernel_baseline
    return jnp.sum(kernel_weight * source_particles[3][:, :, None, :], axis=(1, 3))


def summed_force(target_particles, target_term_rows, source_particles, kernel_scale):
    kernel_baseline = jnp.maximum(1.0 - 0.25 * squared_distance(target_particles, source_particles), 0.0)
    kernel_weight = (1.5 * kernel_scale) * kernel_baseline * kernel_baseline * source_particles[3][:, :, None, :]
    kernel_weight = kernel_weight * (target_term_rows[:, None, :, None] + source_particles[4][:, :, None, :])
    return jnp.stack([jnp.sum(kernel_weight * (target_particles[component][:, None, :, None] - source_particles[component][:, :, None, :]), axis=(1, 3)) for component in range(3)])


def cell_density_rows(target_particles, source_particle, cell_index_list, kernel_scale):
    cell_count = cell_index_list.shape[0]
    target_view = target_particles.reshape(3, cell_count, CELL_PARTICLES)
    cell_particle_view = source_particle.reshape(source_particle.shape[0], -1, CELL_PARTICLES)

    def one_block(block_start):
        block_index_list = lax.dynamic_slice_in_dim(cell_index_list, block_start, cell_block, 0)
        block_target_rows = lax.dynamic_slice_in_dim(target_view, block_start, cell_block, 1)
        return summed_density(block_target_rows, cell_particle_view[:, block_index_list], kernel_scale)

    starts = jnp.arange(cell_count // cell_block, dtype=jnp.int32) * cell_block
    return lax.map(one_block, starts).reshape(-1)


def cell_force_rows(target_particles, target_term_rows, source_particle, cell_index_list, kernel_scale):
    cell_count = cell_index_list.shape[0]
    target_view = target_particles.reshape(3, cell_count, CELL_PARTICLES)
    term_view = target_term_rows.reshape(cell_count, CELL_PARTICLES)
    cell_particle_view = source_particle.reshape(source_particle.shape[0], -1, CELL_PARTICLES)

    def one_block(block_start):
        block_index_list = lax.dynamic_slice_in_dim(cell_index_list, block_start, cell_block, 0)
        block_target_rows = lax.dynamic_slice_in_dim(target_view, block_start, cell_block, 1)
        block_term_rows = lax.dynamic_slice_in_dim(term_view, block_start, cell_block, 0)
        return summed_force(block_target_rows, block_term_rows, cell_particle_view[:, block_index_list], kernel_scale)

    starts = jnp.arange(cell_count // cell_block, dtype=jnp.int32) * cell_block
    blocks = lax.map(one_block, starts)
    return jnp.moveaxis(blocks, 1, 0).reshape(3, -1)


def reference(position, velocity, particle_mass, entropy, density_old, active, neighbours, destination, recv_slot):
    kernel_scale = 8.0 / (NEIGHBOUR_CELLS * CELL_PARTICLES)
    is_active = active == 1
    source_particle = jnp.concatenate([position, particle_mass[None]], axis=0)
    summed_total = cell_density_rows(position, source_particle, neighbours, kernel_scale)
    density = jnp.where(is_active, summed_total, density_old)
    pressure_term = entropy * density ** (gamma_rate - 2.0)
    source_of_force = jnp.concatenate([source_particle, pressure_term[None]], axis=0)
    acceleration = cell_force_rows(position, pressure_term, source_of_force, neighbours, kernel_scale)
    acceleration = jnp.where(is_active[None], acceleration, 0.0)
    new_velocity = velocity + time_step * acceleration
    new_position = position + time_step * new_velocity
    payload = jnp.concatenate([new_position, new_velocity, density[None], entropy[None], particle_mass[None]], axis=0)
    target_rows = destination * RECV_DEV + recv_slot
    return jnp.zeros((9, RECV_DEV * N_CELLS), jnp.float32).at[:, target_rows].set(payload)
```

```python
import functools

import jax
import jax.numpy as jnp
from jax import lax
from jax.experimental import pallas as pl
from jax.experimental.pallas import tpu as pltpu
from jax.sharding import PartitionSpec as P

CELL_PARTICLES = 256
HALO = 4
REACH = 4
PART_DEV = 16384
MOST = 1024
RECV_DEV = 24576
CELLS_DEV = 64
NEIGHBOURS = 6
LANES = 128
ROWS = PART_DEV // LANES
EDGE = 2 * HALO
EXT = CELLS_DEV + 2 * EDGE
EXT_ROWS = 2 * EXT
EDGE_ROWS = 2 * EDGE
HALO_ROWS = 96
GHOST = HALO
LISTED = CELLS_DEV + 2 * GHOST
UNROLL = 8
LIST_SIZE = LISTED * 32 + 4 * UNROLL + 64
GROUPS = 2 * REACH
time_step = 0.25
FIELDS = 9


def bcast(ref, row):
    return ref[pl.ds(row, 8, stride=0), :]


def state_kernel(
    own_ref,
    nbr_ref,
    pos_ref,
    vel_ref,
    mass_ref,
    ent_ref,
    rho_ref,
    act_ref,
    dest_ref,
    slot_ref,
    left_ref,
    right_ref,
    out_ref,
    send_ref,
    xs,
    ys,
    zs,
    ms,
    ps,
    rank,
    count_v,
    dens,
    ax,
    ay,
    az,
    fields,
    parts,
    hi_row,
    lo_row,
    a_block,
    b_block,
    packed,
    stay_rows,
    count_s,
    chunk_list,
    sem,
):
    own = own_ref[0]
    scale = 8.0 / (NEIGHBOURS * CELL_PARTICLES)

    for ref, base in ((xs, 0), (ys, 1), (zs, 2)):
        ref[0:EDGE_ROWS, :] = left_ref[base * 16 : base * 16 + 16, :] * 0.5
        ref[EDGE_ROWS + ROWS :, :] = right_ref[base * 16 : base * 16 + 16, :] * 0.5
    ms[0:EDGE_ROWS, :] = left_ref[48:64, :]
    ms[EDGE_ROWS : EDGE_ROWS + ROWS, :] = mass_ref[...]
    ms[EDGE_ROWS + ROWS :, :] = right_ref[48:64, :]

    def split_rows(i, carry):
        col = pl.multiple_of(i * LANES, LANES)
        p = pos_ref[:, pl.ds(col, LANES)]
        v = vel_ref[:, pl.ds(col, LANES)]
        for c, ref in enumerate((xs, ys, zs)):
            ref[pl.ds(EDGE_ROWS + i, 1), :] = p[c : c + 1, :] * 0.5
            fields[3 + c, pl.ds(i, 1), :] = v[c : c + 1, :]
        return carry

    lax.fori_loop(0, ROWS, split_rows, 0, unroll=4)

    zeros8 = jnp.zeros((8, LANES), jnp.float32)
    act = jnp.concatenate(
        [
            zeros8,
            left_ref[80:88, :],
            (act_ref[...] == 1).astype(jnp.float32),
            right_ref[80:88, :],
            zeros8,
        ],
        axis=0,
    )
    before = (
        lax.broadcasted_iota(jnp.int32, (LANES, LANES), 0)
        < lax.broadcasted_iota(jnp.int32, (LANES, LANES), 1)
    ).astype(jnp.bfloat16)
    act16 = act.astype(jnp.bfloat16)
    inside = jnp.dot(act16, before, preferred_element_type=jnp.float32)
    total = jnp.dot(
        act16, jnp.ones((LANES, LANES), jnp.bfloat16), preferred_element_type=jnp.float32
    )
    shifted = pltpu.roll(total, 1, 0)
    row_id = lax.broadcasted_iota(jnp.int32, (EXT_ROWS, LANES), 0)
    rank[...] = jnp.where(
        act > 0.5, inside + jnp.where(row_id % 2 == 1, shifted, 0.0), -1.0
    )
    count_v[...] = (total + shifted).astype(jnp.int32)
    count_copy = pltpu.make_async_copy(count_v, count_s, sem.at[0])
    count_copy.start()
    dens[...] = jnp.zeros_like(dens)
    for ref in (ax, ay, az):
        ref[...] = jnp.zeros_like(ref)
    count_copy.wait()

    def list_cell(cell, at):
        n = count_s[2 * cell + 1, 0]
        chunks = (n + 7) >> 3
        chunk_list[at] = cell * 64
        chunk_list[at + 1] = cell * 64 + 1

        def more(k, carry):
            chunk_list[at + k] = cell * 64 + k
            return carry

        lax.fori_loop(2, chunks, more, 0)
        return at + chunks

    def pad(at):
        for k in range(UNROLL):
            chunk_list[at + k] = EDGE * 64 + 32

    own_total = lax.fori_loop(EDGE, EDGE + CELLS_DEV, list_cell, 0)
    all_total = lax.fori_loop(EDGE - GHOST, EDGE, list_cell, own_total)
    all_total = lax.fori_loop(
        EDGE + CELLS_DEV, EDGE + CELLS_DEV + GHOST, list_cell, all_total
    )
    pad(all_total)

    sub = lax.broadcasted_iota(jnp.int32, (8, LANES), 0).astype(jnp.float32)

    def chunk_of(position):
        code = chunk_list[position]
        cell = code >> 6
        want = sub + ((code & 63) * 8).astype(jnp.float32)
        picks = [bcast(rank, 2 * cell + h) == want for h in range(2)]
        return cell, picks

    def column(ref, cell, picks):
        both = jnp.where(picks[0], bcast(ref, 2 * cell), 0.0) + jnp.where(
            picks[1], bcast(ref, 2 * cell + 1), 0.0
        )
        return jnp.sum(both, axis=1, keepdims=True)

    def spread(ref, cell, picks, value):
        for h in range(2):
            row = jnp.sum(jnp.where(picks[h], value, 0.0), axis=0, keepdims=True)
            ref[pl.ds(2 * cell + h, 1), :] += row

    def density_step(step, carry):
        done = []
        for u in range(UNROLL):
            cell, picks = chunk_of(step * UNROLL + u)
            cx, cy, cz = (column(ref, cell, picks) for ref in (xs, ys, zs))
            total_rows = jnp.zeros((8, LANES), jnp.float32)
            for q in range(NEIGHBOURS):
                source = nbr_ref[(cell - (EDGE - GHOST)) * NEIGHBOURS + q]
                for h in range(2):
                    row = 2 * source + h
                    dx = cx - bcast(xs, row)
                    dy = cy - bcast(ys, row)
                    dz = cz - bcast(zs, row)
                    u1 = jnp.maximum(1.0 - (dx * dx + dy * dy + dz * dz), 0.0)
                    total_rows += u1 * u1 * u1 * bcast(ms, row)
            value = jnp.sum(total_rows, axis=1, keepdims=True) * scale
            done.append((cell, picks, value))
        for cell, picks, value in done:
            spread(dens, cell, picks, value)
        return carry

    lax.fori_loop(0, (all_total + UNROLL - 1) // UNROLL, density_step, 0)

    ones8 = jnp.ones((8, LANES), jnp.float32)
    rho_old = jnp.concatenate(
        [ones8, left_ref[72:80, :], rho_ref[...], right_ref[72:80, :], ones8], axis=0
    )
    entropy = jnp.concatenate(
        [zeros8, left_ref[64:72, :], ent_ref[...], right_ref[64:72, :], zeros8], axis=0
    )
    rho = jnp.where(rank[...] >= 0.0, dens[...], rho_old)
    dens[...] = rho
    ps[...] = entropy * jnp.exp(jnp.log(rho) * (-1.0 / 3.0))

    def force_step(step, carry):
        done = []
        for u in range(UNROLL):
            cell, picks = chunk_of(step * UNROLL + u)
            cx, cy, cz, cp = (column(ref, cell, picks) for ref in (xs, ys, zs, ps))
            sx = jnp.zeros((8, LANES), jnp.float32)
            sy = jnp.zeros((8, LANES), jnp.float32)
            sz = jnp.zeros((8, LANES), jnp.float32)
            for q in range(NEIGHBOURS):
                source = nbr_ref[(cell - (EDGE - GHOST)) * NEIGHBOURS + q]
                for h in range(2):
                    row = 2 * source + h
                    dx = cx - bcast(xs, row)
                    dy = cy - bcast(ys, row)
                    dz = cz - bcast(zs, row)
                    u1 = jnp.maximum(1.0 - (dx * dx + dy * dy + dz * dz), 0.0)
                    w = u1 * u1 * (bcast(ms, row) * (cp + bcast(ps, row)))
                    sx += w * dx
                    sy += w * dy
                    sz += w * dz
            values = [
                jnp.sum(s, axis=1, keepdims=True) * (3.0 * scale) for s in (sx, sy, sz)
            ]
            done.append((cell, picks, values))
        for cell, picks, values in done:
            for ref, value in zip((ax, ay, az), values):
                spread(ref, cell, picks, value)
        return carry

    lax.fori_loop(0, (own_total + UNROLL - 1) // UNROLL, force_step, 0)

    own_rows = slice(EDGE_ROWS, EDGE_ROWS + ROWS)
    for c, (ref, acc) in enumerate(((xs, ax), (ys, ay), (zs, az))):
        kicked = fields[3 + c] + time_step * acc[own_rows, :]
        fields[3 + c] = kicked
        fields[c] = ref[own_rows, :] * 2.0 + time_step * kicked
    fields[6] = dens[own_rows, :]
    fields[7] = ent_ref[...]
    fields[8] = mass_ref[...]

    dest = dest_ref[...]
    staying = dest == own
    away = (dest - own) & 127
    signed = jnp.where(away > 64, away - 128, away)
    group = jnp.where(signed < 0, signed + REACH, signed + REACH - 1)
    place = (slot_ref[...] - PART_DEV) & (MOST - 1)
    hi = (group >> 1) * 8 + (place >> 7)
    lo = (group & 1) * LANES + (place & (LANES - 1))
    hi_row[...] = jnp.where(staying, -1, hi).astype(jnp.float32)
    lo_row[...] = jnp.where(staying, -1, lo).astype(jnp.float32)
    keep = staying
    for v in range(FIELDS):
        whole = fields[v]
        head = whole.astype(jnp.bfloat16).astype(jnp.float32)
        parts[v] = head
        parts[FIELDS + v] = whole - head
        fields[v] = jnp.where(keep, whole, 0.0)

    def stay_step(i, carry):
        col = pl.multiple_of(i * LANES, LANES)
        for v in range(FIELDS):
            stay_rows[v : v + 1, pl.ds(col, LANES)] = fields[v, pl.ds(i, 1), :]
        return carry

    lax.fori_loop(0, ROWS, stay_step, 0, unroll=4)
    stay_copy = pltpu.make_async_copy(
        stay_rows, out_ref.at[:, pl.ds(0, PART_DEV)], sem.at[1]
    )
    stay_copy.start()

    packed[...] = jnp.zeros_like(packed)
    hi_iota = lax.broadcasted_iota(jnp.int32, (32, LANES), 0).astype(jnp.float32)
    lo_iota = lax.broadcasted_iota(jnp.int32, (256, LANES), 0).astype(jnp.float32)
    per = 4

    def pack_step(step, carry):
        for j in range(per):
            row = step * per + j
            cols = slice(j * LANES, (j + 1) * LANES)
            hi_b = jnp.concatenate([bcast(hi_row, row)] * 4, axis=0)
            pick = (hi_b == hi_iota).astype(jnp.bfloat16)
            lo_b = jnp.concatenate([bcast(lo_row, row)] * 32, axis=0)
            b_block[:, cols] = (lo_b == lo_iota).astype(jnp.bfloat16)
            for v in range(2 * FIELDS):
                value = parts[v, pl.ds(row, 8, stride=0), :]
                value = jnp.concatenate([value] * 4, axis=0).astype(jnp.bfloat16)
                a_block[32 * v : 32 * v + 32, cols] = pick * value
        packed[...] += lax.dot_general(
            a_block[...],
            b_block[...],
            (((1,), (1,)), ((), ())),
            preferred_element_type=jnp.float32,
        )
        return carry

    lax.fori_loop(0, ROWS // per, pack_step, 0)
    for g in range(GROUPS):
        cols = slice((g & 1) * LANES, (g & 1) * LANES + LANES)
        for v in range(FIELDS):
            r = 32 * v + (g >> 1) * 8
            send_ref[g, v] = (
                packed[r : r + 8, cols] + packed[32 * FIELDS + r : 32 * FIELDS + r + 8, cols]
            )
    stay_copy.wait()


def assemble_kernel(*refs):
    arrived = refs[:GROUPS]
    out_ref, rows, sem = refs[GROUPS + 1 :]
    for g in range(GROUPS):
        for r in range(8):
            col = g * MOST + r * LANES
            for v in range(FIELDS):
                rows[v : v + 1, col : col + LANES] = arrived[g][v, r : r + 1, :]
    copy = pltpu.make_async_copy(
        rows, out_ref.at[:, pl.ds(PART_DEV, GROUPS * MOST)], sem.at[0]
    )
    copy.start()
    copy.wait()


def swapped(block, pairs):
    route = [(a, b) for a, b in pairs] + [(b, a) for a, b in pairs]
    return lax.ppermute(block, "cells", route)


def edge_rows(position, mass, entropy, rho, act, nbr, start, ghost_start):
    wide = slice(start, start + EDGE * CELL_PARTICLES)
    near = slice(ghost_start * CELL_PARTICLES, (ghost_start + GHOST) * CELL_PARTICLES)
    listed = nbr[ghost_start : ghost_start + GHOST].astype(jnp.float32).reshape(-1)
    tail = jnp.pad(listed, (0, 8 * LANES - listed.shape[0]))
    return jnp.concatenate(
        [
            position[:, wide].reshape(-1),
            mass[wide],
            entropy[near],
            rho[near],
            act[near],
            tail,
        ]
    ).reshape(HALO_ROWS, LANES)


def per_device(
    position,
    velocity,
    particle_mass,
    entropy,
    density_old,
    active,
    neighbours,
    destination,
    recv_slot,
):
    count = lax.axis_size("cells")
    own = lax.axis_index("cells")
    all_cells = CELLS_DEV * count
    act_f = (active == 1).astype(jnp.float32)
    low_edge = edge_rows(
        position, particle_mass, entropy, density_old, act_f, neighbours, 0, 0
    )
    high_edge = edge_rows(
        position,
        particle_mass,
        entropy,
        density_old,
        act_f,
        neighbours,
        PART_DEV - EDGE * CELL_PARTICLES,
        CELLS_DEV - GHOST,
    )
    even = own % 2 == 0
    near_pairs = [(2 * k, 2 * k + 1) for k in range(count // 2)]
    far_pairs = [(2 * k + 1, (2 * k + 2) % count) for k in range(count // 2)]
    far = swapped(jnp.where(even, low_edge, high_edge), far_pairs)
    near = swapped(jnp.where(even, high_edge, low_edge), near_pairs)
    left = jnp.where(even, far, near)
    right = jnp.where(even, near, far)
    listed = GHOST * NEIGHBOURS
    lists = jnp.concatenate(
        [
            left[88, :listed].astype(jnp.int32),
            neighbours.reshape(-1),
            right[88, :listed].astype(jnp.int32),
        ]
    )
    lists = (lists - (own * CELLS_DEV - EDGE)) % all_cells

    vm = pl.BlockSpec(memory_space=pltpu.VMEM)
    sm = pl.BlockSpec(memory_space=pltpu.SMEM)
    hbm = pl.BlockSpec(memory_space=pl.ANY)
    square = (ROWS, LANES)
    ext = pltpu.VMEM((EXT_ROWS, LANES), jnp.float32)
    out, send = pl.pallas_call(
        state_kernel,
        out_shape=(
            jax.ShapeDtypeStruct((FIELDS, RECV_DEV), jnp.float32),
            jax.ShapeDtypeStruct((GROUPS, FIELDS, 8, LANES), jnp.float32),
        ),
        in_specs=[sm, sm] + [vm] * 10,
        out_specs=(hbm, vm),
        scratch_shapes=[
            ext,
            ext,
            ext,
            ext,
            ext,
            ext,
            pltpu.VMEM((EXT_ROWS, LANES), jnp.int32),
            ext,
            ext,
            ext,
            ext,
            pltpu.VMEM((FIELDS, ROWS, LANES), jnp.float32),
            pltpu.VMEM((2 * FIELDS, ROWS, LANES), jnp.float32),
            pltpu.VMEM(square, jnp.float32),
            pltpu.VMEM(square, jnp.float32),
            pltpu.VMEM((64 * FIELDS, 4 * LANES), jnp.bfloat16),
            pltpu.VMEM((256, 4 * LANES), jnp.bfloat16),
            pltpu.VMEM((64 * FIELDS, 256), jnp.float32),
            pltpu.VMEM((FIELDS, PART_DEV), jnp.float32),
            pltpu.SMEM((EXT_ROWS, LANES), jnp.int32),
            pltpu.SMEM((LIST_SIZE,), jnp.int32),
            pltpu.SemaphoreType.DMA((2,)),
        ],
        compiler_params=pltpu.CompilerParams(vmem_limit_bytes=40 * 2**20),
    )(
        own.reshape(1),
        lists,
        position,
        velocity,
        particle_mass.reshape(square),
        entropy.reshape(square),
        density_old.reshape(square),
        active.reshape(square),
        destination.reshape(square),
        recv_slot.reshape(square),
        left,
        right,
    )
    offsets = list(range(-REACH, 0)) + list(range(1, REACH + 1))
    arrived = []
    for g, offset in enumerate(offsets):
        route = [((i - offset) % count, i) for i in range(count)]
        arrived.append(lax.ppermute(send[g], "cells", route))
    return pl.pallas_call(
        assemble_kernel,
        out_shape=jax.ShapeDtypeStruct((FIELDS, RECV_DEV), jnp.float32),
        in_specs=[vm] * GROUPS + [hbm],
        out_specs=hbm,
        scratch_shapes=[
            pltpu.VMEM((FIELDS, GROUPS * MOST), jnp.float32),
            pltpu.SemaphoreType.DMA((1,)),
        ],
        input_output_aliases={GROUPS: 0},
        compiler_params=pltpu.CompilerParams(vmem_limit_bytes=16 * 2**20),
    )(*arrived, out)


def solution(mesh):
    placed = (
        P(None, "cells"),
        P(None, "cells"),
        P("cells"),
        P("cells"),
        P("cells"),
        P("cells"),
        P("cells", None),
        P("cells"),
        P("cells"),
    )
    return jax.shard_map(
        per_device, mesh=mesh, in_specs=placed, out_specs=P(None, "cells"), check_vma=False
    )
```

```python
import functools

import jax
import jax.numpy as jnp
from jax import lax
from jax.experimental import pallas as pl
from jax.experimental.pallas import tpu as pltpu
from jax.sharding import PartitionSpec as P

CELL_PARTICLES = 256
HALO = 4
REACH = 4
PART_DEV = 16384
MOST = 1024
RECV_DEV = 24576
CELLS_DEV = 64
NEIGHBOURS = 6
LANES = 128
ROWS = PART_DEV // LANES
EDGE = 2 * HALO
EXT = CELLS_DEV + 2 * EDGE
EXT_ROWS = 2 * EXT
EDGE_ROWS = 2 * EDGE
HALO_ROWS = 96
GHOST = HALO
LISTED = CELLS_DEV + 2 * GHOST
OWN = slice(EDGE_ROWS, EDGE_ROWS + ROWS)
PACK_ROWS = 8
DUMMY = EDGE * 64 + 32 + (8 << 20)
UNROLL = 8
LIST_SIZE = LISTED * 32 + 64
GROUPS = 2 * REACH
time_step = 0.25
FIELDS = 9


def bcast(ref, row):
    return ref[pl.ds(row, 8, stride=0), :]


def edge_kernel(
    own_ref, pos_ref, mass_ref, ent_ref, rho_ref, act_ref, nbr_ref, far_ref, near_ref,
    pos_v, act_v, nbr_v, sem
):
    even = own_ref[0] % 2 == 0
    copies = []
    nbr_copy = pltpu.make_async_copy(nbr_ref, nbr_v, sem.at[0])
    nbr_copy.start()
    for side, ref in enumerate((far_ref, near_ref)):
        low = even if side == 0 else jnp.logical_not(even)
        wide = pl.multiple_of(jnp.where(low, 0, ROWS - EDGE_ROWS), 8)
        near = pl.multiple_of(jnp.where(low, 0, ROWS - 8), 8)
        lane = pl.multiple_of(jnp.where(low, 0, PART_DEV - EDGE * CELL_PARTICLES), LANES)
        base = 1 + 5 * side
        pairs = [
            (pos_ref.at[:, pl.ds(lane, EDGE * CELL_PARTICLES)], pos_v.at[side]),
            (mass_ref.at[pl.ds(wide, EDGE_ROWS)], ref.at[pl.ds(48, EDGE_ROWS)]),
            (ent_ref.at[pl.ds(near, 8)], ref.at[pl.ds(64, 8)]),
            (rho_ref.at[pl.ds(near, 8)], ref.at[pl.ds(72, 8)]),
            (act_ref.at[pl.ds(near, 8)], act_v.at[side]),
        ]
        for k, (a, b) in enumerate(pairs):
            copy = pltpu.make_async_copy(a, b, sem.at[base + k])
            copy.start()
            copies.append(copy)
    nbr_copy.wait()
    for copy in copies:
        copy.wait()
    lists = nbr_v[...].astype(jnp.float32)
    for side, ref in enumerate((far_ref, near_ref)):
        for c in range(3):
            for i in range(EDGE_ROWS):
                ref[16 * c + i : 16 * c + i + 1, :] = (
                    pos_v[side, c : c + 1, i * LANES : (i + 1) * LANES] * 0.5
                )
        ref[80:88, :] = (act_v[side] == 1).astype(jnp.float32)
        ref[88:96, :] = jnp.zeros((8, LANES), jnp.float32)
        ref[88 : 88 + NEIGHBOURS, 0:CELLS_DEV] = lists


def state_kernel(
    own_ref, pos_ref, vel_ref, mass_ref, ent_ref, rho_ref, act_ref, dest_ref, slot_ref,
    nbr_ref, far_ref, near_ref,
    kept_ref, to_far, to_far2, to_next, to_next2, to_other,
    pos_v, vel_v, act_v, dest_v, slot_v, nbr_v,
    xs, ys, zs, ms, ps, es, rho_old, rank, dens, ax, ay, az,
    fields, key, shifts, parts, hi_row, lo_row, a0, b0, packed, blocks,
    table_v, table, chunk_list, sem,
):
    own = own_ref[0]
    even = own % 2 == 0
    scale = 8.0 / (NEIGHBOURS * CELL_PARTICLES)
    loads = [
        (pos_ref, pos_v),
        (vel_ref, vel_v),
        (mass_ref, ms.at[pl.ds(EDGE_ROWS, ROWS)]),
        (ent_ref, es.at[pl.ds(EDGE_ROWS, ROWS)]),
        (rho_ref, rho_old.at[pl.ds(EDGE_ROWS, ROWS)]),
        (act_ref, act_v),
        (dest_ref, dest_v),
        (slot_ref, slot_v),
        (nbr_ref, nbr_v),
    ]
    loads = [pltpu.make_async_copy(a, b, sem.at[k]) for k, (a, b) in enumerate(loads)]
    for copy in loads:
        copy.start()

    def side_rows(first, last):
        f, n = far_ref[first:last, :], near_ref[first:last, :]
        return jnp.where(even, f, n), jnp.where(even, n, f)

    high = slice(EDGE_ROWS + ROWS, EXT_ROWS)
    for k, ref in enumerate((xs, ys, zs, ms)):
        ref[0:EDGE_ROWS, :], ref[high, :] = side_rows(16 * k, 16 * k + 16)
    zeros8 = jnp.zeros((8, LANES), jnp.float32)
    ghost_act = side_rows(80, 88)
    for ref, rows, fill in ((es, (64, 72), 0.0), (rho_old, (72, 80), 1.0)):
        ref[0:8, :] = zeros8 + fill
        ref[EXT_ROWS - 8 :, :] = zeros8 + fill
        ref[8:16, :], ref[EXT_ROWS - 16 : EXT_ROWS - 8, :] = side_rows(*rows)
    for ref in (dens, ax, ay, az, packed):
        ref[...] = jnp.zeros_like(ref)
    for copy in loads:
        copy.wait()

    act = jnp.concatenate(
        [zeros8, ghost_act[0], (act_v[...] == 1).astype(jnp.float32), ghost_act[1], zeros8],
        axis=0,
    )
    before = (
        lax.broadcasted_iota(jnp.int32, (LANES, LANES), 0)
        < lax.broadcasted_iota(jnp.int32, (LANES, LANES), 1)
    ).astype(jnp.bfloat16)
    ones = jnp.ones((LANES, LANES), jnp.bfloat16)
    act16 = act.astype(jnp.bfloat16)
    in_lanes = lax.dot_general(
        ones[0:16], act16, (((1,), (1,)), ((), ())), preferred_element_type=jnp.float32
    )
    table_v[0:8, 0:EXT_ROWS] = in_lanes[0:8].astype(jnp.int32)
    shift = own * CELLS_DEV - EDGE
    near_lists = side_rows(88, 96)
    pad = jnp.zeros((8 - NEIGHBOURS, CELLS_DEV), jnp.int32)
    table_v[8:16, 0:CELLS_DEV] = (jnp.concatenate([nbr_v[...], pad]) - shift) & 8191
    for k in range(2):
        table_v[16 + 8 * k : 24 + 8 * k, 0:LANES] = (
            near_lists[k].astype(jnp.int32) - shift
        ) & 8191
    table_copy = pltpu.make_async_copy(table_v, table, sem.at[9])
    table_copy.start()
    inside = jnp.dot(act16, before, preferred_element_type=jnp.float32)
    total = jnp.dot(act16, ones, preferred_element_type=jnp.float32)
    row_id = lax.broadcasted_iota(jnp.int32, (EXT_ROWS, LANES), 0)
    rank[...] = jnp.where(
        act > 0.5, inside + jnp.where(row_id % 2 == 1, pltpu.roll(total, 1, 0), 0.0), -1.0
    )

    dest = dest_v[...]
    away = (dest - own) & 127
    signed = jnp.where(away > 64, away - 128, away)
    group = jnp.where(signed < 0, signed + REACH, signed + REACH - 1)
    place = (slot_v[...] - PART_DEV) & (MOST - 1)
    moving = dest != own
    hi = (group >> 1) * 8 + (place >> 7)
    lo = (group & 1) * LANES + (place & (LANES - 1))
    key[...] = jnp.where(moving, hi * 256 + lo, -1)
    mover16 = moving.astype(jnp.float32).astype(jnp.bfloat16)
    above = lax.dot_general(
        before, mover16, (((0,), (0,)), ((), ())), preferred_element_type=jnp.float32
    ).astype(jnp.int32)
    in_column = jnp.dot(ones, mover16, preferred_element_type=jnp.float32).astype(jnp.int32)
    own_row = lax.broadcasted_iota(jnp.int32, (ROWS, LANES), 0)
    remaining = jnp.where(moving, own_row - above, 0)
    for bit in range(7):
        coming = pltpu.roll(remaining, ROWS - (1 << bit), 0)
        lands = (coming >> bit) & 1
        leaves = (remaining >> bit) & 1
        shifts[bit] = lands
        remaining = jnp.where(lands == 1, coming, jnp.where(leaves == 1, 0, remaining))
    mover_rows = jnp.max(in_column)

    def moved_up(x):
        for bit in range(7):
            x = jnp.where(shifts[bit] == 1, pltpu.roll(x, ROWS - (1 << bit), 0), x)
        return x

    new_key = jnp.where(own_row < in_column, moved_up(key[...]), -1)
    hi_row[...] = (new_key >> 8).astype(jnp.float32)
    lo_row[...] = (new_key & 255).astype(jnp.float32)

    def split_rows(i, carry):
        col = pl.multiple_of(i * LANES, LANES)
        p = pos_v[:, pl.ds(col, LANES)]
        v = vel_v[:, pl.ds(col, LANES)]
        for c, ref in enumerate((xs, ys, zs)):
            fields[c, pl.ds(i, 1), :] = p[c : c + 1, :]
            fields[3 + c, pl.ds(i, 1), :] = v[c : c + 1, :]
        return carry

    lax.fori_loop(0, ROWS, split_rows, 0, unroll=8)
    for c, ref in enumerate((xs, ys, zs)):
        ref[OWN, :] = fields[c] * 0.5
    fields[6] = rho_old[OWN, :]
    fields[7] = es[OWN, :]
    fields[8] = ms[OWN, :]
    table_copy.wait()

    cells = [(EDGE + k, k, 8) for k in range(CELLS_DEV)]
    cells += [(EDGE - GHOST + k, CELLS_DEV - GHOST + k, 16) for k in range(GHOST)]
    cells += [(EDGE + CELLS_DEV + k, k, 24) for k in range(GHOST)]
    at, most, own_total = 0, 0, 0
    for number, (cell, lane, row) in enumerate(cells):
        n = table[0, 2 * cell] + table[0, 2 * cell + 1]
        code = (row << 20) + (lane << 13) + (cell << 6)
        for k in range(4):
            chunk_list[at + k] = code + k
        at = at + ((n + 7) >> 3)
        most = jnp.maximum(most, n)
        if number == CELLS_DEV - 1:
            own_total = at
    all_total = at

    @pl.when(most > 32)
    def _():
        def refill(first, count, lane0, row):
            def one(k, start):
                cell = first + k
                n = table[0, 2 * cell] + table[0, 2 * cell + 1]
                code = (row << 20) + ((lane0 + k) << 13) + (cell << 6)

                def put(j, carry):
                    chunk_list[start + j] = code + j
                    return carry

                lax.fori_loop(0, (n + 7) >> 3, put, 0)
                return start + ((n + 7) >> 3)

            return lambda start: lax.fori_loop(0, count, one, start)

        start = refill(EDGE, CELLS_DEV, 0, 8)(0)
        start = refill(EDGE - GHOST, GHOST, CELLS_DEV - GHOST, 16)(start)
        refill(EDGE + CELLS_DEV, GHOST, 0, 24)(start)

    sub = lax.broadcasted_iota(jnp.int32, (8, LANES), 0).astype(jnp.float32)

    def chunk_of(position, limit):
        code = chunk_list[jnp.maximum(jnp.minimum(position, limit - 1), 0)]
        code = jnp.where(position < limit, code, DUMMY)
        cell = (code >> 6) & 127
        want = sub + ((code & 63) * 8).astype(jnp.float32)
        picks = [bcast(rank, 2 * cell + h) == want for h in range(2)]
        lane = (code >> 13) & 127
        sources = [table[(code >> 20) + q, lane] for q in range(NEIGHBOURS)]
        return cell, picks, sources

    def column(ref, cell, picks):
        both = jnp.where(picks[0], bcast(ref, 2 * cell), 0.0) + jnp.where(
            picks[1], bcast(ref, 2 * cell + 1), 0.0
        )
        return jnp.sum(both, axis=1, keepdims=True)

    def spread(ref, cell, picks, value):
        for h in range(2):
            row = jnp.sum(jnp.where(picks[h], value, 0.0), axis=0, keepdims=True)
            ref[pl.ds(2 * cell + h, 1), :] += row

    def density_step(step):
        done = []
        for u in range(UNROLL):
            cell, picks, sources = chunk_of(step * UNROLL + u, all_total)
            cx, cy, cz = (column(ref, cell, picks) for ref in (xs, ys, zs))
            total_rows = jnp.zeros((8, LANES), jnp.float32)
            for source in sources:
                for h in range(2):
                    row = 2 * source + h
                    dx = cx - bcast(xs, row)
                    dy = cy - bcast(ys, row)
                    dz = cz - bcast(zs, row)
                    u1 = jnp.maximum(1.0 - (dx * dx + dy * dy + dz * dz), 0.0)
                    total_rows += u1 * u1 * u1 * bcast(ms, row)
            value = jnp.sum(total_rows, axis=1, keepdims=True) * scale
            done.append((cell, picks, value))
        for cell, picks, value in done:
            spread(dens, cell, picks, value)

    def density_loop(step, carry):
        density_step(step)
        return carry

    lax.fori_loop(0, (all_total + UNROLL - 1) // UNROLL, density_loop, 0)

    rho = jnp.where(rank[...] >= 0.0, dens[...], rho_old[...])
    dens[...] = rho
    ps[...] = es[...] * jnp.exp(jnp.log(rho) * (-1.0 / 3.0))

    def force_step(step, carry):
        done = []
        for u in range(UNROLL):
            cell, picks, sources = chunk_of(step * UNROLL + u, own_total)
            cx, cy, cz, cp = (column(ref, cell, picks) for ref in (xs, ys, zs, ps))
            sx = jnp.zeros((8, LANES), jnp.float32)
            sy = jnp.zeros((8, LANES), jnp.float32)
            sz = jnp.zeros((8, LANES), jnp.float32)
            for source in sources:
                for h in range(2):
                    row = 2 * source + h
                    dx = cx - bcast(xs, row)
                    dy = cy - bcast(ys, row)
                    dz = cz - bcast(zs, row)
                    u1 = jnp.maximum(1.0 - (dx * dx + dy * dy + dz * dz), 0.0)
                    w = u1 * u1 * (bcast(ms, row) * (cp + bcast(ps, row)))
                    sx += w * dx
                    sy += w * dy
                    sz += w * dz
            values = [
                jnp.sum(s, axis=1, keepdims=True) * (3.0 * scale * time_step)
                for s in (sx, sy, sz)
            ]
            done.append((cell, picks, values))
        for cell, picks, values in done:
            for ref, value in zip((ax, ay, az), values):
                spread(ref, cell, picks, value)
        return carry

    lax.fori_loop(0, (own_total + UNROLL - 1) // UNROLL, force_step, 0)

    for c, acc in enumerate((ax, ay, az)):
        kicked = fields[3 + c] + acc[OWN, :]
        fields[3 + c] = kicked
        fields[c] = fields[c] + time_step * kicked
    fields[6] = dens[OWN, :]
    stays = dest_v[...] == own
    for v in range(FIELDS):
        whole = fields[v]
        kept_ref[v] = jnp.where(stays, whole, 0.0)
        whole = moved_up(whole)
        first = whole.astype(jnp.bfloat16).astype(jnp.float32)
        parts[v] = first
        parts[FIELDS + v] = whole - first

    bf = jnp.bfloat16
    iota16 = lax.broadcasted_iota(jnp.int32, (16, LANES), 0).astype(jnp.float32).astype(bf)
    one16, zero16 = jnp.ones((16, LANES), bf), jnp.zeros((16, LANES), bf)

    def twice(x):
        return jnp.concatenate([x, x], axis=0).astype(bf)

    def pack_step(step, carry):
        for j in range(PACK_ROWS):
            row = step * PACK_ROWS + j
            cols = slice(j * LANES, (j + 1) * LANES)
            hi_b, lo_b = twice(bcast(hi_row, row)), twice(bcast(lo_row, row))
            for k in range(16):
                b0[16 * k : 16 * k + 16, cols] = jnp.where(
                    lo_b == iota16 + bf(16 * k), one16, zero16
                )
            upper = hi_b == iota16
            lower = hi_b == iota16 + bf(16)
            for v in range(2 * FIELDS):
                value = twice(parts[v, pl.ds(row, 8, stride=0), :])
                a0[32 * v : 32 * v + 16, cols] = jnp.where(upper, value, zero16)
                a0[32 * v + 16 : 32 * v + 32, cols] = jnp.where(lower, value, zero16)
        packed[...] += lax.dot_general(
            a0[...], b0[...], (((1,), (1,)), ((), ())), preferred_element_type=jnp.float32
        )
        return carry

    lax.fori_loop(0, (mover_rows + PACK_ROWS - 1) // PACK_ROWS, pack_step, 0)

    for g in range(GROUPS):
        cols = slice((g & 1) * LANES, (g & 1) * LANES + LANES)
        for v in range(FIELDS):
            r = 32 * v + (g >> 1) * 8
            s = r + 32 * FIELDS
            blocks[g, v] = packed[r : r + 8, cols] + packed[s : s + 8, cols]
    turn = 1 - 2 * (own & 1)
    for ref, step in zip((to_next, to_next2, to_far, to_far2), chip_steps(own)):
        ref[0] = blocks[group_of(2 * step)]
        ref[1] = blocks[group_of(2 * step + turn)]
    to_other[...] = blocks[group_of(turn)]


def chip_steps(own):
    even = jnp.where((own >> 1) & 1 == 0, 1, -1)
    low = jnp.where((own >> 2) & 1 == 0, 2, -2)
    return even, -even, low, -low


def group_of(offset):
    g = jnp.where(offset < 0, offset + REACH, offset + REACH - 1)
    return jnp.minimum(jnp.maximum(g, 0), GROUPS - 1)


def stay_kernel(kept_ref, out_ref, rows, sem):
    def step(i, carry):
        col = pl.multiple_of(i * LANES, LANES)
        for v in range(FIELDS):
            rows[v : v + 1, pl.ds(col, LANES)] = kept_ref[v, pl.ds(i, 1), :]
        return carry

    lax.fori_loop(0, ROWS, step, 0, unroll=8)
    copy = pltpu.make_async_copy(rows, out_ref.at[:, pl.ds(0, PART_DEV)], sem.at[0])
    copy.start()
    copy.wait()


def assemble_kernel(
    own_ref, next_ref, next2_ref, far_ref, far2_ref, other_ref,
    x_next, x_next2, x_far, x_far2, held_ref, out_ref, rows, sem
):
    del held_ref
    own = own_ref[0]
    turn = 1 - 2 * (own & 1)
    steps = chip_steps(own)
    low = (own >> 2) & 1 == 0
    pick_low = low == (turn < 0)
    parts = [(ref, (0,), -2 * step) for ref, step in zip((next_ref, next2_ref, far_ref, far2_ref), steps)]
    parts += [(ref, (1,), -2 * step - turn) for ref, step in zip((x_next, x_next2), steps)]
    parts += [(other_ref, (), -turn)]
    parts += [(None, (), 3 * turn)]

    for ref, index, offset in parts:
        start = group_of(offset) * MOST
        for v in range(FIELDS):
            if ref is None:
                tile = jnp.where(pick_low, x_far[1, v], x_far2[1, v])
            else:
                tile = ref[index + (v,)]
            for r in range(8):
                col = pl.multiple_of(start + r * LANES, LANES)
                rows[v : v + 1, pl.ds(col, LANES)] = tile[r : r + 1, :]
    copy = pltpu.make_async_copy(
        rows, out_ref.at[:, pl.ds(PART_DEV, GROUPS * MOST)], sem.at[0]
    )
    copy.start()
    copy.wait()


def swapped(block, pairs):
    route = [(a, b) for a, b in pairs] + [(b, a) for a, b in pairs]
    return lax.ppermute(block, "cells", route)


def per_device(
    position,
    velocity,
    particle_mass,
    entropy,
    density_old,
    active,
    neighbours,
    destination,
    recv_slot,
):
    count = lax.axis_size("cells")
    own = lax.axis_index("cells").reshape(1)
    square = (ROWS, LANES)
    mass, ent, rho, act = (
        a.reshape(square) for a in (particle_mass, entropy, density_old, active)
    )
    lists = neighbours.T
    vm = pl.BlockSpec(memory_space=pltpu.VMEM)
    sm = pl.BlockSpec(memory_space=pltpu.SMEM)
    hbm = pl.BlockSpec(memory_space=pl.ANY)
    f32, i32 = jnp.float32, jnp.int32
    far, near = pl.pallas_call(
        edge_kernel,
        out_shape=(jax.ShapeDtypeStruct((HALO_ROWS, LANES), f32),) * 2,
        in_specs=[sm] + [hbm] * 6,
        out_specs=(vm, vm),
        scratch_shapes=[
            pltpu.VMEM((2, 3, EDGE * CELL_PARTICLES), f32),
            pltpu.VMEM((2, 8, LANES), i32),
            pltpu.VMEM((NEIGHBOURS, CELLS_DEV), i32),
            pltpu.SemaphoreType.DMA((11,)),
        ],
        compiler_params=pltpu.CompilerParams(vmem_limit_bytes=56 * 2**20),
    )(own, position, mass, ent, rho, act, lists)
    near_pairs = [(2 * k, 2 * k + 1) for k in range(count // 2)]
    far_pairs = [(2 * k + 1, (2 * k + 2) % count) for k in range(count // 2)]
    far = swapped(far, far_pairs)
    near = swapped(near, near_pairs)

    ext = pltpu.VMEM((EXT_ROWS, LANES), f32)
    flat = pltpu.VMEM((3, PART_DEV), f32)
    whole = pltpu.VMEM(square, i32)
    pair = jax.ShapeDtypeStruct((2, FIELDS, 8, LANES), f32)
    kept, *sends = pl.pallas_call(
        state_kernel,
        out_shape=(
            jax.ShapeDtypeStruct((FIELDS, ROWS, LANES), f32),
            pair,
            pair,
            pair,
            pair,
            jax.ShapeDtypeStruct((FIELDS, 8, LANES), f32),
        ),
        in_specs=[sm] + [hbm] * 9 + [vm] * 2,
        out_specs=(vm,) * 6,
        scratch_shapes=[flat, flat, whole, whole, whole]
        + [pltpu.VMEM((NEIGHBOURS, CELLS_DEV), i32)]
        + [ext] * 12
        + [
            pltpu.VMEM((FIELDS, ROWS, LANES), f32),
            whole,
            pltpu.VMEM((7, ROWS, LANES), i32),
            pltpu.VMEM((2 * FIELDS, ROWS, LANES), f32),
            pltpu.VMEM(square, f32),
            pltpu.VMEM(square, f32),
            pltpu.VMEM((64 * FIELDS, PACK_ROWS * LANES), jnp.bfloat16),
            pltpu.VMEM((256, PACK_ROWS * LANES), jnp.bfloat16),
            pltpu.VMEM((64 * FIELDS, 256), f32),
            pltpu.VMEM((GROUPS, FIELDS, 8, LANES), f32),
            pltpu.VMEM((32, 256), i32),
            pltpu.SMEM((32, 256), i32),
            pltpu.SMEM((LIST_SIZE,), i32),
            pltpu.SemaphoreType.DMA((10,)),
        ],
        compiler_params=pltpu.CompilerParams(vmem_limit_bytes=56 * 2**20),
    )(
        own,
        position,
        velocity,
        mass,
        ent,
        rho,
        act,
        destination.reshape(square),
        recv_slot.reshape(square),
        lists,
        far,
        near,
    )
    to_far, to_far2, to_next, to_next2, to_other = sends
    chips = count // 2

    def chip_pairs(distance, first):
        firsts = [c for c in range(chips) if (c // distance) % 2 == first]
        return [
            (2 * c + core, 2 * ((c + distance) % chips) + core)
            for c in firsts
            for core in range(2)
        ]

    other = swapped(to_other, near_pairs)
    next2 = swapped(to_next2, chip_pairs(1, 1))
    far2 = swapped(to_far2, chip_pairs(2, 1))
    next1 = swapped(to_next, chip_pairs(1, 0))
    far1 = swapped(to_far, chip_pairs(2, 0))
    crossed = [swapped(x, near_pairs) for x in (next1, next2, far1, far2)]
    held = pl.pallas_call(
        stay_kernel,
        out_shape=jax.ShapeDtypeStruct((FIELDS, RECV_DEV), f32),
        in_specs=[vm],
        out_specs=hbm,
        scratch_shapes=[
            pltpu.VMEM((FIELDS, PART_DEV), f32),
            pltpu.SemaphoreType.DMA((1,)),
        ],
        compiler_params=pltpu.CompilerParams(vmem_limit_bytes=16 * 2**20),
    )(kept)
    return pl.pallas_call(
        assemble_kernel,
        out_shape=jax.ShapeDtypeStruct((FIELDS, RECV_DEV), f32),
        in_specs=[sm] + [vm] * 9 + [hbm],
        out_specs=hbm,
        scratch_shapes=[
            pltpu.VMEM((FIELDS, GROUPS * MOST), f32),
            pltpu.SemaphoreType.DMA((1,)),
        ],
        input_output_aliases={10: 0},
        compiler_params=pltpu.CompilerParams(vmem_limit_bytes=16 * 2**20),
    )(own, next1, next2, far1, far2, other, *crossed, held)


def solution(mesh):
    placed = (
        P(None, "cells"),
        P(None, "cells"),
        P("cells"),
        P("cells"),
        P("cells"),
        P("cells"),
        P("cells", None),
        P("cells"),
        P("cells"),
    )
    return jax.shard_map(
        per_device, mesh=mesh, in_specs=placed, out_specs=P(None, "cells"), check_vma=False
    )
```

```python
import functools

import jax
import jax.numpy as jnp
from jax import lax
from jax.experimental import pallas as pl
from jax.experimental.pallas import tpu as pltpu
from jax.sharding import PartitionSpec as P

CELL_PARTICLES = 256
HALO = 4
REACH = 4
PART_DEV = 16384
MOST = 1024
RECV_DEV = 24576
CELLS_DEV = 64
NEIGHBOURS = 6
LANES = 128
ROWS = PART_DEV // LANES
EDGE = 2 * HALO
EXT = CELLS_DEV + 2 * EDGE
EXT_ROWS = 2 * EXT
EDGE_ROWS = 2 * EDGE
HALO_ROWS = 96
GHOST = HALO
LISTED = CELLS_DEV + 2 * GHOST
OWN = slice(EDGE_ROWS, EDGE_ROWS + ROWS)
PACK_ROWS = 8
DUMMY = EDGE * 64 + 32 + (8 << 20)
UNROLL = 16
LIST_SIZE = LISTED * 32 + 64
GROUPS = 2 * REACH
time_step = 0.25
FIELDS = 9


def bcast(ref, row):
    return ref[pl.ds(row, 8, stride=0), :]


def edge_kernel(
    own_ref, pos_ref, mass_ref, ent_ref, rho_ref, act_ref, nbr_ref, far_ref, near_ref,
    pos_v, act_v, nbr_v, sem
):
    even = own_ref[0] % 2 == 0
    copies = []
    nbr_copy = pltpu.make_async_copy(nbr_ref, nbr_v, sem.at[0])
    nbr_copy.start()
    for side, ref in enumerate((far_ref, near_ref)):
        low = even if side == 0 else jnp.logical_not(even)
        wide = pl.multiple_of(jnp.where(low, 0, ROWS - EDGE_ROWS), 8)
        near = pl.multiple_of(jnp.where(low, 0, ROWS - 8), 8)
        lane = pl.multiple_of(jnp.where(low, 0, PART_DEV - EDGE * CELL_PARTICLES), LANES)
        base = 1 + 5 * side
        pairs = [
            (pos_ref.at[:, pl.ds(lane, EDGE * CELL_PARTICLES)], pos_v.at[side]),
            (mass_ref.at[pl.ds(wide, EDGE_ROWS)], ref.at[pl.ds(48, EDGE_ROWS)]),
            (ent_ref.at[pl.ds(near, 8)], ref.at[pl.ds(64, 8)]),
            (rho_ref.at[pl.ds(near, 8)], ref.at[pl.ds(72, 8)]),
            (act_ref.at[pl.ds(near, 8)], act_v.at[side]),
        ]
        for k, (a, b) in enumerate(pairs):
            copy = pltpu.make_async_copy(a, b, sem.at[base + k])
            copy.start()
            copies.append(copy)
    nbr_copy.wait()
    for copy in copies:
        copy.wait()
    lists = nbr_v[...].astype(jnp.float32)
    for side, ref in enumerate((far_ref, near_ref)):
        for c in range(3):
            for i in range(EDGE_ROWS):
                ref[16 * c + i : 16 * c + i + 1, :] = (
                    pos_v[side, c : c + 1, i * LANES : (i + 1) * LANES] * 0.5
                )
        ref[80:88, :] = (act_v[side] == 1).astype(jnp.float32)
        ref[88:96, :] = jnp.zeros((8, LANES), jnp.float32)
        ref[88 : 88 + NEIGHBOURS, 0:CELLS_DEV] = lists


def state_kernel(
    own_ref, pos_ref, vel_ref, mass_ref, ent_ref, rho_ref, act_ref, dest_ref, slot_ref,
    nbr_ref, far_in, near_in,
    kept_ref, to_far, to_far2, to_next, to_next2, to_other,
    pos_v, vel_v, act_v, dest_v, slot_v, nbr_v,
    xs, ys, zs, ms, ps, es, rho_old, rank, dens, ax, ay, az,
    fields, key, shifts, parts, hi_row, lo_row, a0, b0, packed, blocks,
    far_ref, near_ref, table_v, table, chunk_list, sem,
):
    own = own_ref[0]
    even = own % 2 == 0
    scale = 8.0 / (NEIGHBOURS * CELL_PARTICLES)
    loads = [
        (act_ref, act_v),
        (nbr_ref, nbr_v),
        (far_in, far_ref),
        (near_in, near_ref),
        (dest_ref, dest_v),
        (slot_ref, slot_v),
        (rho_ref, rho_old.at[pl.ds(EDGE_ROWS, ROWS)]),
        (mass_ref, ms.at[pl.ds(EDGE_ROWS, ROWS)]),
        (ent_ref, es.at[pl.ds(EDGE_ROWS, ROWS)]),
        (pos_ref, pos_v),
        (vel_ref, vel_v),
    ]
    loads = [pltpu.make_async_copy(a, b, sem.at[k]) for k, (a, b) in enumerate(loads)]
    for copy in loads:
        copy.start()
    for ref in (dens, ax, ay, az, packed):
        ref[...] = jnp.zeros_like(ref)
    for copy in loads[:4]:
        copy.wait()

    def side_rows(first, last):
        f, n = far_ref[first:last, :], near_ref[first:last, :]
        return jnp.where(even, f, n), jnp.where(even, n, f)

    zeros8 = jnp.zeros((8, LANES), jnp.float32)
    ghost_act = side_rows(80, 88)

    act = jnp.concatenate(
        [zeros8, ghost_act[0], (act_v[...] == 1).astype(jnp.float32), ghost_act[1], zeros8],
        axis=0,
    )
    before = (
        lax.broadcasted_iota(jnp.int32, (LANES, LANES), 0)
        < lax.broadcasted_iota(jnp.int32, (LANES, LANES), 1)
    ).astype(jnp.bfloat16)
    ones = jnp.ones((LANES, LANES), jnp.bfloat16)
    act16 = act.astype(jnp.bfloat16)
    in_lanes = lax.dot_general(
        ones[0:16], act16, (((1,), (1,)), ((), ())), preferred_element_type=jnp.float32
    )
    halves = lax.broadcasted_iota(jnp.int32, (EXT_ROWS, LANES), 0) >> 1
    joined = (halves == lax.broadcasted_iota(jnp.int32, (EXT_ROWS, LANES), 1)).astype(jnp.bfloat16)
    in_cells = jnp.dot(in_lanes.astype(jnp.bfloat16), joined, preferred_element_type=jnp.float32)
    table_v[0:8, :] = in_cells[0:8].astype(jnp.int32)
    shift = own * CELLS_DEV - EDGE
    near_lists = side_rows(88, 96)
    pad = jnp.zeros((8 - NEIGHBOURS, CELLS_DEV), jnp.int32)
    table_v[8:16, 0:CELLS_DEV] = (jnp.concatenate([nbr_v[...], pad]) - shift) & 8191
    for k in range(2):
        table_v[16 + 8 * k : 24 + 8 * k, 0:LANES] = (
            near_lists[k].astype(jnp.int32) - shift
        ) & 8191
    table_copy = pltpu.make_async_copy(table_v, table, sem.at[11])
    table_copy.start()
    high = slice(EDGE_ROWS + ROWS, EXT_ROWS)
    for k, ref in enumerate((xs, ys, zs, ms)):
        ref[0:EDGE_ROWS, :], ref[high, :] = side_rows(16 * k, 16 * k + 16)
    for ref, rows, fill in ((es, (64, 72), 0.0), (rho_old, (72, 80), 1.0)):
        ref[0:8, :] = zeros8 + fill
        ref[EXT_ROWS - 8 :, :] = zeros8 + fill
        ref[8:16, :], ref[EXT_ROWS - 16 : EXT_ROWS - 8, :] = side_rows(*rows)
    inside = jnp.dot(act16, before, preferred_element_type=jnp.float32)
    total = jnp.dot(act16, ones, preferred_element_type=jnp.float32)
    row_id = lax.broadcasted_iota(jnp.int32, (EXT_ROWS, LANES), 0)
    rank[...] = jnp.where(
        act > 0.5, inside + jnp.where(row_id % 2 == 1, pltpu.roll(total, 1, 0), 0.0), -1.0
    )

    for copy in loads[4:]:
        copy.wait()

    dest = dest_v[...]
    away = (dest - own) & 127
    signed = jnp.where(away > 64, away - 128, away)
    group = jnp.where(signed < 0, signed + REACH, signed + REACH - 1)
    place = (slot_v[...] - PART_DEV) & (MOST - 1)
    moving = dest != own
    hi = (group >> 1) * 8 + (place >> 7)
    lo = (group & 1) * LANES + (place & (LANES - 1))
    key[...] = jnp.where(moving, hi * 256 + lo, -1)
    mover16 = moving.astype(jnp.float32).astype(jnp.bfloat16)
    above = lax.dot_general(
        before, mover16, (((0,), (0,)), ((), ())), preferred_element_type=jnp.float32
    ).astype(jnp.int32)
    in_column = jnp.dot(ones, mover16, preferred_element_type=jnp.float32).astype(jnp.int32)
    own_row = lax.broadcasted_iota(jnp.int32, (ROWS, LANES), 0)
    remaining = jnp.where(moving, own_row - above, 0)
    for bit in range(7):
        coming = pltpu.roll(remaining, ROWS - (1 << bit), 0)
        lands = (coming >> bit) & 1
        leaves = (remaining >> bit) & 1
        shifts[bit] = lands
        remaining = jnp.where(lands == 1, coming, jnp.where(leaves == 1, 0, remaining))
    mover_rows = jnp.max(in_column)

    def moved_up(x):
        for bit in range(7):
            x = jnp.where(shifts[bit] == 1, pltpu.roll(x, ROWS - (1 << bit), 0), x)
        return x

    new_key = jnp.where(own_row < in_column, moved_up(key[...]), -1)
    hi_row[...] = (new_key >> 8).astype(jnp.float32)
    lo_row[...] = (new_key & 255).astype(jnp.float32)

    def split_rows(i, carry):
        col = pl.multiple_of(i * LANES, LANES)
        p = pos_v[:, pl.ds(col, LANES)]
        v = vel_v[:, pl.ds(col, LANES)]
        for c, ref in enumerate((xs, ys, zs)):
            fields[c, pl.ds(i, 1), :] = p[c : c + 1, :]
            fields[3 + c, pl.ds(i, 1), :] = v[c : c + 1, :]
        return carry

    lax.fori_loop(0, ROWS, split_rows, 0, unroll=8)
    for c, ref in enumerate((xs, ys, zs)):
        ref[OWN, :] = fields[c] * 0.5
    fields[6] = rho_old[OWN, :]
    fields[7] = es[OWN, :]
    fields[8] = ms[OWN, :]
    table_copy.wait()

    cells = [(EDGE + k, k, 8) for k in range(CELLS_DEV)]
    cells += [(EDGE - GHOST + k, CELLS_DEV - GHOST + k, 16) for k in range(GHOST)]
    cells += [(EDGE + CELLS_DEV + k, k, 24) for k in range(GHOST)]
    at, most, own_total = 0, 0, 0
    for number, (cell, lane, row) in enumerate(cells):
        n = table[0, cell]
        code = (row << 20) + (lane << 13) + (cell << 6)
        for k in range(4):
            chunk_list[at + k] = code + k
        at = at + ((n + 7) >> 3)
        most = jnp.maximum(most, n)
        if number == CELLS_DEV - 1:
            own_total = at
    all_total = at

    @pl.when(most > 32)
    def _():
        def refill(first, count, lane0, row):
            def one(k, start):
                cell = first + k
                n = table[0, cell]
                code = (row << 20) + ((lane0 + k) << 13) + (cell << 6)

                def put(j, carry):
                    chunk_list[start + j] = code + j
                    return carry

                lax.fori_loop(0, (n + 7) >> 3, put, 0)
                return start + ((n + 7) >> 3)

            return lambda start: lax.fori_loop(0, count, one, start)

        start = refill(EDGE, CELLS_DEV, 0, 8)(0)
        start = refill(EDGE - GHOST, GHOST, CELLS_DEV - GHOST, 16)(start)
        refill(EDGE + CELLS_DEV, GHOST, 0, 24)(start)

    sub = lax.broadcasted_iota(jnp.int32, (8, LANES), 0).astype(jnp.float32)

    def chunk_of(position, limit):
        code = chunk_list[jnp.maximum(jnp.minimum(position, limit - 1), 0)]
        code = jnp.where(position < limit, code, DUMMY)
        cell = (code >> 6) & 127
        want = sub + ((code & 63) * 8).astype(jnp.float32)
        picks = [bcast(rank, 2 * cell + h) == want for h in range(2)]
        lane = (code >> 13) & 127
        sources = [table[(code >> 20) + q, lane] for q in range(NEIGHBOURS)]
        return cell, picks, sources

    def column(ref, cell, picks):
        both = jnp.where(picks[0], bcast(ref, 2 * cell), 0.0) + jnp.where(
            picks[1], bcast(ref, 2 * cell + 1), 0.0
        )
        return jnp.sum(both, axis=1, keepdims=True)

    def spread(ref, cell, picks, value):
        for h in range(2):
            row = jnp.sum(jnp.where(picks[h], value, 0.0), axis=0, keepdims=True)
            ref[pl.ds(2 * cell + h, 1), :] += row

    def density_step(step):
        done = []
        for u in range(UNROLL):
            cell, picks, sources = chunk_of(step * UNROLL + u, all_total)
            cx, cy, cz = (column(ref, cell, picks) for ref in (xs, ys, zs))
            total_rows = jnp.zeros((8, LANES), jnp.float32)
            for source in sources:
                for h in range(2):
                    row = 2 * source + h
                    dx = cx - bcast(xs, row)
                    dy = cy - bcast(ys, row)
                    dz = cz - bcast(zs, row)
                    u1 = jnp.maximum(1.0 - (dx * dx + dy * dy + dz * dz), 0.0)
                    total_rows += u1 * u1 * u1 * bcast(ms, row)
            value = jnp.sum(total_rows, axis=1, keepdims=True) * scale
            done.append((cell, picks, value))
        for cell, picks, value in done:
            spread(dens, cell, picks, value)

    def density_loop(step, carry):
        density_step(step)
        return carry

    lax.fori_loop(0, (all_total + UNROLL - 1) // UNROLL, density_loop, 0)

    rho = jnp.where(rank[...] >= 0.0, dens[...], rho_old[...])
    dens[...] = rho
    ps[...] = es[...] * jnp.exp(jnp.log(rho) * (-1.0 / 3.0))

    def force_step(step, carry):
        done = []
        for u in range(UNROLL):
            cell, picks, sources = chunk_of(step * UNROLL + u, own_total)
            cx, cy, cz, cp = (column(ref, cell, picks) for ref in (xs, ys, zs, ps))
            sx = jnp.zeros((8, LANES), jnp.float32)
            sy = jnp.zeros((8, LANES), jnp.float32)
            sz = jnp.zeros((8, LANES), jnp.float32)
            for source in sources:
                for h in range(2):
                    row = 2 * source + h
                    dx = cx - bcast(xs, row)
                    dy = cy - bcast(ys, row)
                    dz = cz - bcast(zs, row)
                    u1 = jnp.maximum(1.0 - (dx * dx + dy * dy + dz * dz), 0.0)
                    w = u1 * u1 * (bcast(ms, row) * (cp + bcast(ps, row)))
                    sx += w * dx
                    sy += w * dy
                    sz += w * dz
            values = [
                jnp.sum(s, axis=1, keepdims=True) * (3.0 * scale * time_step)
                for s in (sx, sy, sz)
            ]
            done.append((cell, picks, values))
        for cell, picks, values in done:
            for ref, value in zip((ax, ay, az), values):
                spread(ref, cell, picks, value)
        return carry

    lax.fori_loop(0, (own_total + UNROLL - 1) // UNROLL, force_step, 0)

    for c, acc in enumerate((ax, ay, az)):
        kicked = fields[3 + c] + acc[OWN, :]
        fields[3 + c] = kicked
        fields[c] = fields[c] + time_step * kicked
    fields[6] = dens[OWN, :]
    stays = dest_v[...] == own
    for v in range(FIELDS):
        whole = fields[v]
        kept_ref[v] = jnp.where(stays, whole, 0.0)
        whole = moved_up(whole)
        first = whole.astype(jnp.bfloat16).astype(jnp.float32)
        parts[v] = first
        parts[FIELDS + v] = whole - first

    bf = jnp.bfloat16
    iota16 = lax.broadcasted_iota(jnp.int32, (16, LANES), 0).astype(jnp.float32).astype(bf)
    one16, zero16 = jnp.ones((16, LANES), bf), jnp.zeros((16, LANES), bf)

    def twice(x):
        return jnp.concatenate([x, x], axis=0).astype(bf)

    def pack_step(step, carry):
        for j in range(PACK_ROWS):
            row = step * PACK_ROWS + j
            cols = slice(j * LANES, (j + 1) * LANES)
            hi_b, lo_b = twice(bcast(hi_row, row)), twice(bcast(lo_row, row))
            for k in range(16):
                b0[16 * k : 16 * k + 16, cols] = jnp.where(
                    lo_b == iota16 + bf(16 * k), one16, zero16
                )
            upper = hi_b == iota16
            lower = hi_b == iota16 + bf(16)
            for v in range(2 * FIELDS):
                value = twice(parts[v, pl.ds(row, 8, stride=0), :])
                a0[32 * v : 32 * v + 16, cols] = jnp.where(upper, value, zero16)
                a0[32 * v + 16 : 32 * v + 32, cols] = jnp.where(lower, value, zero16)
        packed[...] += lax.dot_general(
            a0[...], b0[...], (((1,), (1,)), ((), ())), preferred_element_type=jnp.float32
        )
        return carry

    lax.fori_loop(0, (mover_rows + PACK_ROWS - 1) // PACK_ROWS, pack_step, 0)

    for g in range(GROUPS):
        cols = slice((g & 1) * LANES, (g & 1) * LANES + LANES)
        for v in range(FIELDS):
            r = 32 * v + (g >> 1) * 8
            s = r + 32 * FIELDS
            blocks[g, v] = packed[r : r + 8, cols] + packed[s : s + 8, cols]
    turn = 1 - 2 * (own & 1)
    for ref, step in zip((to_next, to_next2, to_far, to_far2), chip_steps(own)):
        ref[0] = blocks[group_of(2 * step)]
        ref[1] = blocks[group_of(2 * step + turn)]
    to_other[...] = blocks[group_of(turn)]


def chip_steps(own):
    even = jnp.where((own >> 1) & 1 == 0, 1, -1)
    low = jnp.where((own >> 2) & 1 == 0, 2, -2)
    return even, -even, low, -low


def group_of(offset):
    g = jnp.where(offset < 0, offset + REACH, offset + REACH - 1)
    return jnp.minimum(jnp.maximum(g, 0), GROUPS - 1)


def stay_kernel(kept_ref, out_ref, kept_v, rows, sem):
    load = pltpu.make_async_copy(kept_ref, kept_v, sem.at[1])
    load.start()
    load.wait()

    def step(i, carry):
        col = pl.multiple_of(i * LANES, LANES)
        for v in range(FIELDS):
            rows[v : v + 1, pl.ds(col, LANES)] = kept_v[v, pl.ds(i, 1), :]
        return carry

    lax.fori_loop(0, ROWS, step, 0, unroll=8)
    copy = pltpu.make_async_copy(rows, out_ref.at[:, pl.ds(0, PART_DEV)], sem.at[0])
    copy.start()
    copy.wait()


def assemble_kernel(
    own_ref, next_ref, next2_ref, far_ref, far2_ref, other_ref,
    x_next, x_next2, x_far, x_far2, held_ref, out_ref, rows, sem
):
    del held_ref
    own = own_ref[0]
    turn = 1 - 2 * (own & 1)
    steps = chip_steps(own)
    low = (own >> 2) & 1 == 0
    pick_low = low == (turn < 0)
    parts = [(ref, (0,), -2 * step) for ref, step in zip((next_ref, next2_ref, far_ref, far2_ref), steps)]
    parts += [(ref, (1,), -2 * step - turn) for ref, step in zip((x_next, x_next2), steps)]
    parts += [(other_ref, (), -turn)]
    parts += [(None, (), 3 * turn)]

    for ref, index, offset in parts:
        start = group_of(offset) * MOST
        for v in range(FIELDS):
            if ref is None:
                tile = jnp.where(pick_low, x_far[1, v], x_far2[1, v])
            else:
                tile = ref[index + (v,)]
            for r in range(8):
                col = pl.multiple_of(start + r * LANES, LANES)
                rows[v : v + 1, pl.ds(col, LANES)] = tile[r : r + 1, :]
    copy = pltpu.make_async_copy(
        rows, out_ref.at[:, pl.ds(PART_DEV, GROUPS * MOST)], sem.at[0]
    )
    copy.start()
    copy.wait()


def swapped(block, pairs):
    route = [(a, b) for a, b in pairs] + [(b, a) for a, b in pairs]
    return lax.ppermute(block, "cells", route)


def per_device(
    position,
    velocity,
    particle_mass,
    entropy,
    density_old,
    active,
    neighbours,
    destination,
    recv_slot,
):
    count = lax.axis_size("cells")
    own = lax.axis_index("cells").reshape(1)
    square = (ROWS, LANES)
    mass, ent, rho, act = (
        a.reshape(square) for a in (particle_mass, entropy, density_old, active)
    )
    lists = neighbours.T
    vm = pl.BlockSpec(memory_space=pltpu.VMEM)
    sm = pl.BlockSpec(memory_space=pltpu.SMEM)
    hbm = pl.BlockSpec(memory_space=pl.ANY)
    f32, i32 = jnp.float32, jnp.int32
    far, near = pl.pallas_call(
        edge_kernel,
        out_shape=(jax.ShapeDtypeStruct((HALO_ROWS, LANES), f32),) * 2,
        in_specs=[sm] + [hbm] * 6,
        out_specs=(vm, vm),
        scratch_shapes=[
            pltpu.VMEM((2, 3, EDGE * CELL_PARTICLES), f32),
            pltpu.VMEM((2, 8, LANES), i32),
            pltpu.VMEM((NEIGHBOURS, CELLS_DEV), i32),
            pltpu.SemaphoreType.DMA((11,)),
        ],
        compiler_params=pltpu.CompilerParams(vmem_limit_bytes=64 * 2**20),
    )(own, position, mass, ent, rho, act, lists)
    near_pairs = [(2 * k, 2 * k + 1) for k in range(count // 2)]
    far_pairs = [(2 * k + 1, (2 * k + 2) % count) for k in range(count // 2)]
    far = swapped(far, far_pairs)
    near = swapped(near, near_pairs)

    ext = pltpu.VMEM((EXT_ROWS, LANES), f32)
    flat = pltpu.VMEM((3, PART_DEV), f32)
    whole = pltpu.VMEM(square, i32)
    pair = jax.ShapeDtypeStruct((2, FIELDS, 8, LANES), f32)
    kept, *sends = pl.pallas_call(
        state_kernel,
        out_shape=(
            jax.ShapeDtypeStruct((FIELDS, ROWS, LANES), f32),
            pair,
            pair,
            pair,
            pair,
            jax.ShapeDtypeStruct((FIELDS, 8, LANES), f32),
        ),
        in_specs=[sm] + [hbm] * 11,
        out_specs=(vm,) * 6,
        scratch_shapes=[flat, flat, whole, whole, whole]
        + [pltpu.VMEM((NEIGHBOURS, CELLS_DEV), i32)]
        + [ext] * 12
        + [
            pltpu.VMEM((FIELDS, ROWS, LANES), f32),
            whole,
            pltpu.VMEM((7, ROWS, LANES), i32),
            pltpu.VMEM((2 * FIELDS, ROWS, LANES), f32),
            pltpu.VMEM(square, f32),
            pltpu.VMEM(square, f32),
            pltpu.VMEM((64 * FIELDS, PACK_ROWS * LANES), jnp.bfloat16),
            pltpu.VMEM((256, PACK_ROWS * LANES), jnp.bfloat16),
            pltpu.VMEM((64 * FIELDS, 256), f32),
            pltpu.VMEM((GROUPS, FIELDS, 8, LANES), f32),
            pltpu.VMEM((HALO_ROWS, LANES), f32),
            pltpu.VMEM((HALO_ROWS, LANES), f32),
            pltpu.VMEM((32, LANES), i32),
            pltpu.SMEM((32, LANES), i32),
            pltpu.SMEM((LIST_SIZE,), i32),
            pltpu.SemaphoreType.DMA((12,)),
        ],
        compiler_params=pltpu.CompilerParams(vmem_limit_bytes=64 * 2**20),
    )(
        own,
        position,
        velocity,
        mass,
        ent,
        rho,
        act,
        destination.reshape(square),
        recv_slot.reshape(square),
        lists,
        far,
        near,
    )
    to_far, to_far2, to_next, to_next2, to_other = sends
    chips = count // 2

    def chip_pairs(distance, first):
        firsts = [c for c in range(chips) if (c // distance) % 2 == first]
        return [
            (2 * c + core, 2 * ((c + distance) % chips) + core)
            for c in firsts
            for core in range(2)
        ]

    other = swapped(to_other, near_pairs)
    next2 = swapped(to_next2, chip_pairs(1, 1))
    far2 = swapped(to_far2, chip_pairs(2, 1))
    next1 = swapped(to_next, chip_pairs(1, 0))
    far1 = swapped(to_far, chip_pairs(2, 0))
    held = pl.pallas_call(
        stay_kernel,
        out_shape=jax.ShapeDtypeStruct((FIELDS, RECV_DEV), f32),
        in_specs=[hbm],
        out_specs=hbm,
        scratch_shapes=[
            pltpu.VMEM((FIELDS, ROWS, LANES), f32),
            pltpu.VMEM((FIELDS, PART_DEV), f32),
            pltpu.SemaphoreType.DMA((2,)),
        ],
        compiler_params=pltpu.CompilerParams(vmem_limit_bytes=64 * 2**20),
        cost_estimate=pl.CostEstimate(
            flops=4 * 2**20, bytes_accessed=4 * 2**20, transcendentals=0
        ),
    )(kept)
    next1, held = lax.optimization_barrier((next1, held))
    crossed = [swapped(x, near_pairs) for x in (next1, next2, far1, far2)]
    return pl.pallas_call(
        assemble_kernel,
        out_shape=jax.ShapeDtypeStruct((FIELDS, RECV_DEV), f32),
        in_specs=[sm] + [vm] * 9 + [hbm],
        out_specs=hbm,
        scratch_shapes=[
            pltpu.VMEM((FIELDS, GROUPS * MOST), f32),
            pltpu.SemaphoreType.DMA((1,)),
        ],
        input_output_aliases={10: 0},
        compiler_params=pltpu.CompilerParams(vmem_limit_bytes=16 * 2**20),
    )(own, next1, next2, far1, far2, other, *crossed, held)


def solution(mesh):
    placed = (
        P(None, "cells"),
        P(None, "cells"),
        P("cells"),
        P("cells"),
        P("cells"),
        P("cells"),
        P("cells", None),
        P("cells"),
        P("cells"),
    )
    return jax.shard_map(
        per_device, mesh=mesh, in_specs=placed, out_specs=P(None, "cells"), check_vma=False
    )
```

```python
import functools

import jax
import jax.numpy as jnp
from jax import lax
from jax.experimental import pallas as pl
from jax.experimental.pallas import tpu as pltpu
from jax.sharding import PartitionSpec as P

CELL_PARTICLES = 256
HALO = 4
REACH = 4
PART_DEV = 16384
MOST = 1024
RECV_DEV = 24576
CELLS_DEV = 64
NEIGHBOURS = 6
LANES = 128
ROWS = PART_DEV // LANES
EDGE = 2 * HALO
EXT = CELLS_DEV + 2 * EDGE
EXT_ROWS = 2 * EXT
EDGE_ROWS = 2 * EDGE
HALO_ROWS = 96
GHOST = HALO
LISTED = CELLS_DEV + 2 * GHOST
OWN = slice(EDGE_ROWS, EDGE_ROWS + ROWS)
PACK_ROWS = 16
KEPT_STEPS = 8
TERMS = 2 * NEIGHBOURS
DUMMY = EDGE * 64 + 32 + (8 << 20)
UNROLL = 16
LIST_SIZE = LISTED * 32 + 64
GROUPS = 2 * REACH
time_step = 0.25
FIELDS = 9


def bcast(ref, row):
    return ref[pl.ds(row, 8, stride=0), :]


def edge_kernel(
    own_ref, pos_ref, mass_ref, ent_ref, rho_ref, act_ref, nbr_ref, far_ref, near_ref,
    pos_v, act_v, nbr_v, sem
):
    even = own_ref[0] % 2 == 0
    copies = []
    nbr_copy = pltpu.make_async_copy(nbr_ref, nbr_v, sem.at[0])
    nbr_copy.start()
    for side, ref in enumerate((far_ref, near_ref)):
        low = even if side == 0 else jnp.logical_not(even)
        wide = pl.multiple_of(jnp.where(low, 0, ROWS - EDGE_ROWS), 8)
        near = pl.multiple_of(jnp.where(low, 0, ROWS - 8), 8)
        lane = pl.multiple_of(jnp.where(low, 0, PART_DEV - EDGE * CELL_PARTICLES), LANES)
        base = 1 + 5 * side
        pairs = [
            (pos_ref.at[:, pl.ds(lane, EDGE * CELL_PARTICLES)], pos_v.at[side]),
            (mass_ref.at[pl.ds(wide, EDGE_ROWS)], ref.at[pl.ds(48, EDGE_ROWS)]),
            (ent_ref.at[pl.ds(near, 8)], ref.at[pl.ds(64, 8)]),
            (rho_ref.at[pl.ds(near, 8)], ref.at[pl.ds(72, 8)]),
            (act_ref.at[pl.ds(near, 8)], act_v.at[side]),
        ]
        for k, (a, b) in enumerate(pairs):
            copy = pltpu.make_async_copy(a, b, sem.at[base + k])
            copy.start()
            copies.append(copy)
    nbr_copy.wait()
    for copy in copies:
        copy.wait()
    lists = nbr_v[...].astype(jnp.float32)
    for side, ref in enumerate((far_ref, near_ref)):
        for c in range(3):
            for i in range(EDGE_ROWS):
                ref[16 * c + i : 16 * c + i + 1, :] = (
                    pos_v[side, c : c + 1, i * LANES : (i + 1) * LANES] * 0.5
                )
        ref[80:88, :] = (act_v[side] == 1).astype(jnp.float32)
        ref[88:96, :] = jnp.zeros((8, LANES), jnp.float32)
        ref[88 : 88 + NEIGHBOURS, 0:CELLS_DEV] = lists


def order_kernel(own_ref, dest_in, slot_in, hi_out, lo_out, bits_out, dest_ref, slot_ref, sem):
    own = own_ref[0]
    loads = [
        pltpu.make_async_copy(dest_in, dest_ref, sem.at[0]),
        pltpu.make_async_copy(slot_in, slot_ref, sem.at[1]),
    ]
    for copy in loads:
        copy.start()
    for copy in loads:
        copy.wait()
    before = (
        lax.broadcasted_iota(jnp.int32, (LANES, LANES), 0)
        < lax.broadcasted_iota(jnp.int32, (LANES, LANES), 1)
    ).astype(jnp.bfloat16)
    ones = jnp.ones((LANES, LANES), jnp.bfloat16)
    dest = dest_ref[...]
    away = (dest - own) & 127
    signed = jnp.where(away > 64, away - 128, away)
    group = jnp.where(signed < 0, signed + REACH, signed + REACH - 1)
    place = (slot_ref[...] - PART_DEV) & (MOST - 1)
    moving = dest != own
    hi = (group >> 1) * 8 + (place >> 7)
    lo = (group & 1) * LANES + (place & (LANES - 1))
    key = jnp.where(moving, hi * 256 + lo, -1)
    bits = jnp.zeros((ROWS, LANES), jnp.int32)
    mover16 = moving.astype(jnp.float32).astype(jnp.bfloat16)
    above = lax.dot_general(
        before, mover16, (((0,), (0,)), ((), ())), preferred_element_type=jnp.float32
    ).astype(jnp.int32)
    in_column = jnp.dot(ones, mover16, preferred_element_type=jnp.float32).astype(jnp.int32)
    own_row = lax.broadcasted_iota(jnp.int32, (ROWS, LANES), 0)
    remaining = jnp.where(moving, own_row - above, 0)
    for bit in range(7):
        coming = pltpu.roll(remaining, ROWS - (1 << bit), 0)
        lands = (coming >> bit) & 1
        leaves = (remaining >> bit) & 1
        bits = bits | (lands << bit)
        key = jnp.where(lands == 1, pltpu.roll(key, ROWS - (1 << bit), 0), key)
        remaining = jnp.where(lands == 1, coming, jnp.where(leaves == 1, 0, remaining))
    key = jnp.where(own_row < in_column, key, -1)
    hi_out[...] = (key >> 8).astype(jnp.float32)
    lo_out[...] = (key & 255).astype(jnp.float32)
    bits_out[...] = bits


def state_kernel(
    own_ref, pos_ref, vel_ref, mass_ref, ent_ref, rho_ref, act_ref, dest_ref,
    nbr_ref, far_in, near_in, hi_in, lo_in, bits_in,
    kept_ref, to_far, to_far2, to_next, to_next2, to_other,
    pos_v, vel_v, act_v, dest_v, nbr_v,
    xs, ys, zs, ms, ps, es, rho_old, rank, dens, ax, ay, az,
    fields, bits, parts, hi_row, lo_row, a0, b0, packed, blocks,
    far_ref, near_ref, sq, mp, factors, table_v, table, chunk_list, sem,
):
    own = own_ref[0]
    even = own % 2 == 0
    scale = 8.0 / (NEIGHBOURS * CELL_PARTICLES)
    loads = [
        (act_ref, act_v),
        (nbr_ref, nbr_v),
        (far_in, far_ref),
        (near_in, near_ref),
        (dest_ref, dest_v),
        (hi_in, hi_row),
        (lo_in, lo_row),
        (bits_in, bits),
        (rho_ref, rho_old.at[pl.ds(EDGE_ROWS, ROWS)]),
        (mass_ref, ms.at[pl.ds(EDGE_ROWS, ROWS)]),
        (ent_ref, es.at[pl.ds(EDGE_ROWS, ROWS)]),
        (pos_ref, pos_v),
        (vel_ref, vel_v),
    ]
    loads = [pltpu.make_async_copy(a, b, sem.at[k]) for k, (a, b) in enumerate(loads)]
    for copy in loads:
        copy.start()
    for ref in (dens, ax, ay, az, packed):
        ref[...] = jnp.zeros_like(ref)
    for copy in loads[:4]:
        copy.wait()

    def side_rows(first, last):
        f, n = far_ref[first:last, :], near_ref[first:last, :]
        return jnp.where(even, f, n), jnp.where(even, n, f)

    zeros8 = jnp.zeros((8, LANES), jnp.float32)
    ghost_act = side_rows(80, 88)

    act = jnp.concatenate(
        [zeros8, ghost_act[0], (act_v[...] == 1).astype(jnp.float32), ghost_act[1], zeros8],
        axis=0,
    )
    before = (
        lax.broadcasted_iota(jnp.int32, (LANES, LANES), 0)
        < lax.broadcasted_iota(jnp.int32, (LANES, LANES), 1)
    ).astype(jnp.bfloat16)
    ones = jnp.ones((LANES, LANES), jnp.bfloat16)
    act16 = act.astype(jnp.bfloat16)
    in_lanes = lax.dot_general(
        ones[0:16], act16, (((1,), (1,)), ((), ())), preferred_element_type=jnp.float32
    )
    halves = lax.broadcasted_iota(jnp.int32, (EXT_ROWS, LANES), 0) >> 1
    joined = (halves == lax.broadcasted_iota(jnp.int32, (EXT_ROWS, LANES), 1)).astype(jnp.bfloat16)
    in_cells = jnp.dot(in_lanes.astype(jnp.bfloat16), joined, preferred_element_type=jnp.float32)
    table_v[0:8, :] = in_cells[0:8].astype(jnp.int32)
    shift = own * CELLS_DEV - EDGE
    near_lists = side_rows(88, 96)
    pad = jnp.zeros((8 - NEIGHBOURS, CELLS_DEV), jnp.int32)
    table_v[8:16, 0:CELLS_DEV] = (jnp.concatenate([nbr_v[...], pad]) - shift) & 8191
    for k in range(2):
        table_v[16 + 8 * k : 24 + 8 * k, 0:LANES] = (
            near_lists[k].astype(jnp.int32) - shift
        ) & 8191
    table_copy = pltpu.make_async_copy(table_v, table, sem.at[15])
    table_copy.start()
    high = slice(EDGE_ROWS + ROWS, EXT_ROWS)
    for k, ref in enumerate((xs, ys, zs, ms)):
        ref[0:EDGE_ROWS, :], ref[high, :] = side_rows(16 * k, 16 * k + 16)
    for ref, rows, fill in ((es, (64, 72), 0.0), (rho_old, (72, 80), 1.0)):
        ref[0:8, :] = zeros8 + fill
        ref[EXT_ROWS - 8 :, :] = zeros8 + fill
        ref[8:16, :], ref[EXT_ROWS - 16 : EXT_ROWS - 8, :] = side_rows(*rows)
    inside = jnp.dot(act16, before, preferred_element_type=jnp.float32)
    total = jnp.dot(act16, ones, preferred_element_type=jnp.float32)
    row_id = lax.broadcasted_iota(jnp.int32, (EXT_ROWS, LANES), 0)
    rank[...] = jnp.where(
        act > 0.5, inside + jnp.where(row_id % 2 == 1, pltpu.roll(total, 1, 0), 0.0), -1.0
    )

    for copy in loads[4:]:
        copy.wait()

    def split_rows(i, carry):
        col = pl.multiple_of(i * LANES, LANES)
        p = pos_v[:, pl.ds(col, LANES)]
        v = vel_v[:, pl.ds(col, LANES)]
        for c, ref in enumerate((xs, ys, zs)):
            fields[c, pl.ds(i, 1), :] = p[c : c + 1, :]
            fields[3 + c, pl.ds(i, 1), :] = v[c : c + 1, :]
        return carry

    lax.fori_loop(0, ROWS, split_rows, 0, unroll=8)
    for c, ref in enumerate((xs, ys, zs)):
        ref[OWN, :] = fields[c] * 0.5
    fields[6] = rho_old[OWN, :]
    fields[7] = es[OWN, :]
    fields[8] = ms[OWN, :]
    table_copy.wait()

    cells = [(EDGE + k, k, 8) for k in range(CELLS_DEV)]
    cells += [(EDGE - GHOST + k, CELLS_DEV - GHOST + k, 16) for k in range(GHOST)]
    cells += [(EDGE + CELLS_DEV + k, k, 24) for k in range(GHOST)]
    at, most, own_total = 0, 0, 0
    for number, (cell, lane, row) in enumerate(cells):
        n = table[0, cell]
        code = (row << 20) + (lane << 13) + (cell << 6)
        for k in range(4):
            chunk_list[at + k] = code + k
        at = at + ((n + 7) >> 3)
        most = jnp.maximum(most, n)
        if number == CELLS_DEV - 1:
            own_total = at
    all_total = at

    @pl.when(most > 32)
    def _():
        def refill(first, count, lane0, row):
            def one(k, start):
                cell = first + k
                n = table[0, cell]
                code = (row << 20) + ((lane0 + k) << 13) + (cell << 6)

                def put(j, carry):
                    chunk_list[start + j] = code + j
                    return carry

                lax.fori_loop(0, (n + 7) >> 3, put, 0)
                return start + ((n + 7) >> 3)

            return lambda start: lax.fori_loop(0, count, one, start)

        start = refill(EDGE, CELLS_DEV, 0, 8)(0)
        start = refill(EDGE - GHOST, GHOST, CELLS_DEV - GHOST, 16)(start)
        refill(EDGE + CELLS_DEV, GHOST, 0, 24)(start)

    sub = lax.broadcasted_iota(jnp.int32, (8, LANES), 0).astype(jnp.float32)

    def chunk_of(position, limit):
        code = chunk_list[jnp.maximum(jnp.minimum(position, limit - 1), 0)]
        code = jnp.where(position < limit, code, DUMMY)
        cell = (code >> 6) & 127
        want = sub + ((code & 63) * 8).astype(jnp.float32)
        picks = [bcast(rank, 2 * cell + h) == want for h in range(2)]
        lane = (code >> 13) & 127
        sources = [table[(code >> 20) + q, lane] for q in range(NEIGHBOURS)]
        return cell, picks, sources

    def column(ref, cell, picks):
        both = jnp.where(picks[0], bcast(ref, 2 * cell), 0.0) + jnp.where(
            picks[1], bcast(ref, 2 * cell + 1), 0.0
        )
        return jnp.sum(both, axis=1, keepdims=True)

    def spread(ref, cell, picks, value):
        for h in range(2):
            row = jnp.sum(jnp.where(picks[h], value, 0.0), axis=0, keepdims=True)
            ref[pl.ds(2 * cell + h, 1), :] += row

    sq[...] = -(xs[...] * xs[...] + ys[...] * ys[...] + zs[...] * zs[...])

    def target(cell, picks):
        cx, cy, cz = (column(ref, cell, picks) for ref in (xs, ys, zs))
        inner = 1.0 - (cx * cx + cy * cy + cz * cz)
        return cx, cy, cz, [jnp.broadcast_to(x, (8, LANES)) for x in (inner, 2.0 * cx, 2.0 * cy, 2.0 * cz)]

    def factor(wide, row):
        inner, tx, ty, tz = wide
        near = (inner + bcast(sq, row)) + tx * bcast(xs, row)
        near = (near + ty * bcast(ys, row)) + tz * bcast(zs, row)
        return jnp.maximum(near, 0.0)

    def density_step(step, keep):
        done = []
        for u in range(UNROLL):
            position = step * UNROLL + u
            cell, picks, sources = chunk_of(position, all_total)
            wide = target(cell, picks)[3]
            total_rows = jnp.zeros((8, LANES), jnp.float32)
            for q, source in enumerate(sources):
                for h in range(2):
                    row = 2 * source + h
                    u1 = factor(wide, row)
                    if keep:
                        factors[position * TERMS + 2 * q + h] = u1
                    total_rows += u1 * u1 * u1 * bcast(ms, row)
            value = jnp.sum(total_rows, axis=1, keepdims=True) * scale
            done.append((cell, picks, value))
        for cell, picks, value in done:
            spread(dens, cell, picks, value)

    def loop(limit, body):
        steps = (limit + UNROLL - 1) // UNROLL

        def run(keep):
            def one(step, carry):
                body(step, keep)
                return carry

            return one

        lax.fori_loop(0, jnp.minimum(steps, KEPT_STEPS), run(True), 0)
        lax.fori_loop(KEPT_STEPS, steps, run(False), 0)

    loop(all_total, density_step)

    rho = jnp.where(rank[...] >= 0.0, dens[...], rho_old[...])
    dens[...] = rho
    ps[...] = es[...] * jnp.exp(jnp.log(rho) * (-1.0 / 3.0))

    mp[...] = ms[...] * ps[...]

    def force_step(step, keep):
        done = []
        for u in range(UNROLL):
            position = step * UNROLL + u
            cell, picks, sources = chunk_of(position, own_total)
            cx, cy, cz, wide = target(cell, picks)
            cp = jnp.broadcast_to(column(ps, cell, picks), (8, LANES))
            s0 = jnp.zeros((8, LANES), jnp.float32)
            sums = [s0, s0, s0]
            for q, source in enumerate(sources):
                for h in range(2):
                    row = 2 * source + h
                    if keep:
                        u1 = factors[position * TERMS + 2 * q + h]
                    else:
                        u1 = factor(wide, row)
                    w = (u1 * u1) * (cp * bcast(ms, row) + bcast(mp, row))
                    s0 += w
                    sums = [t + w * bcast(ref, row) for t, ref in zip(sums, (xs, ys, zs))]
            values = [
                jnp.sum(c * s0 - t, axis=1, keepdims=True) * (3.0 * scale * time_step)
                for c, t in zip((cx, cy, cz), sums)
            ]
            done.append((cell, picks, values))
        for cell, picks, values in done:
            for ref, value in zip((ax, ay, az), values):
                spread(ref, cell, picks, value)

    loop(own_total, force_step)

    own_row = lax.broadcasted_iota(jnp.int32, (ROWS, LANES), 0)
    mover_rows = jnp.max(jnp.where(hi_row[...] >= 0.0, own_row + 1, 0))

    def moved_up(x):
        for bit in range(7):
            lands = (bits[...] >> bit) & 1
            x = jnp.where(lands == 1, pltpu.roll(x, ROWS - (1 << bit), 0), x)
        return x

    for c, acc in enumerate((ax, ay, az)):
        kicked = fields[3 + c] + acc[OWN, :]
        fields[3 + c] = kicked
        fields[c] = fields[c] + time_step * kicked
    fields[6] = dens[OWN, :]
    stays = dest_v[...] == own
    for v in range(FIELDS):
        whole = fields[v]
        kept_ref[v] = jnp.where(stays, whole, 0.0)
        whole = moved_up(whole)
        first = whole.astype(jnp.bfloat16).astype(jnp.float32)
        parts[v] = first
        parts[FIELDS + v] = whole - first

    bf = jnp.bfloat16
    iota16 = lax.broadcasted_iota(jnp.int32, (16, LANES), 0).astype(jnp.float32).astype(bf)
    one16, zero16 = jnp.ones((16, LANES), bf), jnp.zeros((16, LANES), bf)

    def twice(x):
        return jnp.concatenate([x, x], axis=0).astype(bf)

    def pack_step(step, carry):
        for j in range(PACK_ROWS):
            row = step * PACK_ROWS + j
            cols = slice(j * LANES, (j + 1) * LANES)
            hi_b, lo_b = twice(bcast(hi_row, row)), twice(bcast(lo_row, row))
            for k in range(16):
                b0[16 * k : 16 * k + 16, cols] = jnp.where(
                    lo_b == iota16 + bf(16 * k), one16, zero16
                )
            upper = hi_b == iota16
            lower = hi_b == iota16 + bf(16)
            for v in range(2 * FIELDS):
                value = twice(parts[v, pl.ds(row, 8, stride=0), :])
                a0[32 * v : 32 * v + 16, cols] = jnp.where(upper, value, zero16)
                a0[32 * v + 16 : 32 * v + 32, cols] = jnp.where(lower, value, zero16)
        packed[...] += lax.dot_general(
            a0[...], b0[...], (((1,), (1,)), ((), ())), preferred_element_type=jnp.float32
        )
        return carry

    lax.fori_loop(0, (mover_rows + PACK_ROWS - 1) // PACK_ROWS, pack_step, 0)

    for g in range(GROUPS):
        cols = slice((g & 1) * LANES, (g & 1) * LANES + LANES)
        for v in range(FIELDS):
            r = 32 * v + (g >> 1) * 8
            s = r + 32 * FIELDS
            blocks[g, v] = packed[r : r + 8, cols] + packed[s : s + 8, cols]
    turn = 1 - 2 * (own & 1)
    for ref, step in zip((to_next, to_next2, to_far, to_far2), chip_steps(own)):
        ref[0] = blocks[group_of(2 * step)]
        ref[1] = blocks[group_of(2 * step + turn)]
    to_other[...] = blocks[group_of(turn)]


def chip_steps(own):
    even = jnp.where((own >> 1) & 1 == 0, 1, -1)
    low = jnp.where((own >> 2) & 1 == 0, 2, -2)
    return even, -even, low, -low


def group_of(offset):
    g = jnp.where(offset < 0, offset + REACH, offset + REACH - 1)
    return jnp.minimum(jnp.maximum(g, 0), GROUPS - 1)


def stay_kernel(kept_ref, out_ref, kept_v, rows, sem):
    load = pltpu.make_async_copy(kept_ref, kept_v, sem.at[1])
    load.start()
    load.wait()

    def step(i, carry):
        col = pl.multiple_of(i * LANES, LANES)
        for v in range(FIELDS):
            rows[v : v + 1, pl.ds(col, LANES)] = kept_v[v, pl.ds(i, 1), :]
        return carry

    lax.fori_loop(0, ROWS, step, 0, unroll=8)
    copy = pltpu.make_async_copy(rows, out_ref.at[:, pl.ds(0, PART_DEV)], sem.at[0])
    copy.start()
    copy.wait()


def assemble_kernel(
    own_ref, next2_ref, far2_ref, next_ref, far_ref, other_ref,
    x_next2, x_far2, x_next, x_far, held_ref, out_ref, rows, sem
):
    del held_ref
    own = own_ref[0]
    turn = 1 - 2 * (own & 1)
    steps = chip_steps(own)
    low = (own >> 2) & 1 == 0
    pick_low = low == (turn < 0)
    parts = [(ref, (0,), -2 * step) for ref, step in zip((next_ref, next2_ref, far_ref, far2_ref), steps)]
    parts += [(ref, (1,), -2 * step - turn) for ref, step in zip((x_next, x_next2), steps)]
    parts += [(other_ref, (), -turn)]
    parts += [(None, (), 3 * turn)]

    for ref, index, offset in parts:
        start = group_of(offset) * MOST
        for v in range(FIELDS):
            if ref is None:
                tile = jnp.where(pick_low, x_far[1, v], x_far2[1, v])
            else:
                tile = ref[index + (v,)]
            for r in range(8):
                col = pl.multiple_of(start + r * LANES, LANES)
                rows[v : v + 1, pl.ds(col, LANES)] = tile[r : r + 1, :]
    copy = pltpu.make_async_copy(
        rows, out_ref.at[:, pl.ds(PART_DEV, GROUPS * MOST)], sem.at[0]
    )
    copy.start()
    copy.wait()


def swapped(block, pairs):
    route = [(a, b) for a, b in pairs] + [(b, a) for a, b in pairs]
    return lax.ppermute(block, "cells", route)


def per_device(
    position,
    velocity,
    particle_mass,
    entropy,
    density_old,
    active,
    neighbours,
    destination,
    recv_slot,
):
    count = lax.axis_size("cells")
    own = lax.axis_index("cells").reshape(1)
    square = (ROWS, LANES)
    mass, ent, rho, act = (
        a.reshape(square) for a in (particle_mass, entropy, density_old, active)
    )
    lists = neighbours.T
    vm = pl.BlockSpec(memory_space=pltpu.VMEM)
    sm = pl.BlockSpec(memory_space=pltpu.SMEM)
    hbm = pl.BlockSpec(memory_space=pl.ANY)
    f32, i32 = jnp.float32, jnp.int32
    far, near = pl.pallas_call(
        edge_kernel,
        out_shape=(jax.ShapeDtypeStruct((HALO_ROWS, LANES), f32),) * 2,
        in_specs=[sm] + [hbm] * 6,
        out_specs=(vm, vm),
        scratch_shapes=[
            pltpu.VMEM((2, 3, EDGE * CELL_PARTICLES), f32),
            pltpu.VMEM((2, 8, LANES), i32),
            pltpu.VMEM((NEIGHBOURS, CELLS_DEV), i32),
            pltpu.SemaphoreType.DMA((11,)),
        ],
        compiler_params=pltpu.CompilerParams(vmem_limit_bytes=64 * 2**20),
    )(own, position, mass, ent, rho, act, lists)
    near_pairs = [(2 * k, 2 * k + 1) for k in range(count // 2)]
    far_pairs = [(2 * k + 1, (2 * k + 2) % count) for k in range(count // 2)]
    far = swapped(far, far_pairs)
    near = swapped(near, near_pairs)

    dest, slot = destination.reshape(square), recv_slot.reshape(square)
    order = pl.pallas_call(
        order_kernel,
        out_shape=(
            jax.ShapeDtypeStruct(square, f32),
            jax.ShapeDtypeStruct(square, f32),
            jax.ShapeDtypeStruct(square, i32),
        ),
        in_specs=[sm] + [hbm] * 2,
        out_specs=(vm,) * 3,
        scratch_shapes=[
            pltpu.VMEM(square, i32),
            pltpu.VMEM(square, i32),
            pltpu.SemaphoreType.DMA((2,)),
        ],
        compiler_params=pltpu.CompilerParams(vmem_limit_bytes=64 * 2**20),
        cost_estimate=pl.CostEstimate(
            flops=2**24, bytes_accessed=2**23, transcendentals=0
        ),
    )(own, dest, slot)
    ext = pltpu.VMEM((EXT_ROWS, LANES), f32)
    flat = pltpu.VMEM((3, PART_DEV), f32)
    whole = pltpu.VMEM(square, i32)
    pair = jax.ShapeDtypeStruct((2, FIELDS, 8, LANES), f32)
    kept, *sends = pl.pallas_call(
        state_kernel,
        out_shape=(
            jax.ShapeDtypeStruct((FIELDS, ROWS, LANES), f32),
            pair,
            pair,
            pair,
            pair,
            jax.ShapeDtypeStruct((FIELDS, 8, LANES), f32),
        ),
        in_specs=[sm] + [hbm] * 13,
        out_specs=(vm,) * 6,
        scratch_shapes=[flat, flat, whole, whole]
        + [pltpu.VMEM((NEIGHBOURS, CELLS_DEV), i32)]
        + [ext] * 12
        + [
            pltpu.VMEM((FIELDS, ROWS, LANES), f32),
            whole,
            pltpu.VMEM((2 * FIELDS, ROWS, LANES), f32),
            pltpu.VMEM(square, f32),
            pltpu.VMEM(square, f32),
            pltpu.VMEM((64 * FIELDS, PACK_ROWS * LANES), jnp.bfloat16),
            pltpu.VMEM((256, PACK_ROWS * LANES), jnp.bfloat16),
            pltpu.VMEM((64 * FIELDS, 256), f32),
            pltpu.VMEM((GROUPS, FIELDS, 8, LANES), f32),
            pltpu.VMEM((HALO_ROWS, LANES), f32),
            pltpu.VMEM((HALO_ROWS, LANES), f32),
            ext,
            ext,
            pltpu.VMEM((KEPT_STEPS * UNROLL * TERMS, 8, LANES), f32),
            pltpu.VMEM((32, LANES), i32),
            pltpu.SMEM((32, LANES), i32),
            pltpu.SMEM((LIST_SIZE,), i32),
            pltpu.SemaphoreType.DMA((16,)),
        ],
        compiler_params=pltpu.CompilerParams(vmem_limit_bytes=64 * 2**20),
    )(
        own,
        position,
        velocity,
        mass,
        ent,
        rho,
        act,
        dest,
        lists,
        far,
        near,
        *order,
    )
    to_far, to_far2, to_next, to_next2, to_other = sends
    chips = count // 2

    def chip_pairs(distance, first):
        firsts = [c for c in range(chips) if (c // distance) % 2 == first]
        return [
            (2 * c + core, 2 * ((c + distance) % chips) + core)
            for c in firsts
            for core in range(2)
        ]

    other = swapped(to_other, near_pairs)
    next2 = swapped(to_next2, chip_pairs(1, 1))
    far2 = swapped(to_far2, chip_pairs(2, 1))
    next1 = swapped(to_next, chip_pairs(1, 0))
    far1 = swapped(to_far, chip_pairs(2, 0))
    held = pl.pallas_call(
        stay_kernel,
        out_shape=jax.ShapeDtypeStruct((FIELDS, RECV_DEV), f32),
        in_specs=[hbm],
        out_specs=hbm,
        scratch_shapes=[
            pltpu.VMEM((FIELDS, ROWS, LANES), f32),
            pltpu.VMEM((FIELDS, PART_DEV), f32),
            pltpu.SemaphoreType.DMA((2,)),
        ],
        compiler_params=pltpu.CompilerParams(vmem_limit_bytes=64 * 2**20 - 450 * 2**10),
        cost_estimate=pl.CostEstimate(
            flops=4 * 2**20, bytes_accessed=4 * 2**20, transcendentals=0
        ),
    )(kept)
    far1, held = lax.optimization_barrier((far1, held))
    crossed = [swapped(x, near_pairs) for x in (next2, far2, next1, far1)]
    return pl.pallas_call(
        assemble_kernel,
        out_shape=jax.ShapeDtypeStruct((FIELDS, RECV_DEV), f32),
        in_specs=[sm] + [vm] * 9 + [hbm],
        out_specs=hbm,
        scratch_shapes=[
            pltpu.VMEM((FIELDS, GROUPS * MOST), f32),
            pltpu.SemaphoreType.DMA((1,)),
        ],
        input_output_aliases={10: 0},
        compiler_params=pltpu.CompilerParams(vmem_limit_bytes=16 * 2**20),
    )(own, next2, far2, next1, far1, other, *crossed, held)


def solution(mesh):
    placed = (
        P(None, "cells"),
        P(None, "cells"),
        P("cells"),
        P("cells"),
        P("cells"),
        P("cells"),
        P("cells", None),
        P("cells"),
        P("cells"),
    )
    return jax.shard_map(
        per_device, mesh=mesh, in_specs=placed, out_specs=P(None, "cells"), check_vma=False
    )
```

```python
import functools

import jax
import jax.numpy as jnp
from jax import lax
from jax.experimental import pallas as pl
from jax.experimental.pallas import tpu as pltpu
from jax.sharding import PartitionSpec as P

CELL_PARTICLES = 256
HALO = 4
REACH = 4
PART_DEV = 16384
MOST = 1024
RECV_DEV = 24576
CELLS_DEV = 64
NEIGHBOURS = 6
LANES = 128
ROWS = PART_DEV // LANES
EDGE = 2 * HALO
EXT = CELLS_DEV + 2 * EDGE
EXT_ROWS = 2 * EXT
EDGE_ROWS = 2 * EDGE
HALO_ROWS = 96
GHOST = HALO
LISTED = CELLS_DEV + 2 * GHOST
OWN = slice(EDGE_ROWS, EDGE_ROWS + ROWS)
PACK_ROWS = 16
KEPT_STEPS = 8
TERMS = 2 * NEIGHBOURS
DUMMY = EDGE * 64 + 32 + (8 << 20)
UNROLL = 16
LIST_SIZE = LISTED * 32 + 64
GROUPS = 2 * REACH
time_step = 0.25
FIELDS = 9


def bcast(ref, row):
    return ref[pl.ds(row, 8, stride=0), :]


def edge_kernel(
    own_ref, pos_ref, mass_ref, ent_ref, rho_ref, act_ref, nbr_ref, far_ref, near_ref,
    pos_v, act_v, nbr_v, sem
):
    even = own_ref[0] % 2 == 0
    copies = []
    nbr_copy = pltpu.make_async_copy(nbr_ref, nbr_v, sem.at[0])
    nbr_copy.start()
    for side, ref in enumerate((far_ref, near_ref)):
        low = even if side == 0 else jnp.logical_not(even)
        wide = pl.multiple_of(jnp.where(low, 0, ROWS - EDGE_ROWS), 8)
        near = pl.multiple_of(jnp.where(low, 0, ROWS - 8), 8)
        lane = pl.multiple_of(jnp.where(low, 0, PART_DEV - EDGE * CELL_PARTICLES), LANES)
        base = 1 + 5 * side
        pairs = [
            (pos_ref.at[:, pl.ds(lane, EDGE * CELL_PARTICLES)], pos_v.at[side]),
            (mass_ref.at[pl.ds(wide, EDGE_ROWS)], ref.at[pl.ds(48, EDGE_ROWS)]),
            (ent_ref.at[pl.ds(near, 8)], ref.at[pl.ds(64, 8)]),
            (rho_ref.at[pl.ds(near, 8)], ref.at[pl.ds(72, 8)]),
            (act_ref.at[pl.ds(near, 8)], act_v.at[side]),
        ]
        for k, (a, b) in enumerate(pairs):
            copy = pltpu.make_async_copy(a, b, sem.at[base + k])
            copy.start()
            copies.append(copy)
    nbr_copy.wait()
    for copy in copies:
        copy.wait()
    lists = nbr_v[...].astype(jnp.float32)
    for side, ref in enumerate((far_ref, near_ref)):
        for c in range(3):
            for i in range(EDGE_ROWS):
                ref[16 * c + i : 16 * c + i + 1, :] = (
                    pos_v[side, c : c + 1, i * LANES : (i + 1) * LANES] * 0.5
                )
        ref[80:88, :] = (act_v[side] == 1).astype(jnp.float32)
        ref[88:96, :] = jnp.zeros((8, LANES), jnp.float32)
        ref[88 : 88 + NEIGHBOURS, 0:CELLS_DEV] = lists


def order_kernel(own_ref, dest_in, slot_in, hi_out, lo_out, bits_out, dest_ref, slot_ref, sem):
    own = own_ref[0]
    loads = [
        pltpu.make_async_copy(dest_in, dest_ref, sem.at[0]),
        pltpu.make_async_copy(slot_in, slot_ref, sem.at[1]),
    ]
    for copy in loads:
        copy.start()
    for copy in loads:
        copy.wait()
    before = (
        lax.broadcasted_iota(jnp.int32, (LANES, LANES), 0)
        < lax.broadcasted_iota(jnp.int32, (LANES, LANES), 1)
    ).astype(jnp.bfloat16)
    ones = jnp.ones((LANES, LANES), jnp.bfloat16)
    dest = dest_ref[...]
    away = (dest - own) & 127
    signed = jnp.where(away > 64, away - 128, away)
    group = jnp.where(signed < 0, signed + REACH, signed + REACH - 1)
    place = (slot_ref[...] - PART_DEV) & (MOST - 1)
    moving = dest != own
    hi = (group >> 1) * 8 + (place >> 7)
    lo = (group & 1) * LANES + (place & (LANES - 1))
    key = jnp.where(moving, hi * 256 + lo, -1)
    bits = jnp.zeros((ROWS, LANES), jnp.int32)
    mover16 = moving.astype(jnp.float32).astype(jnp.bfloat16)
    above = lax.dot_general(
        before, mover16, (((0,), (0,)), ((), ())), preferred_element_type=jnp.float32
    ).astype(jnp.int32)
    in_column = jnp.dot(ones, mover16, preferred_element_type=jnp.float32).astype(jnp.int32)
    own_row = lax.broadcasted_iota(jnp.int32, (ROWS, LANES), 0)
    remaining = jnp.where(moving, own_row - above, 0)
    for bit in range(7):
        coming = pltpu.roll(remaining, ROWS - (1 << bit), 0)
        lands = (coming >> bit) & 1
        leaves = (remaining >> bit) & 1
        bits = bits | (lands << bit)
        key = jnp.where(lands == 1, pltpu.roll(key, ROWS - (1 << bit), 0), key)
        remaining = jnp.where(lands == 1, coming, jnp.where(leaves == 1, 0, remaining))
    key = jnp.where(own_row < in_column, key, -1)
    hi_out[...] = (key >> 8).astype(jnp.float32)
    lo_out[...] = (key & 255).astype(jnp.float32)
    bits_out[...] = bits


def state_kernel(
    own_ref, pos_ref, vel_ref, mass_ref, ent_ref, rho_ref, act_ref, dest_ref,
    nbr_ref, far_in, near_in, hi_in, lo_in, bits_in,
    kept_ref, to_far, to_far2, to_next, to_next2, to_other,
    pos_v, vel_v, act_v, dest_v, nbr_v,
    xs, ys, zs, ms, ps, es, rho_old, rank, dens, ax, ay, az,
    fields, bits, parts, hi_row, lo_row, a0, b0, packed, blocks,
    far_ref, near_ref, sq, mp, factors, table_v, table, chunk_list, sem,
):
    own = own_ref[0]
    even = own % 2 == 0
    scale = 8.0 / (NEIGHBOURS * CELL_PARTICLES)
    loads = [
        (act_ref, act_v),
        (nbr_ref, nbr_v),
        (far_in, far_ref),
        (near_in, near_ref),
        (dest_ref, dest_v),
        (hi_in, hi_row),
        (lo_in, lo_row),
        (bits_in, bits),
        (rho_ref, rho_old.at[pl.ds(EDGE_ROWS, ROWS)]),
        (mass_ref, ms.at[pl.ds(EDGE_ROWS, ROWS)]),
        (ent_ref, es.at[pl.ds(EDGE_ROWS, ROWS)]),
        (pos_ref, pos_v),
        (vel_ref, vel_v),
    ]
    loads = [pltpu.make_async_copy(a, b, sem.at[k]) for k, (a, b) in enumerate(loads)]
    for copy in loads:
        copy.start()
    for ref in (dens, ax, ay, az, packed):
        ref[...] = jnp.zeros_like(ref)
    for copy in loads[:4]:
        copy.wait()

    def side_rows(first, last):
        f, n = far_ref[first:last, :], near_ref[first:last, :]
        return jnp.where(even, f, n), jnp.where(even, n, f)

    zeros8 = jnp.zeros((8, LANES), jnp.float32)
    ghost_act = side_rows(80, 88)

    act = jnp.concatenate(
        [zeros8, ghost_act[0], (act_v[...] == 1).astype(jnp.float32), ghost_act[1], zeros8],
        axis=0,
    )
    before = (
        lax.broadcasted_iota(jnp.int32, (LANES, LANES), 0)
        < lax.broadcasted_iota(jnp.int32, (LANES, LANES), 1)
    ).astype(jnp.bfloat16)
    ones = jnp.ones((LANES, LANES), jnp.bfloat16)
    act16 = act.astype(jnp.bfloat16)
    in_lanes = lax.dot_general(
        ones[0:16], act16, (((1,), (1,)), ((), ())), preferred_element_type=jnp.float32
    )
    halves = lax.broadcasted_iota(jnp.int32, (EXT_ROWS, LANES), 0) >> 1
    joined = (halves == lax.broadcasted_iota(jnp.int32, (EXT_ROWS, LANES), 1)).astype(jnp.bfloat16)
    in_cells = jnp.dot(in_lanes.astype(jnp.bfloat16), joined, preferred_element_type=jnp.float32)
    table_v[0:8, :] = in_cells[0:8].astype(jnp.int32)
    shift = own * CELLS_DEV - EDGE
    near_lists = side_rows(88, 96)
    pad = jnp.zeros((8 - NEIGHBOURS, CELLS_DEV), jnp.int32)
    table_v[8:16, 0:CELLS_DEV] = (jnp.concatenate([nbr_v[...], pad]) - shift) & 8191
    for k in range(2):
        table_v[16 + 8 * k : 24 + 8 * k, 0:LANES] = (
            near_lists[k].astype(jnp.int32) - shift
        ) & 8191
    table_copy = pltpu.make_async_copy(table_v, table, sem.at[15])
    table_copy.start()
    high = slice(EDGE_ROWS + ROWS, EXT_ROWS)
    for k, ref in enumerate((xs, ys, zs, ms)):
        ref[0:EDGE_ROWS, :], ref[high, :] = side_rows(16 * k, 16 * k + 16)
    for ref, rows, fill in ((es, (64, 72), 0.0), (rho_old, (72, 80), 1.0)):
        ref[0:8, :] = zeros8 + fill
        ref[EXT_ROWS - 8 :, :] = zeros8 + fill
        ref[8:16, :], ref[EXT_ROWS - 16 : EXT_ROWS - 8, :] = side_rows(*rows)
    inside = jnp.dot(act16, before, preferred_element_type=jnp.float32)
    total = jnp.dot(act16, ones, preferred_element_type=jnp.float32)
    row_id = lax.broadcasted_iota(jnp.int32, (EXT_ROWS, LANES), 0)
    rank[...] = jnp.where(
        act > 0.5, inside + jnp.where(row_id % 2 == 1, pltpu.roll(total, 1, 0), 0.0), -1.0
    )

    for copy in loads[4:]:
        copy.wait()

    def split_rows(i, carry):
        col = pl.multiple_of(i * LANES, LANES)
        p = pos_v[:, pl.ds(col, LANES)]
        v = vel_v[:, pl.ds(col, LANES)]
        for c, ref in enumerate((xs, ys, zs)):
            fields[c, pl.ds(i, 1), :] = p[c : c + 1, :]
            fields[3 + c, pl.ds(i, 1), :] = v[c : c + 1, :]
        return carry

    lax.fori_loop(0, ROWS, split_rows, 0, unroll=8)
    for c, ref in enumerate((xs, ys, zs)):
        ref[OWN, :] = fields[c] * 0.5
    fields[6] = rho_old[OWN, :]
    fields[7] = es[OWN, :]
    fields[8] = ms[OWN, :]
    table_copy.wait()

    cells = [(EDGE + k, k, 8) for k in range(CELLS_DEV)]
    cells += [(EDGE - GHOST + k, CELLS_DEV - GHOST + k, 16) for k in range(GHOST)]
    cells += [(EDGE + CELLS_DEV + k, k, 24) for k in range(GHOST)]
    at, most, own_total = 0, 0, 0
    for number, (cell, lane, row) in enumerate(cells):
        n = table[0, cell]
        code = (row << 20) + (lane << 13) + (cell << 6)
        for k in range(4):
            chunk_list[at + k] = code + k
        at = at + ((n + 7) >> 3)
        most = jnp.maximum(most, n)
        if number == CELLS_DEV - 1:
            own_total = at
    all_total = at

    @pl.when(most > 32)
    def _():
        def refill(first, count, lane0, row):
            def one(k, start):
                cell = first + k
                n = table[0, cell]
                code = (row << 20) + ((lane0 + k) << 13) + (cell << 6)

                def put(j, carry):
                    chunk_list[start + j] = code + j
                    return carry

                lax.fori_loop(0, (n + 7) >> 3, put, 0)
                return start + ((n + 7) >> 3)

            return lambda start: lax.fori_loop(0, count, one, start)

        start = refill(EDGE, CELLS_DEV, 0, 8)(0)
        start = refill(EDGE - GHOST, GHOST, CELLS_DEV - GHOST, 16)(start)
        refill(EDGE + CELLS_DEV, GHOST, 0, 24)(start)

    sub = lax.broadcasted_iota(jnp.int32, (8, LANES), 0).astype(jnp.float32)

    def chunk_of(position, limit):
        code = chunk_list[jnp.maximum(jnp.minimum(position, limit - 1), 0)]
        code = jnp.where(position < limit, code, DUMMY)
        cell = (code >> 6) & 127
        want = sub + ((code & 63) * 8).astype(jnp.float32)
        picks = [bcast(rank, 2 * cell + h) == want for h in range(2)]
        lane = (code >> 13) & 127
        sources = [table[(code >> 20) + q, lane] for q in range(NEIGHBOURS)]
        return cell, picks, sources

    def column(ref, cell, picks):
        both = jnp.where(picks[0], bcast(ref, 2 * cell), 0.0) + jnp.where(
            picks[1], bcast(ref, 2 * cell + 1), 0.0
        )
        return jnp.sum(both, axis=1, keepdims=True)

    def spread(ref, cell, picks, value):
        for h in range(2):
            row = jnp.sum(jnp.where(picks[h], value, 0.0), axis=0, keepdims=True)
            ref[pl.ds(2 * cell + h, 1), :] += row

    sq[...] = -(xs[...] * xs[...] + ys[...] * ys[...] + zs[...] * zs[...])

    def target(cell, picks):
        cx, cy, cz = (column(ref, cell, picks) for ref in (xs, ys, zs))
        inner = 1.0 - (cx * cx + cy * cy + cz * cz)
        return cx, cy, cz, [jnp.broadcast_to(x, (8, LANES)) for x in (inner, 2.0 * cx, 2.0 * cy, 2.0 * cz)]

    def factor(wide, row):
        inner, tx, ty, tz = wide
        near = (inner + bcast(sq, row)) + tx * bcast(xs, row)
        near = (near + ty * bcast(ys, row)) + tz * bcast(zs, row)
        return jnp.maximum(near, 0.0)

    def density_step(step, keep):
        done = []
        for u in range(UNROLL):
            position = step * UNROLL + u
            cell, picks, sources = chunk_of(position, all_total)
            wide = target(cell, picks)[3]
            total_rows = jnp.zeros((8, LANES), jnp.float32)
            for q, source in enumerate(sources):
                for h in range(2):
                    row = 2 * source + h
                    u1 = factor(wide, row)
                    if keep:
                        factors[position * TERMS + 2 * q + h] = u1
                    total_rows += u1 * u1 * u1 * bcast(ms, row)
            value = jnp.sum(total_rows, axis=1, keepdims=True) * scale
            done.append((cell, picks, value))
        for cell, picks, value in done:
            spread(dens, cell, picks, value)

    def loop(limit, body):
        steps = (limit + UNROLL - 1) // UNROLL

        def run(keep):
            def one(step, carry):
                body(step, keep)
                return carry

            return one

        lax.fori_loop(0, jnp.minimum(steps, KEPT_STEPS), run(True), 0)
        lax.fori_loop(KEPT_STEPS, steps, run(False), 0)

    loop(all_total, density_step)

    rho = jnp.where(rank[...] >= 0.0, dens[...], rho_old[...])
    dens[...] = rho
    ps[...] = es[...] * jnp.exp(jnp.log(rho) * (-1.0 / 3.0))

    mp[...] = ms[...] * ps[...]

    def force_step(step, keep):
        done = []
        for u in range(UNROLL):
            position = step * UNROLL + u
            cell, picks, sources = chunk_of(position, own_total)
            cx, cy, cz, wide = target(cell, picks)
            cp = jnp.broadcast_to(column(ps, cell, picks), (8, LANES))
            s0 = jnp.zeros((8, LANES), jnp.float32)
            sums = [s0, s0, s0]
            for q, source in enumerate(sources):
                for h in range(2):
                    row = 2 * source + h
                    if keep:
                        u1 = factors[position * TERMS + 2 * q + h]
                    else:
                        u1 = factor(wide, row)
                    w = (u1 * u1) * (cp * bcast(ms, row) + bcast(mp, row))
                    s0 += w
                    sums = [t + w * bcast(ref, row) for t, ref in zip(sums, (xs, ys, zs))]
            values = [
                jnp.sum(c * s0 - t, axis=1, keepdims=True) * (3.0 * scale * time_step)
                for c, t in zip((cx, cy, cz), sums)
            ]
            done.append((cell, picks, values))
        for cell, picks, values in done:
            for ref, value in zip((ax, ay, az), values):
                spread(ref, cell, picks, value)

    loop(own_total, force_step)

    own_row = lax.broadcasted_iota(jnp.int32, (ROWS, LANES), 0)
    mover_rows = jnp.max(jnp.where(hi_row[...] >= 0.0, own_row + 1, 0))

    def moved_up(x):
        for bit in range(7):
            lands = (bits[...] >> bit) & 1
            x = jnp.where(lands == 1, pltpu.roll(x, ROWS - (1 << bit), 0), x)
        return x

    for c, acc in enumerate((ax, ay, az)):
        kicked = fields[3 + c] + acc[OWN, :]
        fields[3 + c] = kicked
        fields[c] = fields[c] + time_step * kicked
    fields[6] = dens[OWN, :]
    stays = dest_v[...] == own
    for v in range(FIELDS):
        whole = fields[v]
        kept_ref[v] = jnp.where(stays, whole, 0.0)
        whole = moved_up(whole)
        first = whole.astype(jnp.bfloat16).astype(jnp.float32)
        parts[v] = first
        parts[FIELDS + v] = whole - first

    bf = jnp.bfloat16
    iota16 = lax.broadcasted_iota(jnp.int32, (16, LANES), 0).astype(jnp.float32).astype(bf)
    one16, zero16 = jnp.ones((16, LANES), bf), jnp.zeros((16, LANES), bf)

    def twice(x):
        return jnp.concatenate([x, x], axis=0).astype(bf)

    def pack_step(step, carry):
        for j in range(PACK_ROWS):
            row = step * PACK_ROWS + j
            cols = slice(j * LANES, (j + 1) * LANES)
            hi_b, lo_b = twice(bcast(hi_row, row)), twice(bcast(lo_row, row))
            for k in range(16):
                b0[16 * k : 16 * k + 16, cols] = jnp.where(
                    lo_b == iota16 + bf(16 * k), one16, zero16
                )
            upper = hi_b == iota16
            lower = hi_b == iota16 + bf(16)
            for v in range(2 * FIELDS):
                value = twice(parts[v, pl.ds(row, 8, stride=0), :])
                a0[32 * v : 32 * v + 16, cols] = jnp.where(upper, value, zero16)
                a0[32 * v + 16 : 32 * v + 32, cols] = jnp.where(lower, value, zero16)
        packed[...] += lax.dot_general(
            a0[...], b0[...], (((1,), (1,)), ((), ())), preferred_element_type=jnp.float32
        )
        return carry

    lax.fori_loop(0, (mover_rows + PACK_ROWS - 1) // PACK_ROWS, pack_step, 0)

    for g in range(GROUPS):
        cols = slice((g & 1) * LANES, (g & 1) * LANES + LANES)
        for v in range(FIELDS):
            r = 32 * v + (g >> 1) * 8
            s = r + 32 * FIELDS
            blocks[g, v] = packed[r : r + 8, cols] + packed[s : s + 8, cols]
    turn = 1 - 2 * (own & 1)
    for ref, step in zip((to_next, to_next2, to_far, to_far2), chip_steps(own)):
        ref[0] = blocks[group_of(2 * step)]
        ref[1] = blocks[group_of(2 * step + turn)]
    to_other[...] = blocks[group_of(turn)]


def chip_steps(own):
    even = jnp.where((own >> 1) & 1 == 0, 1, -1)
    low = jnp.where((own >> 2) & 1 == 0, 2, -2)
    return even, -even, low, -low


def group_of(offset):
    g = jnp.where(offset < 0, offset + REACH, offset + REACH - 1)
    return jnp.minimum(jnp.maximum(g, 0), GROUPS - 1)


def stay_kernel(kept_ref, out_ref, kept_v, rows, sem):
    load = pltpu.make_async_copy(kept_ref, kept_v, sem.at[1])
    load.start()
    load.wait()

    def step(i, carry):
        col = pl.multiple_of(i * LANES, LANES)
        for v in range(FIELDS):
            rows[v : v + 1, pl.ds(col, LANES)] = kept_v[v, pl.ds(i, 1), :]
        return carry

    lax.fori_loop(0, ROWS, step, 0, unroll=8)
    copy = pltpu.make_async_copy(rows, out_ref.at[:, pl.ds(0, PART_DEV)], sem.at[0])
    copy.start()
    copy.wait()


def assemble_kernel(
    own_ref, far2_ref, next2_ref, far_ref, next_ref, other_ref,
    x_far2, x_next2, x_far, x_next, held_ref, out_ref, rows, sem
):
    del held_ref
    own = own_ref[0]
    turn = 1 - 2 * (own & 1)
    steps = chip_steps(own)
    low = (own >> 2) & 1 == 0
    pick_low = low == (turn < 0)
    parts = [(ref, (0,), -2 * step) for ref, step in zip((next_ref, next2_ref, far_ref, far2_ref), steps)]
    parts += [(ref, (1,), -2 * step - turn) for ref, step in zip((x_next, x_next2), steps)]
    parts += [(other_ref, (), -turn)]
    parts += [(None, (), 3 * turn)]

    for ref, index, offset in parts:
        start = group_of(offset) * MOST
        for v in range(FIELDS):
            if ref is None:
                tile = jnp.where(pick_low, x_far[1, v], x_far2[1, v])
            else:
                tile = ref[index + (v,)]
            for r in range(8):
                col = pl.multiple_of(start + r * LANES, LANES)
                rows[v : v + 1, pl.ds(col, LANES)] = tile[r : r + 1, :]
    copy = pltpu.make_async_copy(
        rows, out_ref.at[:, pl.ds(PART_DEV, GROUPS * MOST)], sem.at[0]
    )
    copy.start()
    copy.wait()


def swapped(block, pairs):
    route = [(a, b) for a, b in pairs] + [(b, a) for a, b in pairs]
    return lax.ppermute(block, "cells", route)


def per_device(
    position,
    velocity,
    particle_mass,
    entropy,
    density_old,
    active,
    neighbours,
    destination,
    recv_slot,
):
    count = lax.axis_size("cells")
    own = lax.axis_index("cells").reshape(1)
    square = (ROWS, LANES)
    mass, ent, rho, act = (
        a.reshape(square) for a in (particle_mass, entropy, density_old, active)
    )
    lists = neighbours.T
    vm = pl.BlockSpec(memory_space=pltpu.VMEM)
    sm = pl.BlockSpec(memory_space=pltpu.SMEM)
    hbm = pl.BlockSpec(memory_space=pl.ANY)
    f32, i32 = jnp.float32, jnp.int32
    far, near = pl.pallas_call(
        edge_kernel,
        out_shape=(jax.ShapeDtypeStruct((HALO_ROWS, LANES), f32),) * 2,
        in_specs=[sm] + [hbm] * 6,
        out_specs=(vm, vm),
        scratch_shapes=[
            pltpu.VMEM((2, 3, EDGE * CELL_PARTICLES), f32),
            pltpu.VMEM((2, 8, LANES), i32),
            pltpu.VMEM((NEIGHBOURS, CELLS_DEV), i32),
            pltpu.SemaphoreType.DMA((11,)),
        ],
        compiler_params=pltpu.CompilerParams(vmem_limit_bytes=64 * 2**20),
    )(own, position, mass, ent, rho, act, lists)
    near_pairs = [(2 * k, 2 * k + 1) for k in range(count // 2)]
    far_pairs = [(2 * k + 1, (2 * k + 2) % count) for k in range(count // 2)]
    far = swapped(far, far_pairs)
    near = swapped(near, near_pairs)

    dest, slot = destination.reshape(square), recv_slot.reshape(square)
    order = pl.pallas_call(
        order_kernel,
        out_shape=(
            jax.ShapeDtypeStruct(square, f32),
            jax.ShapeDtypeStruct(square, f32),
            jax.ShapeDtypeStruct(square, i32),
        ),
        in_specs=[sm] + [hbm] * 2,
        out_specs=(vm,) * 3,
        scratch_shapes=[
            pltpu.VMEM(square, i32),
            pltpu.VMEM(square, i32),
            pltpu.SemaphoreType.DMA((2,)),
        ],
        compiler_params=pltpu.CompilerParams(vmem_limit_bytes=64 * 2**20),
        cost_estimate=pl.CostEstimate(
            flops=2**24, bytes_accessed=2**23, transcendentals=0
        ),
    )(own, dest, slot)
    ext = pltpu.VMEM((EXT_ROWS, LANES), f32)
    flat = pltpu.VMEM((3, PART_DEV), f32)
    whole = pltpu.VMEM(square, i32)
    pair = jax.ShapeDtypeStruct((2, FIELDS, 8, LANES), f32)
    kept, *sends = pl.pallas_call(
        state_kernel,
        out_shape=(
            jax.ShapeDtypeStruct((FIELDS, ROWS, LANES), f32),
            pair,
            pair,
            pair,
            pair,
            jax.ShapeDtypeStruct((FIELDS, 8, LANES), f32),
        ),
        in_specs=[sm] + [hbm] * 13,
        out_specs=(vm,) * 6,
        scratch_shapes=[flat, flat, whole, whole]
        + [pltpu.VMEM((NEIGHBOURS, CELLS_DEV), i32)]
        + [ext] * 12
        + [
            pltpu.VMEM((FIELDS, ROWS, LANES), f32),
            whole,
            pltpu.VMEM((2 * FIELDS, ROWS, LANES), f32),
            pltpu.VMEM(square, f32),
            pltpu.VMEM(square, f32),
            pltpu.VMEM((64 * FIELDS, PACK_ROWS * LANES), jnp.bfloat16),
            pltpu.VMEM((256, PACK_ROWS * LANES), jnp.bfloat16),
            pltpu.VMEM((64 * FIELDS, 256), f32),
            pltpu.VMEM((GROUPS, FIELDS, 8, LANES), f32),
            pltpu.VMEM((HALO_ROWS, LANES), f32),
            pltpu.VMEM((HALO_ROWS, LANES), f32),
            ext,
            ext,
            pltpu.VMEM((KEPT_STEPS * UNROLL * TERMS, 8, LANES), f32),
            pltpu.VMEM((32, LANES), i32),
            pltpu.SMEM((32, LANES), i32),
            pltpu.SMEM((LIST_SIZE,), i32),
            pltpu.SemaphoreType.DMA((16,)),
        ],
        compiler_params=pltpu.CompilerParams(vmem_limit_bytes=64 * 2**20),
    )(
        own,
        position,
        velocity,
        mass,
        ent,
        rho,
        act,
        dest,
        lists,
        far,
        near,
        *order,
    )
    to_far, to_far2, to_next, to_next2, to_other = sends
    chips = count // 2

    def chip_pairs(distance, first):
        firsts = [c for c in range(chips) if (c // distance) % 2 == first]
        return [
            (2 * c + core, 2 * ((c + distance) % chips) + core)
            for c in firsts
            for core in range(2)
        ]

    other = swapped(to_other, near_pairs)
    next2 = swapped(to_next2, chip_pairs(1, 1))
    far2 = swapped(to_far2, chip_pairs(2, 1))
    next1 = swapped(to_next, chip_pairs(1, 0))
    far1 = swapped(to_far, chip_pairs(2, 0))
    held = pl.pallas_call(
        stay_kernel,
        out_shape=jax.ShapeDtypeStruct((FIELDS, RECV_DEV), f32),
        in_specs=[hbm],
        out_specs=hbm,
        scratch_shapes=[
            pltpu.VMEM((FIELDS, ROWS, LANES), f32),
            pltpu.VMEM((FIELDS, PART_DEV), f32),
            pltpu.SemaphoreType.DMA((2,)),
        ],
        compiler_params=pltpu.CompilerParams(vmem_limit_bytes=64 * 2**20 - 450 * 2**10),
        cost_estimate=pl.CostEstimate(
            flops=4 * 2**20, bytes_accessed=4 * 2**20, transcendentals=0
        ),
    )(kept)
    far2, held = lax.optimization_barrier((far2, held))
    crossed = [swapped(x, near_pairs) for x in (far2, next2, far1, next1)]
    return pl.pallas_call(
        assemble_kernel,
        out_shape=jax.ShapeDtypeStruct((FIELDS, RECV_DEV), f32),
        in_specs=[sm] + [vm] * 9 + [hbm],
        out_specs=hbm,
        scratch_shapes=[
            pltpu.VMEM((FIELDS, GROUPS * MOST), f32),
            pltpu.SemaphoreType.DMA((1,)),
        ],
        input_output_aliases={10: 0},
        compiler_params=pltpu.CompilerParams(vmem_limit_bytes=16 * 2**20),
    )(own, far2, next2, far1, next1, other, *crossed, held)


def solution(mesh):
    placed = (
        P(None, "cells"),
        P(None, "cells"),
        P("cells"),
        P("cells"),
        P("cells"),
        P("cells"),
        P("cells", None),
        P("cells"),
        P("cells"),
    )
    return jax.shard_map(
        per_device, mesh=mesh, in_specs=placed, out_specs=P(None, "cells"), check_vma=False
    )
```

```python
import functools

import jax
import jax.numpy as jnp
from jax import lax
from jax.experimental import pallas as pl
from jax.experimental.pallas import tpu as pltpu
from jax.sharding import PartitionSpec as P

CELL_PARTICLES = 256
HALO = 4
REACH = 4
PART_DEV = 16384
MOST = 1024
RECV_DEV = 24576
CELLS_DEV = 64
NEIGHBOURS = 6
LANES = 128
ROWS = PART_DEV // LANES
EDGE = 2 * HALO
EXT = CELLS_DEV + 2 * EDGE
EXT_ROWS = 2 * EXT
EDGE_ROWS = 2 * EDGE
HALO_ROWS = 96
GHOST = HALO
LISTED = CELLS_DEV + 2 * GHOST
OWN = slice(EDGE_ROWS, EDGE_ROWS + ROWS)
PACK_ROWS = 16
KEPT_STEPS = 8
TERMS = 2 * NEIGHBOURS
DUMMY = EDGE * 64 + 32 + (8 << 20)
UNROLL = 16
LIST_SIZE = LISTED * 32 + 64
GROUPS = 2 * REACH
time_step = 0.25
FIELDS = 9


def bcast(ref, row):
    return ref[pl.ds(row, 8, stride=0), :]


def edge_kernel(
    own_ref, pos_ref, mass_ref, ent_ref, rho_ref, act_ref, nbr_ref, far_out, near_out,
    far_ref, near_ref, pos_v, act_v, nbr_v, sem
):
    even = own_ref[0] % 2 == 0
    copies = []
    nbr_copy = pltpu.make_async_copy(nbr_ref, nbr_v, sem.at[0])
    nbr_copy.start()
    for side, ref in enumerate((far_ref, near_ref)):
        low = even if side == 0 else jnp.logical_not(even)
        wide = pl.multiple_of(jnp.where(low, 0, ROWS - EDGE_ROWS), 8)
        near = pl.multiple_of(jnp.where(low, 0, ROWS - 8), 8)
        lane = pl.multiple_of(jnp.where(low, 0, PART_DEV - EDGE * CELL_PARTICLES), LANES)
        base = 1 + 5 * side
        pairs = [
            (pos_ref.at[:, pl.ds(lane, EDGE * CELL_PARTICLES)], pos_v.at[side]),
            (mass_ref.at[pl.ds(wide, EDGE_ROWS)], ref.at[pl.ds(48, EDGE_ROWS)]),
            (ent_ref.at[pl.ds(near, 8)], ref.at[pl.ds(64, 8)]),
            (rho_ref.at[pl.ds(near, 8)], ref.at[pl.ds(72, 8)]),
            (act_ref.at[pl.ds(near, 8)], act_v.at[side]),
        ]
        for k, (a, b) in enumerate(pairs):
            copy = pltpu.make_async_copy(a, b, sem.at[base + k])
            copy.start()
            copies.append(copy)
    nbr_copy.wait()
    lists = nbr_v[...].astype(jnp.float32)
    outs = []
    for side, (ref, out) in enumerate(((far_ref, far_out), (near_ref, near_out))):
        ref[88:96, :] = jnp.zeros((8, LANES), jnp.float32)
        ref[88 : 88 + NEIGHBOURS, 0:CELLS_DEV] = lists
        for copy in copies[5 * side : 5 * side + 5]:
            copy.wait()
        for c in range(3):
            for i in range(EDGE_ROWS):
                ref[16 * c + i : 16 * c + i + 1, :] = (
                    pos_v[side, c : c + 1, i * LANES : (i + 1) * LANES] * 0.5
                )
        ref[80:88, :] = (act_v[side] == 1).astype(jnp.float32)
        copy = pltpu.make_async_copy(ref, out, sem.at[11 + side])
        copy.start()
        outs.append(copy)
    for copy in outs:
        copy.wait()


def order_kernel(own_ref, dest_in, slot_in, hi_out, lo_out, bits_out, dest_ref, slot_ref, sem):
    own = own_ref[0]
    loads = [
        pltpu.make_async_copy(dest_in, dest_ref, sem.at[0]),
        pltpu.make_async_copy(slot_in, slot_ref, sem.at[1]),
    ]
    for copy in loads:
        copy.start()
    for copy in loads:
        copy.wait()
    before = (
        lax.broadcasted_iota(jnp.int32, (LANES, LANES), 0)
        < lax.broadcasted_iota(jnp.int32, (LANES, LANES), 1)
    ).astype(jnp.bfloat16)
    ones = jnp.ones((LANES, LANES), jnp.bfloat16)
    dest = dest_ref[...]
    away = (dest - own) & 127
    signed = jnp.where(away > 64, away - 128, away)
    group = jnp.where(signed < 0, signed + REACH, signed + REACH - 1)
    place = (slot_ref[...] - PART_DEV) & (MOST - 1)
    moving = dest != own
    hi = (group >> 1) * 8 + (place >> 7)
    lo = (group & 1) * LANES + (place & (LANES - 1))
    key = jnp.where(moving, hi * 256 + lo, -1)
    bits = jnp.zeros((ROWS, LANES), jnp.int32)
    mover16 = moving.astype(jnp.float32).astype(jnp.bfloat16)
    above = lax.dot_general(
        before, mover16, (((0,), (0,)), ((), ())), preferred_element_type=jnp.float32
    ).astype(jnp.int32)
    in_column = jnp.dot(ones, mover16, preferred_element_type=jnp.float32).astype(jnp.int32)
    own_row = lax.broadcasted_iota(jnp.int32, (ROWS, LANES), 0)
    remaining = jnp.where(moving, own_row - above, 0)
    for bit in range(7):
        coming = pltpu.roll(remaining, ROWS - (1 << bit), 0)
        lands = (coming >> bit) & 1
        leaves = (remaining >> bit) & 1
        bits = bits | (lands << bit)
        key = jnp.where(lands == 1, pltpu.roll(key, ROWS - (1 << bit), 0), key)
        remaining = jnp.where(lands == 1, coming, jnp.where(leaves == 1, 0, remaining))
    key = jnp.where(own_row < in_column, key, -1)
    hi_out[...] = (key >> 8).astype(jnp.float32)
    lo_out[...] = (key & 255).astype(jnp.float32)
    bits_out[...] = bits


def state_kernel(
    own_ref, pos_ref, vel_ref, mass_ref, ent_ref, rho_ref, act_ref, dest_ref,
    nbr_ref, far_in, near_in, hi_in, lo_in, bits_in,
    kept_out, to_far, to_far2, to_next, to_next2, to_other,
    pos_v, vel_v, act_v, dest_v, nbr_v,
    xs, ys, zs, ms, ps, es, rho_old, rank, dens, ax, ay, az,
    fields, bits, parts, hi_row, lo_row, a0, b0, packed, blocks,
    kept_ref, far_ref, near_ref, sq, mp, factors, table_v, table, chunk_list, sem,
):
    own = own_ref[0]
    even = own % 2 == 0
    scale = 8.0 / (NEIGHBOURS * CELL_PARTICLES)
    loads = [
        (act_ref, act_v),
        (nbr_ref, nbr_v),
        (far_in, far_ref),
        (near_in, near_ref),
        (dest_ref, dest_v),
        (hi_in, hi_row),
        (lo_in, lo_row),
        (bits_in, bits),
        (rho_ref, rho_old.at[pl.ds(EDGE_ROWS, ROWS)]),
        (mass_ref, ms.at[pl.ds(EDGE_ROWS, ROWS)]),
        (ent_ref, es.at[pl.ds(EDGE_ROWS, ROWS)]),
        (pos_ref, pos_v),
        (vel_ref, vel_v),
    ]
    loads = [pltpu.make_async_copy(a, b, sem.at[k]) for k, (a, b) in enumerate(loads)]
    for copy in loads:
        copy.start()
    for ref in (dens, ax, ay, az, packed):
        ref[...] = jnp.zeros_like(ref)
    for copy in loads[:4]:
        copy.wait()

    def side_rows(first, last):
        f, n = far_ref[first:last, :], near_ref[first:last, :]
        return jnp.where(even, f, n), jnp.where(even, n, f)

    zeros8 = jnp.zeros((8, LANES), jnp.float32)
    ghost_act = side_rows(80, 88)

    act = jnp.concatenate(
        [zeros8, ghost_act[0], (act_v[...] == 1).astype(jnp.float32), ghost_act[1], zeros8],
        axis=0,
    )
    before = (
        lax.broadcasted_iota(jnp.int32, (LANES, LANES), 0)
        < lax.broadcasted_iota(jnp.int32, (LANES, LANES), 1)
    ).astype(jnp.bfloat16)
    ones = jnp.ones((LANES, LANES), jnp.bfloat16)
    act16 = act.astype(jnp.bfloat16)
    in_lanes = lax.dot_general(
        ones[0:16], act16, (((1,), (1,)), ((), ())), preferred_element_type=jnp.float32
    )
    halves = lax.broadcasted_iota(jnp.int32, (EXT_ROWS, LANES), 0) >> 1
    joined = (halves == lax.broadcasted_iota(jnp.int32, (EXT_ROWS, LANES), 1)).astype(jnp.bfloat16)
    in_cells = jnp.dot(in_lanes.astype(jnp.bfloat16), joined, preferred_element_type=jnp.float32)
    table_v[0:8, :] = in_cells[0:8].astype(jnp.int32)
    shift = own * CELLS_DEV - EDGE
    near_lists = side_rows(88, 96)
    pad = jnp.zeros((8 - NEIGHBOURS, CELLS_DEV), jnp.int32)
    table_v[8:16, 0:CELLS_DEV] = (jnp.concatenate([nbr_v[...], pad]) - shift) & 8191
    for k in range(2):
        table_v[16 + 8 * k : 24 + 8 * k, 0:LANES] = (
            near_lists[k].astype(jnp.int32) - shift
        ) & 8191
    table_copy = pltpu.make_async_copy(table_v, table, sem.at[15])
    table_copy.start()
    high = slice(EDGE_ROWS + ROWS, EXT_ROWS)
    for k, ref in enumerate((xs, ys, zs, ms)):
        ref[0:EDGE_ROWS, :], ref[high, :] = side_rows(16 * k, 16 * k + 16)
    for ref, rows, fill in ((es, (64, 72), 0.0), (rho_old, (72, 80), 1.0)):
        ref[0:8, :] = zeros8 + fill
        ref[EXT_ROWS - 8 :, :] = zeros8 + fill
        ref[8:16, :], ref[EXT_ROWS - 16 : EXT_ROWS - 8, :] = side_rows(*rows)
    inside = jnp.dot(act16, before, preferred_element_type=jnp.float32)
    total = jnp.dot(act16, ones, preferred_element_type=jnp.float32)
    row_id = lax.broadcasted_iota(jnp.int32, (EXT_ROWS, LANES), 0)
    rank[...] = jnp.where(
        act > 0.5, inside + jnp.where(row_id % 2 == 1, pltpu.roll(total, 1, 0), 0.0), -1.0
    )

    for copy in loads[4:]:
        copy.wait()

    def split_rows(i, carry):
        col = pl.multiple_of(i * LANES, LANES)
        p = pos_v[:, pl.ds(col, LANES)]
        v = vel_v[:, pl.ds(col, LANES)]
        for c, ref in enumerate((xs, ys, zs)):
            fields[c, pl.ds(i, 1), :] = p[c : c + 1, :]
            fields[3 + c, pl.ds(i, 1), :] = v[c : c + 1, :]
        return carry

    lax.fori_loop(0, ROWS, split_rows, 0, unroll=8)
    for c, ref in enumerate((xs, ys, zs)):
        ref[OWN, :] = fields[c] * 0.5
    fields[6] = rho_old[OWN, :]
    fields[7] = es[OWN, :]
    fields[8] = ms[OWN, :]
    table_copy.wait()

    cells = [(EDGE + k, k, 8) for k in range(CELLS_DEV)]
    cells += [(EDGE - GHOST + k, CELLS_DEV - GHOST + k, 16) for k in range(GHOST)]
    cells += [(EDGE + CELLS_DEV + k, k, 24) for k in range(GHOST)]
    at, most, own_total = 0, 0, 0
    for number, (cell, lane, row) in enumerate(cells):
        n = table[0, cell]
        code = (row << 20) + (lane << 13) + (cell << 6)
        for k in range(4):
            chunk_list[at + k] = code + k
        at = at + ((n + 7) >> 3)
        most = jnp.maximum(most, n)
        if number == CELLS_DEV - 1:
            own_total = at
    all_total = at

    @pl.when(most > 32)
    def _():
        def refill(first, count, lane0, row):
            def one(k, start):
                cell = first + k
                n = table[0, cell]
                code = (row << 20) + ((lane0 + k) << 13) + (cell << 6)

                def put(j, carry):
                    chunk_list[start + j] = code + j
                    return carry

                lax.fori_loop(0, (n + 7) >> 3, put, 0)
                return start + ((n + 7) >> 3)

            return lambda start: lax.fori_loop(0, count, one, start)

        start = refill(EDGE, CELLS_DEV, 0, 8)(0)
        start = refill(EDGE - GHOST, GHOST, CELLS_DEV - GHOST, 16)(start)
        refill(EDGE + CELLS_DEV, GHOST, 0, 24)(start)

    sub = lax.broadcasted_iota(jnp.int32, (8, LANES), 0).astype(jnp.float32)

    def chunk_of(position, limit):
        code = chunk_list[jnp.maximum(jnp.minimum(position, limit - 1), 0)]
        code = jnp.where(position < limit, code, DUMMY)
        cell = (code >> 6) & 127
        want = sub + ((code & 63) * 8).astype(jnp.float32)
        picks = [bcast(rank, 2 * cell + h) == want for h in range(2)]
        lane = (code >> 13) & 127
        sources = [table[(code >> 20) + q, lane] for q in range(NEIGHBOURS)]
        return cell, picks, sources

    def column(ref, cell, picks):
        both = jnp.where(picks[0], bcast(ref, 2 * cell), 0.0) + jnp.where(
            picks[1], bcast(ref, 2 * cell + 1), 0.0
        )
        return jnp.sum(both, axis=1, keepdims=True)

    def spread(ref, cell, picks, value):
        for h in range(2):
            row = jnp.sum(jnp.where(picks[h], value, 0.0), axis=0, keepdims=True)
            ref[pl.ds(2 * cell + h, 1), :] += row

    sq[...] = -(xs[...] * xs[...] + ys[...] * ys[...] + zs[...] * zs[...])

    def target(cell, picks):
        cx, cy, cz = (column(ref, cell, picks) for ref in (xs, ys, zs))
        inner = 1.0 - (cx * cx + cy * cy + cz * cz)
        return cx, cy, cz, [jnp.broadcast_to(x, (8, LANES)) for x in (inner, 2.0 * cx, 2.0 * cy, 2.0 * cz)]

    def factor(wide, row):
        inner, tx, ty, tz = wide
        near = (inner + bcast(sq, row)) + tx * bcast(xs, row)
        near = (near + ty * bcast(ys, row)) + tz * bcast(zs, row)
        return jnp.maximum(near, 0.0)

    def density_step(step, keep):
        done = []
        for u in range(UNROLL):
            position = step * UNROLL + u
            cell, picks, sources = chunk_of(position, all_total)
            wide = target(cell, picks)[3]
            total_rows = jnp.zeros((8, LANES), jnp.float32)
            for q, source in enumerate(sources):
                for h in range(2):
                    row = 2 * source + h
                    u1 = factor(wide, row)
                    if keep:
                        factors[position * TERMS + 2 * q + h] = u1
                    total_rows += u1 * u1 * u1 * bcast(ms, row)
            value = jnp.sum(total_rows, axis=1, keepdims=True) * scale
            done.append((cell, picks, value))
        for cell, picks, value in done:
            spread(dens, cell, picks, value)

    def loop(limit, body):
        steps = (limit + UNROLL - 1) // UNROLL

        def run(keep):
            def one(step, carry):
                body(step, keep)
                return carry

            return one

        lax.fori_loop(0, jnp.minimum(steps, KEPT_STEPS), run(True), 0)
        lax.fori_loop(KEPT_STEPS, steps, run(False), 0)

    loop(all_total, density_step)

    rho = jnp.where(rank[...] >= 0.0, dens[...], rho_old[...])
    dens[...] = rho
    ps[...] = es[...] * jnp.exp(jnp.log(rho) * (-1.0 / 3.0))

    mp[...] = ms[...] * ps[...]

    def force_step(step, keep):
        done = []
        for u in range(UNROLL):
            position = step * UNROLL + u
            cell, picks, sources = chunk_of(position, own_total)
            cx, cy, cz, wide = target(cell, picks)
            cp = jnp.broadcast_to(column(ps, cell, picks), (8, LANES))
            s0 = jnp.zeros((8, LANES), jnp.float32)
            sums = [s0, s0, s0]
            for q, source in enumerate(sources):
                for h in range(2):
                    row = 2 * source + h
                    if keep:
                        u1 = factors[position * TERMS + 2 * q + h]
                    else:
                        u1 = factor(wide, row)
                    w = (u1 * u1) * (cp * bcast(ms, row) + bcast(mp, row))
                    s0 += w
                    sums = [t + w * bcast(ref, row) for t, ref in zip(sums, (xs, ys, zs))]
            values = [
                jnp.sum(c * s0 - t, axis=1, keepdims=True) * (3.0 * scale * time_step)
                for c, t in zip((cx, cy, cz), sums)
            ]
            done.append((cell, picks, values))
        for cell, picks, values in done:
            for ref, value in zip((ax, ay, az), values):
                spread(ref, cell, picks, value)

    loop(own_total, force_step)

    own_row = lax.broadcasted_iota(jnp.int32, (ROWS, LANES), 0)
    mover_rows = jnp.max(jnp.where(hi_row[...] >= 0.0, own_row + 1, 0))

    def moved_up(x):
        for bit in range(7):
            lands = (bits[...] >> bit) & 1
            x = jnp.where(lands == 1, pltpu.roll(x, ROWS - (1 << bit), 0), x)
        return x

    for c, acc in enumerate((ax, ay, az)):
        kicked = fields[3 + c] + acc[OWN, :]
        fields[3 + c] = kicked
        fields[c] = fields[c] + time_step * kicked
    fields[6] = dens[OWN, :]
    stays = dest_v[...] == own
    for v in range(FIELDS):
        whole = fields[v]
        kept_ref[v] = jnp.where(stays, whole, 0.0)
        whole = moved_up(whole)
        first = whole.astype(jnp.bfloat16).astype(jnp.float32)
        parts[v] = first
        parts[FIELDS + v] = whole - first

    kept_copy = pltpu.make_async_copy(kept_ref, kept_out, sem.at[14])
    kept_copy.start()

    bf = jnp.bfloat16
    iota16 = lax.broadcasted_iota(jnp.int32, (16, LANES), 0).astype(jnp.float32).astype(bf)
    one16, zero16 = jnp.ones((16, LANES), bf), jnp.zeros((16, LANES), bf)

    def twice(x):
        return jnp.concatenate([x, x], axis=0).astype(bf)

    def pack_step(step, carry):
        for j in range(PACK_ROWS):
            row = step * PACK_ROWS + j
            cols = slice(j * LANES, (j + 1) * LANES)
            hi_b, lo_b = twice(bcast(hi_row, row)), twice(bcast(lo_row, row))
            for k in range(16):
                b0[16 * k : 16 * k + 16, cols] = jnp.where(
                    lo_b == iota16 + bf(16 * k), one16, zero16
                )
            upper = hi_b == iota16
            lower = hi_b == iota16 + bf(16)
            for v in range(2 * FIELDS):
                value = twice(parts[v, pl.ds(row, 8, stride=0), :])
                a0[32 * v : 32 * v + 16, cols] = jnp.where(upper, value, zero16)
                a0[32 * v + 16 : 32 * v + 32, cols] = jnp.where(lower, value, zero16)
        packed[...] += lax.dot_general(
            a0[...], b0[...], (((1,), (1,)), ((), ())), preferred_element_type=jnp.float32
        )
        return carry

    lax.fori_loop(0, (mover_rows + PACK_ROWS - 1) // PACK_ROWS, pack_step, 0)

    for g in range(GROUPS):
        cols = slice((g & 1) * LANES, (g & 1) * LANES + LANES)
        for v in range(FIELDS):
            r = 32 * v + (g >> 1) * 8
            s = r + 32 * FIELDS
            blocks[g, v] = packed[r : r + 8, cols] + packed[s : s + 8, cols]
    turn = 1 - 2 * (own & 1)
    for ref, step in zip((to_next, to_next2, to_far, to_far2), chip_steps(own)):
        ref[0] = blocks[group_of(2 * step)]
        ref[1] = blocks[group_of(2 * step + turn)]
    to_other[...] = blocks[group_of(turn)]
    kept_copy.wait()


def chip_steps(own):
    even = jnp.where((own >> 1) & 1 == 0, 1, -1)
    low = jnp.where((own >> 2) & 1 == 0, 2, -2)
    return even, -even, low, -low


def group_of(offset):
    g = jnp.where(offset < 0, offset + REACH, offset + REACH - 1)
    return jnp.minimum(jnp.maximum(g, 0), GROUPS - 1)


def stay_kernel(kept_ref, out_ref, kept_v, rows, sem):
    load = pltpu.make_async_copy(kept_ref, kept_v, sem.at[1])
    load.start()
    load.wait()

    def step(i, carry):
        col = pl.multiple_of(i * LANES, LANES)
        for v in range(FIELDS):
            rows[v : v + 1, pl.ds(col, LANES)] = kept_v[v, pl.ds(i, 1), :]
        return carry

    lax.fori_loop(0, ROWS, step, 0, unroll=8)
    copy = pltpu.make_async_copy(rows, out_ref.at[:, pl.ds(0, PART_DEV)], sem.at[0])
    copy.start()
    copy.wait()


def assemble_kernel(
    own_ref, far2_ref, next2_ref, far_ref, next_ref, other_ref,
    x_far2, x_next2, x_far, x_next, held_ref, out_ref, rows, sem
):
    del held_ref
    own = own_ref[0]
    turn = 1 - 2 * (own & 1)
    steps = chip_steps(own)
    low = (own >> 2) & 1 == 0
    pick_low = low == (turn < 0)
    parts = [(ref, (0,), -2 * step) for ref, step in zip((next_ref, next2_ref, far_ref, far2_ref), steps)]
    parts += [(ref, (1,), -2 * step - turn) for ref, step in zip((x_next, x_next2), steps)]
    parts += [(other_ref, (), -turn)]
    parts += [(None, (), 3 * turn)]

    for ref, index, offset in parts:
        start = group_of(offset) * MOST
        for v in range(FIELDS):
            if ref is None:
                tile = jnp.where(pick_low, x_far[1, v], x_far2[1, v])
            else:
                tile = ref[index + (v,)]
            for r in range(8):
                col = pl.multiple_of(start + r * LANES, LANES)
                rows[v : v + 1, pl.ds(col, LANES)] = tile[r : r + 1, :]
    copy = pltpu.make_async_copy(
        rows, out_ref.at[:, pl.ds(PART_DEV, GROUPS * MOST)], sem.at[0]
    )
    copy.start()
    copy.wait()


def swapped(block, pairs):
    route = [(a, b) for a, b in pairs] + [(b, a) for a, b in pairs]
    return lax.ppermute(block, "cells", route)


def per_device(
    position,
    velocity,
    particle_mass,
    entropy,
    density_old,
    active,
    neighbours,
    destination,
    recv_slot,
):
    count = lax.axis_size("cells")
    own = lax.axis_index("cells").reshape(1)
    square = (ROWS, LANES)
    mass, ent, rho, act = (
        a.reshape(square) for a in (particle_mass, entropy, density_old, active)
    )
    lists = neighbours.T
    vm = pl.BlockSpec(memory_space=pltpu.VMEM)
    sm = pl.BlockSpec(memory_space=pltpu.SMEM)
    hbm = pl.BlockSpec(memory_space=pl.ANY)
    f32, i32 = jnp.float32, jnp.int32
    far, near = pl.pallas_call(
        edge_kernel,
        out_shape=(jax.ShapeDtypeStruct((HALO_ROWS, LANES), f32),) * 2,
        in_specs=[sm] + [hbm] * 6,
        out_specs=(hbm, hbm),
        scratch_shapes=[
            pltpu.VMEM((HALO_ROWS, LANES), f32),
            pltpu.VMEM((HALO_ROWS, LANES), f32),
            pltpu.VMEM((2, 3, EDGE * CELL_PARTICLES), f32),
            pltpu.VMEM((2, 8, LANES), i32),
            pltpu.VMEM((NEIGHBOURS, CELLS_DEV), i32),
            pltpu.SemaphoreType.DMA((13,)),
        ],
        compiler_params=pltpu.CompilerParams(vmem_limit_bytes=64 * 2**20),
    )(own, position, mass, ent, rho, act, lists)
    near_pairs = [(2 * k, 2 * k + 1) for k in range(count // 2)]
    far_pairs = [(2 * k + 1, (2 * k + 2) % count) for k in range(count // 2)]
    far = swapped(far, far_pairs)
    near = swapped(near, near_pairs)

    dest, slot = destination.reshape(square), recv_slot.reshape(square)
    order = pl.pallas_call(
        order_kernel,
        out_shape=(
            jax.ShapeDtypeStruct(square, f32),
            jax.ShapeDtypeStruct(square, f32),
            jax.ShapeDtypeStruct(square, i32),
        ),
        in_specs=[sm] + [hbm] * 2,
        out_specs=(vm,) * 3,
        scratch_shapes=[
            pltpu.VMEM(square, i32),
            pltpu.VMEM(square, i32),
            pltpu.SemaphoreType.DMA((2,)),
        ],
        compiler_params=pltpu.CompilerParams(vmem_limit_bytes=64 * 2**20),
        cost_estimate=pl.CostEstimate(
            flops=2**24, bytes_accessed=2**23, transcendentals=0
        ),
    )(own, dest, slot)
    ext = pltpu.VMEM((EXT_ROWS, LANES), f32)
    flat = pltpu.VMEM((3, PART_DEV), f32)
    whole = pltpu.VMEM(square, i32)
    pair = jax.ShapeDtypeStruct((2, FIELDS, 8, LANES), f32)
    kept, *sends = pl.pallas_call(
        state_kernel,
        out_shape=(
            jax.ShapeDtypeStruct((FIELDS, ROWS, LANES), f32),
            pair,
            pair,
            pair,
            pair,
            jax.ShapeDtypeStruct((FIELDS, 8, LANES), f32),
        ),
        in_specs=[sm] + [hbm] * 13,
        out_specs=(hbm,) + (vm,) * 5,
        scratch_shapes=[flat, flat, whole, whole]
        + [pltpu.VMEM((NEIGHBOURS, CELLS_DEV), i32)]
        + [ext] * 12
        + [
            pltpu.VMEM((FIELDS, ROWS, LANES), f32),
            whole,
            pltpu.VMEM((2 * FIELDS, ROWS, LANES), f32),
            pltpu.VMEM(square, f32),
            pltpu.VMEM(square, f32),
            pltpu.VMEM((64 * FIELDS, PACK_ROWS * LANES), jnp.bfloat16),
            pltpu.VMEM((256, PACK_ROWS * LANES), jnp.bfloat16),
            pltpu.VMEM((64 * FIELDS, 256), f32),
            pltpu.VMEM((GROUPS, FIELDS, 8, LANES), f32),
            pltpu.VMEM((FIELDS, ROWS, LANES), f32),
            pltpu.VMEM((HALO_ROWS, LANES), f32),
            pltpu.VMEM((HALO_ROWS, LANES), f32),
            ext,
            ext,
            pltpu.VMEM((KEPT_STEPS * UNROLL * TERMS, 8, LANES), f32),
            pltpu.VMEM((32, LANES), i32),
            pltpu.SMEM((32, LANES), i32),
            pltpu.SMEM((LIST_SIZE,), i32),
            pltpu.SemaphoreType.DMA((16,)),
        ],
        compiler_params=pltpu.CompilerParams(vmem_limit_bytes=64 * 2**20),
    )(
        own,
        position,
        velocity,
        mass,
        ent,
        rho,
        act,
        dest,
        lists,
        far,
        near,
        *order,
    )
    to_far, to_far2, to_next, to_next2, to_other = sends
    chips = count // 2

    def chip_pairs(distance, first):
        firsts = [c for c in range(chips) if (c // distance) % 2 == first]
        return [
            (2 * c + core, 2 * ((c + distance) % chips) + core)
            for c in firsts
            for core in range(2)
        ]

    other = swapped(to_other, near_pairs)
    next2 = swapped(to_next2, chip_pairs(1, 1))
    far2 = swapped(to_far2, chip_pairs(2, 1))
    next1 = swapped(to_next, chip_pairs(1, 0))
    far1 = swapped(to_far, chip_pairs(2, 0))
    held = pl.pallas_call(
        stay_kernel,
        out_shape=jax.ShapeDtypeStruct((FIELDS, RECV_DEV), f32),
        in_specs=[hbm],
        out_specs=hbm,
        scratch_shapes=[
            pltpu.VMEM((FIELDS, ROWS, LANES), f32),
            pltpu.VMEM((FIELDS, PART_DEV), f32),
            pltpu.SemaphoreType.DMA((2,)),
        ],
        compiler_params=pltpu.CompilerParams(vmem_limit_bytes=64 * 2**20 - 450 * 2**10),
        cost_estimate=pl.CostEstimate(
            flops=4 * 2**20, bytes_accessed=4 * 2**20, transcendentals=0
        ),
    )(kept)
    far2, held = lax.optimization_barrier((far2, held))
    crossed = [swapped(x, near_pairs) for x in (far2, next2, far1, next1)]
    return pl.pallas_call(
        assemble_kernel,
        out_shape=jax.ShapeDtypeStruct((FIELDS, RECV_DEV), f32),
        in_specs=[sm] + [vm] * 9 + [hbm],
        out_specs=hbm,
        scratch_shapes=[
            pltpu.VMEM((FIELDS, GROUPS * MOST), f32),
            pltpu.SemaphoreType.DMA((1,)),
        ],
        input_output_aliases={10: 0},
        compiler_params=pltpu.CompilerParams(vmem_limit_bytes=16 * 2**20),
    )(own, far2, next2, far1, next1, other, *crossed, held)


def solution(mesh):
    placed = (
        P(None, "cells"),
        P(None, "cells"),
        P("cells"),
        P("cells"),
        P("cells"),
        P("cells"),
        P("cells", None),
        P("cells"),
        P("cells"),
    )
    return jax.shard_map(
        per_device, mesh=mesh, in_specs=placed, out_specs=P(None, "cells"), check_vma=False
    )
```

```python
import functools

import jax
import jax.numpy as jnp
from jax import lax
from jax.experimental import pallas as pl
from jax.experimental.pallas import tpu as pltpu
from jax.sharding import PartitionSpec as P

CELL_PARTICLES = 256
HALO = 4
REACH = 4
PART_DEV = 16384
MOST = 1024
RECV_DEV = 24576
CELLS_DEV = 64
NEIGHBOURS = 6
LANES = 128
ROWS = PART_DEV // LANES
EDGE = 2 * HALO
EXT = CELLS_DEV + 2 * EDGE
EXT_ROWS = 2 * EXT
SPARE = 8
EDGE_ROWS = 2 * EDGE
HALO_ROWS = 96
GHOST = HALO
LISTED = CELLS_DEV + 2 * GHOST
OWN = slice(EDGE_ROWS, EDGE_ROWS + ROWS)
PACK_ROWS = 16
KEPT_STEPS = 8
TERMS = 2 * NEIGHBOURS
DUMMY = EDGE * 64 + 32 + (8 << 20)
UNROLL = 16
LIST_SIZE = LISTED * 32 + 64
GROUPS = 2 * REACH
time_step = 0.25
FIELDS = 9


def bcast(ref, row):
    return ref[pl.ds(row, 8, stride=0), :]


def edge_kernel(
    own_ref, pos_ref, mass_ref, ent_ref, rho_ref, act_ref, nbr_ref, far_out, near_out,
    far_ref, near_ref, pos_v, act_v, nbr_v, sem
):
    even = own_ref[0] % 2 == 0
    copies = []
    nbr_copy = pltpu.make_async_copy(nbr_ref, nbr_v, sem.at[0])
    nbr_copy.start()
    for side, ref in enumerate((far_ref, near_ref)):
        low = even if side == 0 else jnp.logical_not(even)
        wide = pl.multiple_of(jnp.where(low, 0, ROWS - EDGE_ROWS), 8)
        near = pl.multiple_of(jnp.where(low, 0, ROWS - 8), 8)
        lane = pl.multiple_of(jnp.where(low, 0, PART_DEV - EDGE * CELL_PARTICLES), LANES)
        base = 1 + 5 * side
        pairs = [
            (pos_ref.at[:, pl.ds(lane, EDGE * CELL_PARTICLES)], pos_v.at[side]),
            (mass_ref.at[pl.ds(wide, EDGE_ROWS)], ref.at[pl.ds(48, EDGE_ROWS)]),
            (ent_ref.at[pl.ds(near, 8)], ref.at[pl.ds(64, 8)]),
            (rho_ref.at[pl.ds(near, 8)], ref.at[pl.ds(72, 8)]),
            (act_ref.at[pl.ds(near, 8)], act_v.at[side]),
        ]
        for k, (a, b) in enumerate(pairs):
            copy = pltpu.make_async_copy(a, b, sem.at[base + k])
            copy.start()
            copies.append(copy)
    nbr_copy.wait()
    lists = nbr_v[...].astype(jnp.float32)
    outs = []
    for side, (ref, out) in enumerate(((far_ref, far_out), (near_ref, near_out))):
        ref[88:96, :] = jnp.zeros((8, LANES), jnp.float32)
        ref[88 : 88 + NEIGHBOURS, 0:CELLS_DEV] = lists
        for copy in copies[5 * side : 5 * side + 5]:
            copy.wait()
        for c in range(3):
            for i in range(EDGE_ROWS):
                ref[16 * c + i : 16 * c + i + 1, :] = (
                    pos_v[side, c : c + 1, i * LANES : (i + 1) * LANES] * 0.5
                )
        ref[80:88, :] = (act_v[side] == 1).astype(jnp.float32)
        copy = pltpu.make_async_copy(ref, out, sem.at[11 + side])
        copy.start()
        outs.append(copy)
    for copy in outs:
        copy.wait()


def order_kernel(own_ref, dest_in, slot_in, hi_out, lo_out, bits_out, dest_ref, slot_ref, sem):
    own = own_ref[0]
    loads = [
        pltpu.make_async_copy(dest_in, dest_ref, sem.at[0]),
        pltpu.make_async_copy(slot_in, slot_ref, sem.at[1]),
    ]
    for copy in loads:
        copy.start()
    for copy in loads:
        copy.wait()
    before = (
        lax.broadcasted_iota(jnp.int32, (LANES, LANES), 0)
        < lax.broadcasted_iota(jnp.int32, (LANES, LANES), 1)
    ).astype(jnp.bfloat16)
    ones = jnp.ones((LANES, LANES), jnp.bfloat16)
    dest = dest_ref[...]
    away = (dest - own) & 127
    signed = jnp.where(away > 64, away - 128, away)
    group = jnp.where(signed < 0, signed + REACH, signed + REACH - 1)
    place = (slot_ref[...] - PART_DEV) & (MOST - 1)
    moving = dest != own
    hi = (group >> 1) * 8 + (place >> 7)
    lo = (group & 1) * LANES + (place & (LANES - 1))
    key = jnp.where(moving, hi * 256 + lo, -1)
    bits = jnp.zeros((ROWS, LANES), jnp.int32)
    mover16 = moving.astype(jnp.float32).astype(jnp.bfloat16)
    above = lax.dot_general(
        before, mover16, (((0,), (0,)), ((), ())), preferred_element_type=jnp.float32
    ).astype(jnp.int32)
    in_column = jnp.dot(ones, mover16, preferred_element_type=jnp.float32).astype(jnp.int32)
    own_row = lax.broadcasted_iota(jnp.int32, (ROWS, LANES), 0)
    remaining = jnp.where(moving, own_row - above, 0)
    for bit in range(7):
        coming = pltpu.roll(remaining, ROWS - (1 << bit), 0)
        lands = (coming >> bit) & 1
        leaves = (remaining >> bit) & 1
        bits = bits | (lands << bit)
        key = jnp.where(lands == 1, pltpu.roll(key, ROWS - (1 << bit), 0), key)
        remaining = jnp.where(lands == 1, coming, jnp.where(leaves == 1, 0, remaining))
    key = jnp.where(own_row < in_column, key, -1)
    hi_out[...] = (key >> 8).astype(jnp.float32)
    lo_out[...] = (key & 255).astype(jnp.float32)
    bits_out[...] = bits


def state_kernel(
    own_ref, pos_ref, vel_ref, mass_ref, ent_ref, rho_ref, act_ref, dest_ref,
    nbr_ref, far_in, near_in, hi_in, lo_in, bits_in,
    kept_out, to_far, to_far2, to_next, to_next2, to_other,
    pos_v, vel_v, act_v, dest_v, nbr_v,
    xs, ys, zs, ms, ps, es, rho_old, rank, dens, ax, ay, az,
    fields, bits, parts, hi_row, lo_row, a0, b0, packed, blocks,
    kept_ref, far_ref, near_ref, sq, mp, factors, table_v, table, chunk_list, sem,
):
    own = own_ref[0]
    even = own % 2 == 0
    scale = 8.0 / (NEIGHBOURS * CELL_PARTICLES)
    loads = [
        (act_ref, act_v),
        (nbr_ref, nbr_v),
        (far_in, far_ref),
        (near_in, near_ref),
        (dest_ref, dest_v),
        (hi_in, hi_row.at[pl.ds(0, ROWS)]),
        (lo_in, lo_row.at[pl.ds(0, ROWS)]),
        (bits_in, bits),
        (rho_ref, rho_old.at[pl.ds(EDGE_ROWS, ROWS)]),
        (mass_ref, ms.at[pl.ds(EDGE_ROWS, ROWS)]),
        (ent_ref, es.at[pl.ds(EDGE_ROWS, ROWS)]),
        (pos_ref, pos_v),
        (vel_ref, vel_v),
    ]
    loads = [pltpu.make_async_copy(a, b, sem.at[k]) for k, (a, b) in enumerate(loads)]
    for copy in loads:
        copy.start()
    for ref in (dens, ax, ay, az, packed):
        ref[...] = jnp.zeros_like(ref)
    for copy in loads[:4]:
        copy.wait()

    def side_rows(first, last):
        f, n = far_ref[first:last, :], near_ref[first:last, :]
        return jnp.where(even, f, n), jnp.where(even, n, f)

    zeros8 = jnp.zeros((8, LANES), jnp.float32)
    ghost_act = side_rows(80, 88)

    act = jnp.concatenate(
        [zeros8, ghost_act[0], (act_v[...] == 1).astype(jnp.float32), ghost_act[1], zeros8],
        axis=0,
    )
    before = (
        lax.broadcasted_iota(jnp.int32, (LANES, LANES), 0)
        < lax.broadcasted_iota(jnp.int32, (LANES, LANES), 1)
    ).astype(jnp.bfloat16)
    ones = jnp.ones((LANES, LANES), jnp.bfloat16)
    act16 = act.astype(jnp.bfloat16)
    in_lanes = lax.dot_general(
        ones[0:16], act16, (((1,), (1,)), ((), ())), preferred_element_type=jnp.float32
    )
    halves = lax.broadcasted_iota(jnp.int32, (EXT_ROWS, LANES), 0) >> 1
    joined = (halves == lax.broadcasted_iota(jnp.int32, (EXT_ROWS, LANES), 1)).astype(jnp.bfloat16)
    in_cells = jnp.dot(in_lanes.astype(jnp.bfloat16), joined, preferred_element_type=jnp.float32)
    table_v[0:8, :] = in_cells[0:8].astype(jnp.int32)
    shift = own * CELLS_DEV - EDGE
    near_lists = side_rows(88, 96)
    pad = jnp.zeros((8 - NEIGHBOURS, CELLS_DEV), jnp.int32)
    table_v[8:16, 0:CELLS_DEV] = (jnp.concatenate([nbr_v[...], pad]) - shift) & 8191
    for k in range(2):
        table_v[16 + 8 * k : 24 + 8 * k, 0:LANES] = (
            near_lists[k].astype(jnp.int32) - shift
        ) & 8191
    table_copy = pltpu.make_async_copy(table_v, table, sem.at[15])
    table_copy.start()
    high = slice(EDGE_ROWS + ROWS, EXT_ROWS)
    for k, ref in enumerate((xs, ys, zs, ms)):
        ref[0:EDGE_ROWS, :], ref[high, :] = side_rows(16 * k, 16 * k + 16)
    for ref, rows, fill in ((es, (64, 72), 0.0), (rho_old, (72, 80), 1.0)):
        ref[0:8, :] = zeros8 + fill
        ref[EXT_ROWS - 8 : EXT_ROWS, :] = zeros8 + fill
        ref[8:16, :], ref[EXT_ROWS - 16 : EXT_ROWS - 8, :] = side_rows(*rows)
    inside = jnp.dot(act16, before, preferred_element_type=jnp.float32)
    total = jnp.dot(act16, ones, preferred_element_type=jnp.float32)
    row_id = lax.broadcasted_iota(jnp.int32, (EXT_ROWS, LANES), 0)
    rank[0:EXT_ROWS, :] = jnp.where(
        act > 0.5, inside + jnp.where(row_id % 2 == 1, pltpu.roll(total, 1, 0), 0.0), -1.0
    )

    for copy in loads[4:]:
        copy.wait()

    def split_rows(i, carry):
        col = pl.multiple_of(i * LANES, LANES)
        p = pos_v[:, pl.ds(col, LANES)]
        v = vel_v[:, pl.ds(col, LANES)]
        for c, ref in enumerate((xs, ys, zs)):
            fields[c, pl.ds(i, 1), :] = p[c : c + 1, :]
            fields[3 + c, pl.ds(i, 1), :] = v[c : c + 1, :]
        return carry

    lax.fori_loop(0, ROWS, split_rows, 0, unroll=8)
    for c, ref in enumerate((xs, ys, zs)):
        ref[OWN, :] = fields[c] * 0.5
    fields[6] = rho_old[OWN, :]
    fields[7] = es[OWN, :]
    fields[8] = ms[OWN, :]
    table_copy.wait()

    cells = [(EDGE + k, k, 8) for k in range(CELLS_DEV)]
    cells += [(EDGE - GHOST + k, CELLS_DEV - GHOST + k, 16) for k in range(GHOST)]
    cells += [(EDGE + CELLS_DEV + k, k, 24) for k in range(GHOST)]
    at, most, own_total = 0, 0, 0
    for number, (cell, lane, row) in enumerate(cells):
        n = table[0, cell]
        code = (row << 20) + (lane << 13) + (cell << 6)
        for k in range(4):
            chunk_list[at + k] = code + k
        at = at + ((n + 7) >> 3)
        most = jnp.maximum(most, n)
        if number == CELLS_DEV - 1:
            own_total = at
    all_total = at

    @pl.when(most > 32)
    def _():
        def refill(first, count, lane0, row):
            def one(k, start):
                cell = first + k
                n = table[0, cell]
                code = (row << 20) + ((lane0 + k) << 13) + (cell << 6)

                def put(j, carry):
                    chunk_list[start + j] = code + j
                    return carry

                lax.fori_loop(0, (n + 7) >> 3, put, 0)
                return start + ((n + 7) >> 3)

            return lambda start: lax.fori_loop(0, count, one, start)

        start = refill(EDGE, CELLS_DEV, 0, 8)(0)
        start = refill(EDGE - GHOST, GHOST, CELLS_DEV - GHOST, 16)(start)
        refill(EDGE + CELLS_DEV, GHOST, 0, 24)(start)

    sub = lax.broadcasted_iota(jnp.int32, (8, LANES), 0).astype(jnp.float32)

    def chunk_of(position, limit):
        code = chunk_list[jnp.maximum(jnp.minimum(position, limit - 1), 0)]
        code = jnp.where(position < limit, code, DUMMY)
        cell = (code >> 6) & 127
        want = sub + ((code & 63) * 8).astype(jnp.float32)
        picks = [bcast(rank, 2 * cell + h) == want for h in range(2)]
        lane = (code >> 13) & 127
        sources = [table[(code >> 20) + q, lane] for q in range(NEIGHBOURS)]
        return cell, picks, sources

    def column(ref, cell, picks):
        both = jnp.where(picks[0], bcast(ref, 2 * cell), 0.0) + jnp.where(
            picks[1], bcast(ref, 2 * cell + 1), 0.0
        )
        return jnp.sum(both, axis=1, keepdims=True)

    def spread(ref, cell, picks, value):
        for h in range(2):
            row = jnp.sum(jnp.where(picks[h], value, 0.0), axis=0, keepdims=True)
            ref[pl.ds(2 * cell + h, 1), :] += row

    sq[0:EXT_ROWS, :] = -sum(r[0:EXT_ROWS, :] * r[0:EXT_ROWS, :] for r in (xs, ys, zs))

    def target(cell, picks):
        cx, cy, cz = (column(ref, cell, picks) for ref in (xs, ys, zs))
        inner = 1.0 - (cx * cx + cy * cy + cz * cz)
        return cx, cy, cz, [jnp.broadcast_to(x, (8, LANES)) for x in (inner, 2.0 * cx, 2.0 * cy, 2.0 * cz)]

    def factor(wide, row):
        inner, tx, ty, tz = wide
        near = (inner + bcast(sq, row)) + tx * bcast(xs, row)
        near = (near + ty * bcast(ys, row)) + tz * bcast(zs, row)
        return jnp.maximum(near, 0.0)

    def density_step(step, keep):
        done = []
        for u in range(UNROLL):
            position = step * UNROLL + u
            cell, picks, sources = chunk_of(position, all_total)
            wide = target(cell, picks)[3]
            total_rows = jnp.zeros((8, LANES), jnp.float32)
            for q, source in enumerate(sources):
                for h in range(2):
                    row = 2 * source + h
                    u1 = factor(wide, row)
                    if keep:
                        factors[position * TERMS + 2 * q + h] = u1
                    total_rows += u1 * u1 * u1 * bcast(ms, row)
            value = jnp.sum(total_rows, axis=1, keepdims=True) * scale
            done.append((cell, picks, value))
        for cell, picks, value in done:
            spread(dens, cell, picks, value)

    def loop(limit, body):
        steps = (limit + UNROLL - 1) // UNROLL

        def run(keep):
            def one(step, carry):
                body(step, keep)
                return carry

            return one

        lax.fori_loop(0, jnp.minimum(steps, KEPT_STEPS), run(True), 0)
        lax.fori_loop(KEPT_STEPS, steps, run(False), 0)

    loop(all_total, density_step)

    used = slice(0, EXT_ROWS)
    rho = jnp.where(rank[used, :] >= 0.0, dens[used, :], rho_old[used, :])
    dens[used, :] = rho
    ps[used, :] = es[used, :] * jnp.exp(jnp.log(rho) * (-1.0 / 3.0))

    mp[used, :] = ms[used, :] * ps[used, :]

    def force_step(step, keep):
        done = []
        for u in range(UNROLL):
            position = step * UNROLL + u
            cell, picks, sources = chunk_of(position, own_total)
            cx, cy, cz, wide = target(cell, picks)
            cp = jnp.broadcast_to(column(ps, cell, picks), (8, LANES))
            s0 = jnp.zeros((8, LANES), jnp.float32)
            sums = [s0, s0, s0]
            for q, source in enumerate(sources):
                for h in range(2):
                    row = 2 * source + h
                    if keep:
                        u1 = factors[position * TERMS + 2 * q + h]
                    else:
                        u1 = factor(wide, row)
                    w = (u1 * u1) * (cp * bcast(ms, row) + bcast(mp, row))
                    s0 += w
                    sums = [t + w * bcast(ref, row) for t, ref in zip(sums, (xs, ys, zs))]
            values = [
                jnp.sum(c * s0 - t, axis=1, keepdims=True) * (3.0 * scale * time_step)
                for c, t in zip((cx, cy, cz), sums)
            ]
            done.append((cell, picks, values))
        for cell, picks, values in done:
            for ref, value in zip((ax, ay, az), values):
                spread(ref, cell, picks, value)

    loop(own_total, force_step)

    own_row = lax.broadcasted_iota(jnp.int32, (ROWS, LANES), 0)
    mover_rows = jnp.max(jnp.where(hi_row[0:ROWS, :] >= 0.0, own_row + 1, 0))

    def moved_up(x):
        for bit in range(7):
            lands = (bits[...] >> bit) & 1
            x = jnp.where(lands == 1, pltpu.roll(x, ROWS - (1 << bit), 0), x)
        return x

    for c, acc in enumerate((ax, ay, az)):
        kicked = fields[3 + c] + acc[OWN, :]
        fields[3 + c] = kicked
        fields[c] = fields[c] + time_step * kicked
    fields[6] = dens[OWN, :]
    stays = dest_v[...] == own
    for v in range(FIELDS):
        whole = fields[v]
        kept_ref[v] = jnp.where(stays, whole, 0.0)
        whole = moved_up(whole)
        first = whole.astype(jnp.bfloat16).astype(jnp.float32)
        parts[v, 0:ROWS, :] = first
        parts[FIELDS + v, 0:ROWS, :] = whole - first

    kept_copy = pltpu.make_async_copy(kept_ref, kept_out, sem.at[14])
    kept_copy.start()

    bf = jnp.bfloat16
    iota16 = lax.broadcasted_iota(jnp.int32, (16, LANES), 0).astype(jnp.float32).astype(bf)
    one16, zero16 = jnp.ones((16, LANES), bf), jnp.zeros((16, LANES), bf)

    def twice(x):
        return jnp.concatenate([x, x], axis=0).astype(bf)

    def pack_step(step, carry):
        for j in range(PACK_ROWS):
            row = step * PACK_ROWS + j
            cols = slice(j * LANES, (j + 1) * LANES)
            hi_b, lo_b = twice(bcast(hi_row, row)), twice(bcast(lo_row, row))
            for k in range(16):
                b0[16 * k : 16 * k + 16, cols] = jnp.where(
                    lo_b == iota16 + bf(16 * k), one16, zero16
                )
            upper = hi_b == iota16
            lower = hi_b == iota16 + bf(16)
            for v in range(2 * FIELDS):
                value = twice(parts[v, pl.ds(row, 8, stride=0), :])
                a0[32 * v : 32 * v + 16, cols] = jnp.where(upper, value, zero16)
                a0[32 * v + 16 : 32 * v + 32, cols] = jnp.where(lower, value, zero16)
        packed[...] += lax.dot_general(
            a0[...], b0[...], (((1,), (1,)), ((), ())), preferred_element_type=jnp.float32
        )
        return carry

    lax.fori_loop(0, (mover_rows + PACK_ROWS - 1) // PACK_ROWS, pack_step, 0)

    for g in range(GROUPS):
        cols = slice((g & 1) * LANES, (g & 1) * LANES + LANES)
        for v in range(FIELDS):
            r = 32 * v + (g >> 1) * 8
            s = r + 32 * FIELDS
            blocks[g, v] = packed[r : r + 8, cols] + packed[s : s + 8, cols]
    turn = 1 - 2 * (own & 1)
    for ref, step in zip((to_next, to_next2, to_far, to_far2), chip_steps(own)):
        ref[0] = blocks[group_of(2 * step)]
        ref[1] = blocks[group_of(2 * step + turn)]
    to_other[...] = blocks[group_of(turn)]
    kept_copy.wait()


def chip_steps(own):
    even = jnp.where((own >> 1) & 1 == 0, 1, -1)
    low = jnp.where((own >> 2) & 1 == 0, 2, -2)
    return even, -even, low, -low


def group_of(offset):
    g = jnp.where(offset < 0, offset + REACH, offset + REACH - 1)
    return jnp.minimum(jnp.maximum(g, 0), GROUPS - 1)


def stay_kernel(kept_ref, out_ref, kept_v, rows, sem):
    load = pltpu.make_async_copy(kept_ref, kept_v, sem.at[1])
    load.start()
    load.wait()

    def step(i, carry):
        col = pl.multiple_of(i * LANES, LANES)
        for v in range(FIELDS):
            rows[v : v + 1, pl.ds(col, LANES)] = kept_v[v, pl.ds(i, 1), :]
        return carry

    lax.fori_loop(0, ROWS, step, 0, unroll=8)
    copy = pltpu.make_async_copy(rows, out_ref.at[:, pl.ds(0, PART_DEV)], sem.at[0])
    copy.start()
    copy.wait()


def assemble_kernel(
    own_ref, far2_ref, next2_ref, far_ref, next_ref, other_ref,
    x_far2, x_next2, x_far, x_next, held_ref, out_ref, rows, sem
):
    del held_ref
    own = own_ref[0]
    turn = 1 - 2 * (own & 1)
    steps = chip_steps(own)
    low = (own >> 2) & 1 == 0
    pick_low = low == (turn < 0)
    parts = [(ref, (0,), -2 * step) for ref, step in zip((next_ref, next2_ref, far_ref, far2_ref), steps)]
    parts += [(ref, (1,), -2 * step - turn) for ref, step in zip((x_next, x_next2), steps)]
    parts += [(other_ref, (), -turn)]
    parts += [(None, (), 3 * turn)]

    for ref, index, offset in parts:
        start = group_of(offset) * MOST
        for v in range(FIELDS):
            if ref is None:
                tile = jnp.where(pick_low, x_far[1, v], x_far2[1, v])
            else:
                tile = ref[index + (v,)]
            for r in range(8):
                col = pl.multiple_of(start + r * LANES, LANES)
                rows[v : v + 1, pl.ds(col, LANES)] = tile[r : r + 1, :]
    copy = pltpu.make_async_copy(
        rows, out_ref.at[:, pl.ds(PART_DEV, GROUPS * MOST)], sem.at[0]
    )
    copy.start()
    copy.wait()


def swapped(block, pairs):
    route = [(a, b) for a, b in pairs] + [(b, a) for a, b in pairs]
    return lax.ppermute(block, "cells", route)


def per_device(
    position,
    velocity,
    particle_mass,
    entropy,
    density_old,
    active,
    neighbours,
    destination,
    recv_slot,
):
    count = lax.axis_size("cells")
    own = lax.axis_index("cells").reshape(1)
    square = (ROWS, LANES)
    mass, ent, rho, act = (
        a.reshape(square) for a in (particle_mass, entropy, density_old, active)
    )
    lists = neighbours.T
    vm = pl.BlockSpec(memory_space=pltpu.VMEM)
    sm = pl.BlockSpec(memory_space=pltpu.SMEM)
    hbm = pl.BlockSpec(memory_space=pl.ANY)
    f32, i32 = jnp.float32, jnp.int32
    far, near = pl.pallas_call(
        edge_kernel,
        out_shape=(jax.ShapeDtypeStruct((HALO_ROWS, LANES), f32),) * 2,
        in_specs=[sm] + [hbm] * 6,
        out_specs=(hbm, hbm),
        scratch_shapes=[
            pltpu.VMEM((HALO_ROWS, LANES), f32),
            pltpu.VMEM((HALO_ROWS, LANES), f32),
            pltpu.VMEM((2, 3, EDGE * CELL_PARTICLES), f32),
            pltpu.VMEM((2, 8, LANES), i32),
            pltpu.VMEM((NEIGHBOURS, CELLS_DEV), i32),
            pltpu.SemaphoreType.DMA((13,)),
        ],
        compiler_params=pltpu.CompilerParams(vmem_limit_bytes=64 * 2**20),
    )(own, position, mass, ent, rho, act, lists)
    near_pairs = [(2 * k, 2 * k + 1) for k in range(count // 2)]
    far_pairs = [(2 * k + 1, (2 * k + 2) % count) for k in range(count // 2)]
    far = swapped(far, far_pairs)
    near = swapped(near, near_pairs)

    dest, slot = destination.reshape(square), recv_slot.reshape(square)
    order = pl.pallas_call(
        order_kernel,
        out_shape=(
            jax.ShapeDtypeStruct(square, f32),
            jax.ShapeDtypeStruct(square, f32),
            jax.ShapeDtypeStruct(square, i32),
        ),
        in_specs=[sm] + [hbm] * 2,
        out_specs=(vm,) * 3,
        scratch_shapes=[
            pltpu.VMEM(square, i32),
            pltpu.VMEM(square, i32),
            pltpu.SemaphoreType.DMA((2,)),
        ],
        compiler_params=pltpu.CompilerParams(vmem_limit_bytes=64 * 2**20),
        cost_estimate=pl.CostEstimate(
            flops=2**24, bytes_accessed=2**23, transcendentals=0
        ),
    )(own, dest, slot)
    ext = pltpu.VMEM((EXT_ROWS + SPARE, LANES), f32)
    flat = pltpu.VMEM((3, PART_DEV), f32)
    whole = pltpu.VMEM(square, i32)
    pair = jax.ShapeDtypeStruct((2, FIELDS, 8, LANES), f32)
    kept, *sends = pl.pallas_call(
        state_kernel,
        out_shape=(
            jax.ShapeDtypeStruct((FIELDS, ROWS, LANES), f32),
            pair,
            pair,
            pair,
            pair,
            jax.ShapeDtypeStruct((FIELDS, 8, LANES), f32),
        ),
        in_specs=[sm] + [hbm] * 13,
        out_specs=(hbm,) + (vm,) * 5,
        scratch_shapes=[flat, flat, whole, whole]
        + [pltpu.VMEM((NEIGHBOURS, CELLS_DEV), i32)]
        + [ext] * 12
        + [
            pltpu.VMEM((FIELDS, ROWS, LANES), f32),
            whole,
            pltpu.VMEM((2 * FIELDS, ROWS + SPARE, LANES), f32),
            pltpu.VMEM((ROWS + SPARE, LANES), f32),
            pltpu.VMEM((ROWS + SPARE, LANES), f32),
            pltpu.VMEM((64 * FIELDS, PACK_ROWS * LANES), jnp.bfloat16),
            pltpu.VMEM((256, PACK_ROWS * LANES), jnp.bfloat16),
            pltpu.VMEM((64 * FIELDS, 256), f32),
            pltpu.VMEM((GROUPS, FIELDS, 8, LANES), f32),
            pltpu.VMEM((FIELDS, ROWS, LANES), f32),
            pltpu.VMEM((HALO_ROWS, LANES), f32),
            pltpu.VMEM((HALO_ROWS, LANES), f32),
            ext,
            ext,
            pltpu.VMEM((KEPT_STEPS * UNROLL * TERMS, 8, LANES), f32),
            pltpu.VMEM((32, LANES), i32),
            pltpu.SMEM((32, LANES), i32),
            pltpu.SMEM((LIST_SIZE,), i32),
            pltpu.SemaphoreType.DMA((16,)),
        ],
        compiler_params=pltpu.CompilerParams(vmem_limit_bytes=64 * 2**20),
    )(
        own,
        position,
        velocity,
        mass,
        ent,
        rho,
        act,
        dest,
        lists,
        far,
        near,
        *order,
    )
    to_far, to_far2, to_next, to_next2, to_other = sends
    chips = count // 2

    def chip_pairs(distance, first):
        firsts = [c for c in range(chips) if (c // distance) % 2 == first]
        return [
            (2 * c + core, 2 * ((c + distance) % chips) + core)
            for c in firsts
            for core in range(2)
        ]

    other = swapped(to_other, near_pairs)
    next2 = swapped(to_next2, chip_pairs(1, 1))
    far2 = swapped(to_far2, chip_pairs(2, 1))
    next1 = swapped(to_next, chip_pairs(1, 0))
    far1 = swapped(to_far, chip_pairs(2, 0))
    held = pl.pallas_call(
        stay_kernel,
        out_shape=jax.ShapeDtypeStruct((FIELDS, RECV_DEV), f32),
        in_specs=[hbm],
        out_specs=hbm,
        scratch_shapes=[
            pltpu.VMEM((FIELDS, ROWS, LANES), f32),
            pltpu.VMEM((FIELDS, PART_DEV), f32),
            pltpu.SemaphoreType.DMA((2,)),
        ],
        compiler_params=pltpu.CompilerParams(vmem_limit_bytes=64 * 2**20 - 450 * 2**10),
        cost_estimate=pl.CostEstimate(
            flops=4 * 2**20, bytes_accessed=4 * 2**20, transcendentals=0
        ),
    )(kept)
    far2, held = lax.optimization_barrier((far2, held))
    crossed = [swapped(x, near_pairs) for x in (far2, next2, far1, next1)]
    return pl.pallas_call(
        assemble_kernel,
        out_shape=jax.ShapeDtypeStruct((FIELDS, RECV_DEV), f32),
        in_specs=[sm] + [vm] * 9 + [hbm],
        out_specs=hbm,
        scratch_shapes=[
            pltpu.VMEM((FIELDS, GROUPS * MOST), f32),
            pltpu.SemaphoreType.DMA((1,)),
        ],
        input_output_aliases={10: 0},
        compiler_params=pltpu.CompilerParams(vmem_limit_bytes=16 * 2**20),
    )(own, far2, next2, far1, next1, other, *crossed, held)


def solution(mesh):
    placed = (
        P(None, "cells"),
        P(None, "cells"),
        P("cells"),
        P("cells"),
        P("cells"),
        P("cells"),
        P("cells", None),
        P("cells"),
        P("cells"),
    )
    return jax.shard_map(
        per_device, mesh=mesh, in_specs=placed, out_specs=P(None, "cells"), check_vma=False
    )
```
